128 devices in a mesh: fsdp: 32 (over y, x_hi, z), seq: 4 (over x_lo, core).
Axes of the slice: x: 4 (x_hi: 2, x_lo: 2; x = x_hi * 2 + x_lo), y: 4, z: 4, core: 2. Of those that a mesh axis runs over, the one named last changes fastest.
Arguments:
- inputs: bfloat16 [32768, 768], P(('fsdp', 'seq')), may hold values from -6 to 6
- proj_in: bfloat16 [768, 2304], P('fsdp'), may hold values from -0.21875 to 0.21875
- bias_query: bfloat16 [768], P('fsdp'), may hold values from -3 to 3
- bias_value: bfloat16 [768], P('fsdp'), may hold values from -3 to 3
- proj_out: bfloat16 [768, 768], P('fsdp'), may hold values from -0.625 to 0.625
- bias_out: bfloat16 [768], P('fsdp'), may hold values from -3 to 3
- norm_gain: bfloat16 [768], P('fsdp'), may hold values from 0.5 to 1.5
- norm_shift: bfloat16 [768], P('fsdp'), may hold values from -2 to 2
- up_weight: bfloat16 [768, 3072], P('fsdp'), may hold values from -0.21875 to 0.21875
- up_bias: bfloat16 [3072], P('fsdp'), may hold values from -3 to 3
- down_weight: bfloat16 [3072, 768], P('fsdp'), may hold values from -0.109375 to 0.109375
- down_bias: bfloat16 [768], P('fsdp'), may hold values from -3 to 3
- post_gain: bfloat16 [768], P('fsdp'), may hold values from 0.5 to 1.5
- post_shift: bfloat16 [768], P('fsdp'), may hold values from -2 to 2
- cotangent: bfloat16 [32768, 768], P(('fsdp', 'seq')), may hold values from -6 to 6
Outputs:
- output: bfloat16 [32768, 768], P(('fsdp', 'seq'))
- grad_input: bfloat16 [32768, 768], P(('fsdp', 'seq'))
- grad_proj_in: float32 [768, 2304], P('fsdp')
- grad_bias_query: float32 [768], P('fsdp')
- grad_bias_value: float32 [768], P('fsdp')
- grad_proj_out: float32 [768, 768], P('fsdp')
- grad_bias_out: float32 [768], P('fsdp')
- grad_norm_gain: float32 [768], P('fsdp')
- grad_norm_shift: float32 [768], P('fsdp')
- grad_up_weight: float32 [768, 3072], P('fsdp')
- grad_up_bias: float32 [3072], P('fsdp')
- grad_down_weight: float32 [3072, 768], P('fsdp')
- grad_down_bias: float32 [768], P('fsdp')
- grad_post_gain: float32 [768], P('fsdp')
- grad_post_shift: float32 [768], P('fsdp')
The draws below stay inside these ranges and needn't reach their ends.
All inputs are finite; a program needn't handle non-finite values.
Results may differ from the reference program's by a relative error of at most 0.025.
Values may be sent and summed in bfloat16 or wider, within the bound.
A program may use at most 128 MiB of HBM per device.

```python
import math
import jax
import jax.numpy as jnp
from jax import lax

D = 768
H = 12
HD = 64
FF = 3072
TOKENS = 32768
LENGTH = 1024
BLOCK = 512
BLOCKS = 2
N_FSDP = 32


def block_levels(key, extent, shards, smallest, top_value):
    loudness = 1.0
    for dim, blocks in shards:
        draws = jax.random.uniform(jax.random.fold_in(jax.random.fold_in(key, 6), dim), (blocks,), jnp.float32, smallest / len(shards), top_value / len(shards))
        loudness = loudness * jnp.repeat(jnp.exp(draws), extent[dim] // blocks).reshape((-1,) + (1,) * (len(extent) - 1 - dim))
    return loudness


def centred(stream_key, extent, deviation, bound, split=(), kind=jnp.bfloat16):
    loudness = block_levels(stream_key, extent, split, -0.22, 0.18) if split else 1.0
    drawn = jax.random.normal(stream_key, extent, jnp.float32) * deviation * loudness
    return jnp.minimum(jnp.maximum(drawn, -bound), bound).astype(kind)


def setup_inputs(seed: int = 0) -> dict:
    seeds = jax.random.split(jax.random.key(seed), 16)
    inputs = centred(seeds[0], (TOKENS, D), 1.0, 6.0, ((0, 128),))
    proj_in = centred(seeds[1], (D, 3 * D), D ** -0.5, 0.21875, ((0, 32),))
    bias_query = centred(seeds[2], (D,), 0.5, 3.0, ((0, 32),))
    bias_value = centred(seeds[3], (D,), 0.5, 3.0, ((0, 32),))
    proj_out = centred(seeds[4], (D, D), (D // 8) ** -0.5, 0.625, ((0, 32),))
    bias_out = centred(seeds[5], (D,), 0.5, 3.0, ((0, 32),))
    norm_gain = jnp.clip(1.0 + 0.1 * jax.random.normal(seeds[6], (D,), jnp.float32), 0.5, 1.5).astype(jnp.bfloat16)
    norm_shift = centred(seeds[7], (D,), 0.3, 2.0, ((0, 32),))
    up_weight = centred(seeds[8], (D, FF), D ** -0.5, 0.21875, ((0, 32),))
    up_bias = centred(seeds[9], (FF,), 0.5, 3.0, ((0, 32),))
    down_weight = centred(seeds[10], (FF, D), FF ** -0.5, 0.109375, ((0, 32),))
    down_bias = centred(seeds[11], (D,), 0.5, 3.0, ((0, 32),))
    post_gain = jnp.clip(1.0 + 0.1 * jax.random.normal(seeds[12], (D,), jnp.float32), 0.5, 1.5).astype(jnp.bfloat16)
    post_shift = centred(seeds[13], (D,), 0.3, 2.0, ((0, 32),))
    cotangent = centred(seeds[14], (TOKENS, D), 1.0, 6.0, ((0, 128),))
    return {"inputs": inputs, "proj_in": proj_in, "bias_query": bias_query, "bias_value": bias_value, "proj_out": proj_out, "bias_out": bias_out, "norm_gain": norm_gain, "norm_shift": norm_shift, "up_weight": up_weight, "up_bias": up_bias, "down_weight": down_weight, "down_bias": down_bias, "post_gain": post_gain, "post_shift": post_shift, "cotangent": cotangent}


@jax.custom_vjp
def low(v):
    return lax.optimization_barrier(v.astype(jnp.bfloat16)).astype(jnp.float32)

@jax.custom_vjp
def low_back(v):
    return v

def low_keep(v):
    return (low(v), None)

def low_pass(kept, grad):
    return (grad,)

def back_keep(v):
    return (v, None)

def back_low(kept, grad):
    return (low(grad),)
low.defvjp(low_keep, low_pass)
low_back.defvjp(back_keep, back_low)
epsilon = 1e-05
highest = lax.Precision.HIGHEST

def product(left, right):
    return jnp.dot(left, right, precision=highest, preferred_element_type=jnp.float32)

def layer_norm(values, gain, shift):
    center = lax.optimization_barrier(jnp.mean(values, axis=-1, keepdims=True))
    centered = values - center
    spread = lax.optimization_barrier(jnp.mean(centered * centered, axis=-1, keepdims=True))
    return centered * lax.rsqrt(spread + epsilon) * gain + shift

def attend_block(queries, keys, values_all, offset):
    scale = 1.0 / math.sqrt(HD)
    scores = jnp.einsum('hqd,hkd->hqk', queries, keys, precision=highest) * scale
    query_pos = offset + jnp.arange(BLOCK, dtype=jnp.int32)[:, None]
    key_pos = jnp.arange(LENGTH, dtype=jnp.int32)[None, :]
    scores = jnp.where(key_pos <= query_pos, scores, -1000000000.0)
    scores = low_back(scores)
    weights = low(jax.nn.softmax(scores, axis=-1))
    return jnp.einsum('hqk,hkd->hqd', weights, values_all, precision=highest)

def layer_forward(seq_in, proj_in, bias_query, bias_value, proj_out, bias_out, norm_gain, norm_shift, up_weight, up_bias, down_weight, down_bias, post_gain, post_shift):
    normed = low(layer_norm(seq_in, norm_gain, norm_shift))
    bias_all = jnp.concatenate([bias_query, jnp.zeros_like(bias_query), bias_value])
    projected = low(low_back(product(normed, proj_in) + bias_all))
    split_heads = projected.reshape(LENGTH, 3, H, HD).transpose(1, 2, 0, 3)
    queries, keys, values_all = (split_heads[0], split_heads[1], split_heads[2])
    query_blocks = queries.reshape(H, BLOCKS, BLOCK, HD).transpose(1, 0, 2, 3)
    offsets = jnp.arange(BLOCKS, dtype=jnp.int32) * BLOCK

    def run_block(block_pair):
        return attend_block(block_pair[0], keys, values_all, block_pair[1])
    context = lax.map(jax.checkpoint(run_block), (query_blocks, offsets))
    context = context.transpose(0, 2, 1, 3).reshape(LENGTH, D)
    context = low(low_back(context))
    residual = seq_in + low_back(product(context, proj_out) + bias_out)
    normed_two = low(layer_norm(residual, post_gain, post_shift))
    hidden = low_back(product(normed_two, up_weight) + up_bias)
    active = low(jax.nn.gelu(hidden, approximate=False))
    return residual + low_back(product(active, down_weight) + down_bias)

def reference(inputs, proj_in, bias_query, bias_value, proj_out, bias_out, norm_gain, norm_shift, up_weight, up_bias, down_weight, down_bias, post_gain, post_shift, cotangent):
    params = tuple((weight_arg.astype(jnp.float32) for weight_arg in (proj_in, bias_query, bias_value, proj_out, bias_out, norm_gain, norm_shift, up_weight, up_bias, down_weight, down_bias, post_gain, post_shift)))
    seq_inputs = inputs.astype(jnp.float32).reshape(N_FSDP, LENGTH, D)
    seq_cots = cotangent.astype(jnp.float32).reshape(N_FSDP, LENGTH, D)

    def per_sequence(running, seq_pair):
        result, pullback = jax.vjp(layer_forward, seq_pair[0], *params)
        grads = pullback(seq_pair[1])
        running = tuple((earlier + increment for earlier, increment in zip(running, grads[1:])))
        return (running, (result, grads[0]))
    start_totals = tuple((jnp.zeros_like(weight_arg) for weight_arg in params))
    totals, (results, input_grads) = lax.scan(per_sequence, start_totals, (seq_inputs, seq_cots))
    return (results.reshape(TOKENS, D).astype(jnp.bfloat16), input_grads.reshape(TOKENS, D).astype(jnp.bfloat16), totals[0], totals[1], totals[2], totals[3], totals[4], totals[5], totals[6], totals[7], totals[8], totals[9], totals[10], totals[11], totals[12])
```

```python
import functools
import math

import jax
import jax.numpy as jnp
from jax import lax
from jax.experimental import pallas as pl
from jax.experimental.pallas import tpu as pltpu
from jax.sharding import PartitionSpec as P

D = 768
H = 12
HD = 64
N = 32
G = 4
ROWS = 24
LEN = 1024
TOK = 256
HEADS = 3
OWN = HEADS * HD
PAD = 256
FFG = 768
epsilon = 1e-05
SCALE = 1.0 / math.sqrt(HD)
MESH = pl.DeviceIdType.MESH


def x_half(f):
    return lax.rem(f // 4, 2)


def place():
    return lax.axis_index("fsdp"), lax.axis_index("seq")


def fan_peer(f, s, t):
    peer = lax.rem(f + t, N)
    return peer, lax.rem(s + 2 * lax.abs(x_half(peer) - x_half(f)), G)


def row_server(f, s, i):
    owner = 8 * s + i
    away = lax.abs(x_half(owner) - x_half(f))
    lo = lax.rem(s // 2 + away, 2)
    return owner, 2 * lo + lax.rem(f, 2)


def row_client(f, s, m):
    group = f // 8
    away = lax.abs(s // 2 - group // 2)
    half = lax.rem(x_half(f) + away, 2)
    return (m // 2) * 8 + half * 4 + lax.rem(m, 2) * 2 + lax.rem(s, 2), group


def client_slot(f):
    return (f // 8) * 2 + lax.rem(f, 4) // 2


def send(src, dst, send_sem, recv_sem, f, s):
    pltpu.make_async_remote_copy(
        src_ref=src,
        dst_ref=dst,
        send_sem=send_sem,
        recv_sem=recv_sem,
        device_id=(f, s),
        device_id_type=MESH,
    ).start()


def take(ref, sem):
    pltpu.make_async_copy(ref, ref, sem).wait()


def loop(count, body):
    lax.fori_loop(0, count, lambda t, carry: (body(t), carry)[1], 0)


def exchange_kernel(kinds, *refs):
    n = len(kinds)
    srcs, dsts = refs[:n], refs[n : 2 * n]
    send_sems, recv_sems, own_sems = refs[2 * n :]
    f, s = place()
    barrier = pltpu.get_barrier_semaphore()

    def greet(peer_f, peer_s):
        pl.semaphore_signal(barrier, inc=1, device_id=(peer_f, peer_s), device_id_type=MESH)

    expected = 0
    if any(k in ("fan", "fan_whole", "fan_sum") for k in kinds):
        loop(N - 1, lambda t: greet(*fan_peer(f, s, t + 1)))
        expected += N - 1
    if any(k in ("seq", "seq_sum") for k in kinds):
        loop(G - 1, lambda t: greet(f, lax.rem(s + t + 1, G)))
        expected += G - 1
    serves_self = jnp.logical_and(
        f // 8 == s, jnp.logical_and(row_server(f, s, lax.rem(f, 8))[1] == s, True)
    )
    others = 8 - serves_self.astype(jnp.int32)

    def guarded(peer, action):
        @pl.when(jnp.logical_or(peer[0] != f, peer[1] != s))
        def _():
            action(*peer)

    if "rows" in kinds:
        loop(8, lambda i: guarded(row_server(f, s, i), greet))
        expected += others
    if "rows_sum" in kinds:
        loop(8, lambda m: guarded(row_client(f, s, m), greet))
        expected += others
    pl.semaphore_wait(barrier, expected)

    for k, kind in enumerate(kinds):
        src, dst = srcs[k], dsts[k]
        ss, rs, own = send_sems.at[k], recv_sems.at[k], own_sems.at[k]
        if kind in ("fan", "fan_whole", "fan_sum"):

            def fan(t, kind=kind, src=src, dst=dst, ss=ss, rs=rs):
                pf, ps = fan_peer(f, s, t + 1)
                block = {"fan": src.at[ps], "fan_sum": src.at[pf], "fan_whole": src}[kind] if kind != "fan_whole" else src
                send(block, dst.at[f], ss, rs, pf, ps)

            loop(N - 1, fan)
            block = src if kind == "fan_whole" else src.at[s] if kind == "fan" else src.at[f]
            pltpu.make_async_copy(block, dst.at[f], own).start()
        elif kind in ("seq", "seq_sum"):

            def around(t, kind=kind, src=src, dst=dst, ss=ss, rs=rs):
                ps = lax.rem(s + t + 1, G)
                send(src if kind == "seq" else src.at[ps], dst.at[s], ss, rs, f, ps)

            loop(G - 1, around)
            pltpu.make_async_copy(src if kind == "seq" else src.at[s], dst.at[s], own).start()
        elif kind == "rows":

            def serve(m, src=src, dst=dst, ss=ss, rs=rs):
                guarded(row_client(f, s, m), functools.partial(send, src, dst.at[lax.rem(f, 8)], ss, rs))

            loop(8, serve)

            @pl.when(serves_self)
            def _(src=src, dst=dst, own=own):
                pltpu.make_async_copy(src, dst.at[lax.rem(f, 8)], own).start()
        else:

            def give(i, src=src, dst=dst, ss=ss, rs=rs):
                guarded(
                    row_server(f, s, i),
                    functools.partial(send, src.at[i], dst.at[client_slot(f)], ss, rs),
                )

            loop(8, give)

            @pl.when(serves_self)
            def _(src=src, dst=dst, own=own):
                pltpu.make_async_copy(src.at[lax.rem(f, 8)], dst.at[client_slot(f)], own).start()

    for k, kind in enumerate(kinds):
        dst = dsts[k]
        ss, rs, own = send_sems.at[k], recv_sems.at[k], own_sems.at[k]
        if kind in ("rows", "rows_sum"):

            @pl.when(serves_self)
            def _(dst=dst, ss=ss, rs=rs, own=own):
                take(dst.at[0], own)
                take(dst.at[pl.ds(0, 7)], ss)
                take(dst.at[pl.ds(0, 7)], rs)

            @pl.when(jnp.logical_not(serves_self))
            def _(dst=dst, ss=ss, rs=rs):
                take(dst, ss)
                take(dst, rs)
        else:
            count = dst.shape[0] - 1
            take(dst.at[0], own)
            take(dst.at[pl.ds(0, count)], ss)
            take(dst.at[pl.ds(0, count)], rs)


def exchange(collective_id, kinds, arrays):
    shapes = []
    for kind, array in zip(kinds, arrays):
        block = array.shape if kind in ("fan_whole", "seq", "rows") else array.shape[1:]
        count = N if kind.startswith("fan") else G if kind.startswith("seq") else 8
        shapes.append(jax.ShapeDtypeStruct((count,) + block, array.dtype))
    n = len(kinds)
    return pl.pallas_call(
        functools.partial(exchange_kernel, kinds),
        out_shape=shapes,
        in_specs=[pl.BlockSpec(memory_space=pl.ANY)] * n,
        out_specs=[pl.BlockSpec(memory_space=pl.ANY)] * n,
        scratch_shapes=[pltpu.SemaphoreType.DMA((n,))] * 3,
        compiler_params=pltpu.CompilerParams(collective_id=collective_id, has_side_effects=True),
    )(*arrays)


def pack(blocks):
    c = blocks.shape[-1] // 2
    return jnp.concatenate([blocks[..., :c], blocks[..., c:]], axis=-2)


def unpack(blocks):
    return jnp.concatenate([blocks[..., :ROWS, :], blocks[..., ROWS:, :]], axis=-1)


def pad_heads(blocks):
    return jnp.pad(blocks, [(0, 0)] * (blocks.ndim - 1) + [(0, PAD - OWN)])


def norm_parts(values):
    center = jnp.mean(values, axis=-1, keepdims=True)
    centered = values - center
    spread = jnp.mean(centered * centered, axis=-1, keepdims=True)
    inverse = lax.rsqrt(spread + epsilon)
    return centered * inverse, inverse


def norm_back(grad, gain, unit, inverse):
    scaled = grad * gain
    mean_one = jnp.mean(scaled, axis=-1, keepdims=True)
    mean_two = jnp.mean(scaled * unit, axis=-1, keepdims=True)
    return inverse * (scaled - mean_one - unit * mean_two)


def dot(a, b):
    return jnp.dot(a, b, preferred_element_type=jnp.float32)


def dot_t(a, b):
    return lax.dot_general(a, b, (((1,), (1,)), ((), ())), preferred_element_type=jnp.float32)


def t_dot(a, b):
    return lax.dot_general(a, b, (((0,), (0,)), ((), ())), preferred_element_type=jnp.float32)


def on_device(
    inputs,
    proj_in,
    bias_query,
    bias_value,
    proj_out,
    bias_out,
    norm_gain,
    norm_shift,
    up_weight,
    up_bias,
    down_weight,
    down_bias,
    post_gain,
    post_shift,
    cotangent,
):
    low = jnp.bfloat16
    full = jnp.float32
    f, s = place()
    split = proj_in.reshape(ROWS, 3, G, OWN).transpose(2, 0, 1, 3)
    send_in = pack(pad_heads(split).reshape(G, ROWS, 3 * PAD))
    send_up = pack(up_weight.reshape(ROWS, G, FFG).transpose(1, 0, 2))
    send_out = pack(proj_out)
    vectors = jnp.stack(
        [norm_gain, norm_shift, post_gain, post_shift, bias_out, down_bias, bias_query, bias_value]
        + [up_bias.reshape(4, ROWS)[i] for i in range(4)]
    )
    spread = jnp.where(
        (jnp.arange(N) == f)[None, :, None], vectors[:, None, :], jnp.zeros((), low)
    ).reshape(12, D)
    spread = jnp.pad(spread, ((0, 4), (0, 0)))
    got_in, got_up, got_out, got_down, got_vec, got_x, got_dy = exchange(
        0,
        ("fan", "fan", "fan_whole", "rows", "fan_whole", "seq", "seq"),
        (send_in, send_up, send_out, down_weight, spread, inputs, cotangent),
    )
    w_in = unpack(got_in).reshape(D, 3 * PAD)
    w_up = unpack(got_up).reshape(D, FFG)
    w_out = unpack(got_out).reshape(D, D)
    w_down = got_down.reshape(FFG, D)
    vec = jnp.sum(got_vec.astype(full), axis=0)
    gain_one, shift_one, gain_two, shift_two, out_shift, down_shift = [vec[i] for i in range(6)]
    query_shift = pad_heads(lax.dynamic_slice_in_dim(vec[6], s * OWN, OWN))
    value_shift = pad_heads(lax.dynamic_slice_in_dim(vec[7], s * OWN, OWN))
    all_up = vec[8:12].reshape(4, N, ROWS).transpose(1, 0, 2).reshape(G, FFG)
    up_shift = lax.dynamic_index_in_dim(all_up, s, keepdims=False)

    x = got_x.reshape(LEN, D).astype(full)
    dy = got_dy.reshape(LEN, D)
    unit_one, inverse_one = norm_parts(x)
    normed = (unit_one * gain_one + shift_one).astype(low)
    bias = jnp.concatenate([query_shift, jnp.zeros_like(query_shift), value_shift])
    projected = (dot(normed, w_in) + bias).astype(low)
    heads = projected.reshape(LEN, 3, PAD)[:, :, :OWN].reshape(LEN, 3, HEADS, HD).transpose(1, 2, 0, 3)
    queries, keys, values = heads[0], heads[1], heads[2]
    scores = jnp.einsum("hqd,hkd->hqk", queries, keys, preferred_element_type=full) * SCALE
    mask = jnp.arange(LEN)[None, :] <= jnp.arange(LEN)[:, None]
    scores = jnp.where(mask, scores, -1e9)
    probs = jax.nn.softmax(scores, axis=-1)
    probs_low = probs.astype(low)
    ctx = jnp.einsum("hqk,hkd->hqd", probs_low, values, preferred_element_type=full)
    ctx_rows = ctx.transpose(1, 0, 2).reshape(LEN, OWN).astype(low)
    (got_ctx,) = exchange(1, ("seq",), (pad_heads(ctx_rows),))
    context = got_ctx[:, :, :OWN].transpose(1, 0, 2).reshape(LEN, D)

    residual = x + dot(context, w_out) + out_shift
    unit_two, inverse_two = norm_parts(residual)
    normed_two = (unit_two * gain_two + shift_two).astype(low)
    hidden = dot(normed_two, w_up) + up_shift
    active, pull_gelu = jax.vjp(functools.partial(jax.nn.gelu, approximate=False), hidden)
    active_low = active.astype(low)
    out_part = dot(active_low, w_down).astype(low).reshape(G, TOK, D)
    grad_down = t_dot(active_low, dy)
    d_hidden = pull_gelu(dot_t(dy, w_down))[0].astype(low)
    grad_up = t_dot(normed_two, d_hidden)
    grad_up_bias = jnp.sum(d_hidden.astype(full), axis=0)
    d_two_part = dot_t(d_hidden, w_up).astype(low).reshape(G, TOK, D)
    got_two, got_outs = exchange(2, ("seq_sum", "seq_sum"), (d_two_part, out_part))

    def own(array):
        return lax.dynamic_slice_in_dim(array, s * TOK, TOK)

    output = (own(residual) + jnp.sum(got_outs.astype(full), axis=0) + down_shift).astype(low)
    d_two = jnp.sum(got_two.astype(full), axis=0)
    unit_own, cot = own(unit_two), cotangent.astype(full)
    grad_post_gain = jnp.sum(d_two * unit_own, axis=0)
    grad_post_shift = jnp.sum(d_two, axis=0)
    d_residual = cot + norm_back(d_two, gain_two, unit_own, own(inverse_two))
    branch_own = d_residual.astype(low)
    (got_branch,) = exchange(3, ("seq",), (branch_own,))
    branch = got_branch.reshape(LEN, D)
    w_out_own = lax.dynamic_slice_in_dim(w_out, s * OWN, OWN)
    d_ctx = dot_t(branch, w_out_own).astype(low)
    grad_out = t_dot(context, pad_heads(lax.dynamic_slice_in_dim(branch, s * OWN, OWN, 1)))
    d_ctx_heads = d_ctx.reshape(LEN, HEADS, HD).transpose(1, 0, 2)
    d_values = jnp.einsum("hqk,hqd->hkd", probs_low, d_ctx_heads, preferred_element_type=full)
    d_probs = jnp.einsum("hqd,hkd->hqk", d_ctx_heads, values, preferred_element_type=full)
    inner = jnp.sum(d_ctx_heads.astype(full) * ctx, axis=-1, keepdims=True)
    d_scores = (probs * (d_probs - inner)).astype(low)
    d_queries = jnp.einsum("hqk,hkd->hqd", d_scores, keys, preferred_element_type=full) * SCALE
    d_keys = jnp.einsum("hqk,hqd->hkd", d_scores, queries, preferred_element_type=full) * SCALE
    d_proj = jnp.stack([d_queries, d_keys, d_values]).transpose(2, 0, 1, 3).reshape(LEN, 3, OWN)
    d_proj = pad_heads(d_proj).astype(low).reshape(LEN, 3 * PAD)
    grad_in = t_dot(normed, d_proj)
    d_bias = jnp.sum(d_proj.astype(full), axis=0)
    d_one_part = dot_t(d_proj, w_in).astype(low).reshape(G, TOK, D)
    (got_one,) = exchange(4, ("seq_sum",), (d_one_part,))
    d_one = jnp.sum(got_one.astype(full), axis=0)
    unit_first = own(unit_one)
    grad_input = d_residual + norm_back(d_one, gain_one, unit_first, own(inverse_one))
    zero = jnp.zeros((D,), full)
    up_rows = grad_up_bias.reshape(8, 4, ROWS).transpose(1, 0, 2).reshape(4, 8 * ROWS)
    sums = jnp.stack(
        [
            jnp.sum(d_one * unit_first, axis=0),
            jnp.sum(d_one, axis=0),
            grad_post_gain,
            grad_post_shift,
            jnp.sum(branch_own.astype(full), axis=0),
            jnp.sum(cot, axis=0),
            lax.dynamic_update_slice_in_dim(zero, d_bias[:OWN], s * OWN, 0),
            lax.dynamic_update_slice_in_dim(zero, d_bias[2 * PAD : 2 * PAD + OWN], s * OWN, 0),
        ]
    )
    sums_up = lax.dynamic_update_slice_in_dim(jnp.zeros((4, D), full), up_rows, s * OWN, 1)
    sums = jnp.pad(jnp.concatenate([sums, sums_up]), ((0, 116), (0, 0)))
    vec_blocks = sums.T.reshape(N, ROWS, 128)

    def cut(grad):
        return pack(grad.reshape(N, ROWS, -1)).astype(low)

    part_in, part_up, part_out, part_down, part_vec = exchange(
        5,
        ("fan_sum", "fan_sum", "fan_sum", "rows_sum", "fan_sum"),
        (cut(grad_in), cut(grad_up), cut(grad_out), grad_down.astype(low).reshape(8, 96, D), vec_blocks),
    )

    def halves(part):
        wide = part.astype(full).reshape(4, 2, 4, *part.shape[1:])
        wide = jnp.sum(wide, axis=(0, 2))
        mine = lax.dynamic_index_in_dim(wide, x_half(f), keepdims=False)
        other = lax.dynamic_index_in_dim(wide, 1 - x_half(f), keepdims=False)
        return jnp.stack([mine, other])

    share = (
        halves(part_in).astype(low),
        halves(part_up).astype(low),
        halves(part_out).astype(low),
        jnp.sum(part_down.astype(full), axis=0).astype(low),
        jnp.sum(part_vec, axis=0),
    )
    all_in, all_up_g, all_out, all_down, all_vec = exchange(6, ("seq",) * 5, share)

    def groups(parts):
        wide = parts.astype(full)
        swapped = jnp.concatenate([wide[2:, 1], wide[:2, 1]])
        return unpack(wide[:, 0] + swapped)

    final_in = groups(all_in).reshape(G, ROWS, 3, PAD)[..., :OWN].transpose(1, 2, 0, 3)
    final_up = groups(all_up_g).transpose(1, 0, 2).reshape(ROWS, G * FFG)
    final_out = groups(all_out)[..., :OWN].transpose(1, 0, 2).reshape(ROWS, D)
    final_down = jnp.sum(all_down.astype(full), axis=0)
    final_vec = jnp.sum(all_vec, axis=0).T
    return (
        output,
        grad_input.astype(low),
        final_in.reshape(ROWS, 3 * D),
        final_vec[6],
        final_vec[7],
        final_out,
        final_vec[4],
        final_vec[0],
        final_vec[1],
        final_up,
        final_vec[8:12].reshape(96),
        final_down,
        final_vec[5],
        final_vec[2],
        final_vec[3],
    )


def solution(mesh):
    rows, wide, flat = P(("fsdp", "seq"), None), P("fsdp", None), P("fsdp")
    return jax.shard_map(
        on_device,
        mesh=mesh,
        in_specs=(rows, wide, flat, flat, wide, flat, flat, flat, wide, flat, wide, flat, flat, flat, rows),
        out_specs=(rows, rows, wide, flat, flat, wide, flat, flat, flat, wide, flat, wide, flat, flat, flat),
        check_vma=False,
    )
```

```python
import functools
import math

import jax
import jax.numpy as jnp
from jax import lax
from jax.experimental import pallas as pl
from jax.experimental.pallas import tpu as pltpu
from jax.sharding import PartitionSpec as P

D = 768
H = 12
HD = 64
N = 32
G = 4
ROWS = 24
LEN = 1024
TOK = 256
HEADS = 3
OWN = HEADS * HD
PAD = 256
FFG = 768
epsilon = 1e-05
SCALE = 1.0 / math.sqrt(HD)
MESH = pl.DeviceIdType.MESH


def x_half(f):
    return lax.rem(f // 4, 2)


def place():
    return lax.axis_index("fsdp"), lax.axis_index("seq")


def fan_peer(f, s, t):
    peer = lax.rem(f + t, N)
    return peer, lax.rem(s + 2 * lax.abs(x_half(peer) - x_half(f)), G)


def row_server(f, s, i):
    owner = 8 * s + i
    away = lax.abs(x_half(owner) - x_half(f))
    lo = lax.rem(s // 2 + away, 2)
    return owner, 2 * lo + lax.rem(f, 2)


def row_client(f, s, m):
    group = f // 8
    away = lax.abs(s // 2 - group // 2)
    half = lax.rem(x_half(f) + away, 2)
    return (m // 2) * 8 + half * 4 + lax.rem(m, 2) * 2 + lax.rem(s, 2), group


def client_slot(f):
    return (f // 8) * 2 + lax.rem(f, 4) // 2


def send(src, dst, send_sem, recv_sem, f, s):
    pltpu.make_async_remote_copy(
        src_ref=src,
        dst_ref=dst,
        send_sem=send_sem,
        recv_sem=recv_sem,
        device_id=(f, s),
        device_id_type=MESH,
    ).start()


def take(ref, sem):
    pltpu.make_async_copy(ref, ref, sem).wait()


def loop(count, body):
    lax.fori_loop(0, count, lambda t, carry: (body(t), carry)[1], 0)


def greet(barrier, f, s):
    pl.semaphore_signal(barrier, inc=1, device_id=(f, s), device_id_type=MESH)


def greet_fan(barrier, f, s):
    loop(N - 1, lambda t: greet(barrier, *fan_peer(f, s, t + 1)))
    return N - 1


def greet_seq(barrier, f, s):
    loop(G - 1, lambda t: greet(barrier, f, lax.rem(s + t + 1, G)))
    return G - 1


def unless_self(f, s, peer, action):
    @pl.when(jnp.logical_or(peer[0] != f, peer[1] != s))
    def _():
        action(*peer)


def serves_self(f, s):
    return jnp.logical_and(f // 8 == s, row_server(f, s, lax.rem(f, 8))[1] == s)


def greet_rows(barrier, f, s, summed):
    peers = row_client if summed else row_server
    loop(8, lambda i: unless_self(f, s, peers(f, s, i), functools.partial(greet, barrier)))
    return 8 - serves_self(f, s).astype(jnp.int32)


def start_fan(kind, src, dst, sems, k, f, s):
    ss, rs, own = [group.at[k] for group in sems]
    block = {"fan": lambda pf, ps: src.at[ps], "fan_sum": lambda pf, ps: src.at[pf]}.get(kind, lambda pf, ps: src)

    def one(t):
        pf, ps = fan_peer(f, s, t + 1)
        send(block(pf, ps), dst.at[f], ss, rs, pf, ps)

    loop(N - 1, one)
    pltpu.make_async_copy(block(f, s), dst.at[f], own).start()


def start_seq(kind, src, dst, sems, k, f, s):
    ss, rs, own = [group.at[k] for group in sems]
    block = (lambda ps: src) if kind == "seq" else (lambda ps: src.at[ps])

    def one(t):
        ps = lax.rem(s + t + 1, G)
        send(block(ps), dst.at[s], ss, rs, f, ps)

    loop(G - 1, one)
    pltpu.make_async_copy(block(s), dst.at[s], own).start()


def start_rows(kind, src, dst, sems, k, f, s):
    ss, rs, own = [group.at[k] for group in sems]
    if kind == "rows":

        def one(m):
            unless_self(f, s, row_client(f, s, m), functools.partial(send, src, dst.at[lax.rem(f, 8)], ss, rs))
    else:

        def one(i):
            unless_self(
                f, s, row_server(f, s, i), functools.partial(send, src.at[i], dst.at[client_slot(f)], ss, rs)
            )

    loop(8, one)

    @pl.when(serves_self(f, s))
    def _():
        if kind == "rows":
            pltpu.make_async_copy(src, dst.at[lax.rem(f, 8)], own).start()
        else:
            pltpu.make_async_copy(src.at[lax.rem(f, 8)], dst.at[client_slot(f)], own).start()


def start(kind, *args):
    (start_fan if kind.startswith("fan") else start_seq if kind.startswith("seq") else start_rows)(kind, *args)


def finish(kind, dst, sems, k, f, s, part):
    ss, rs, own = [group.at[k] for group in sems]
    remote = rs if part == "recv" else ss
    if kind.startswith("rows"):

        @pl.when(serves_self(f, s))
        def _():
            if part == "recv":
                take(dst.at[0], own)
            take(dst.at[pl.ds(0, 7)], remote)

        @pl.when(jnp.logical_not(serves_self(f, s)))
        def _():
            take(dst, remote)
    else:
        if part == "recv":
            take(dst.at[0], own)
        take(dst.at[pl.ds(0, dst.shape[0] - 1)], remote)


def exchange_kernel(kinds, *refs):
    n = len(kinds)
    srcs, dsts, sems = refs[:n], refs[n : 2 * n], refs[2 * n :]
    f, s = place()
    barrier = pltpu.get_barrier_semaphore()
    expected = 0
    if any(k.startswith("fan") for k in kinds):
        expected += greet_fan(barrier, f, s)
    if any(k.startswith("seq") for k in kinds):
        expected += greet_seq(barrier, f, s)
    if "rows" in kinds:
        expected += greet_rows(barrier, f, s, False)
    if "rows_sum" in kinds:
        expected += greet_rows(barrier, f, s, True)
    pl.semaphore_wait(barrier, expected)
    for k, kind in enumerate(kinds):
        start(kind, srcs[k], dsts[k], sems, k, f, s)
    for k, kind in enumerate(kinds):
        finish(kind, dsts[k], sems, k, f, s, "recv")
        finish(kind, dsts[k], sems, k, f, s, "send")


def exchange(collective_id, kinds, arrays):
    shapes = []
    for kind, array in zip(kinds, arrays):
        block = array.shape if kind in ("fan_whole", "seq", "rows") else array.shape[1:]
        count = N if kind.startswith("fan") else G if kind.startswith("seq") else 8
        shapes.append(jax.ShapeDtypeStruct((count,) + block, array.dtype))
    n = len(kinds)
    return pl.pallas_call(
        functools.partial(exchange_kernel, kinds),
        out_shape=shapes,
        in_specs=[pl.BlockSpec(memory_space=pl.ANY)] * n,
        out_specs=[pl.BlockSpec(memory_space=pl.ANY)] * n,
        scratch_shapes=[pltpu.SemaphoreType.DMA((n,))] * 3,
        compiler_params=pltpu.CompilerParams(collective_id=collective_id, has_side_effects=True),
    )(*arrays)


def pack(blocks):
    c = blocks.shape[-1] // 2
    return jnp.concatenate([blocks[..., :c], blocks[..., c:]], axis=-2)


def unpack(blocks):
    return jnp.concatenate([blocks[..., :ROWS, :], blocks[..., ROWS:, :]], axis=-1)


def pad_heads(blocks):
    return jnp.pad(blocks, [(0, 0)] * (blocks.ndim - 1) + [(0, PAD - OWN)])


def norm_parts(values):
    center = jnp.mean(values, axis=-1, keepdims=True)
    centered = values - center
    spread = jnp.mean(centered * centered, axis=-1, keepdims=True)
    inverse = lax.rsqrt(spread + epsilon)
    return centered * inverse, inverse


def norm_back(grad, gain, unit, inverse):
    scaled = grad * gain
    mean_one = jnp.mean(scaled, axis=-1, keepdims=True)
    mean_two = jnp.mean(scaled * unit, axis=-1, keepdims=True)
    return inverse * (scaled - mean_one - unit * mean_two)


def dot(a, b):
    return jnp.dot(a, b, preferred_element_type=jnp.float32)


def dot_t(a, b):
    return lax.dot_general(a, b, (((1,), (1,)), ((), ())), preferred_element_type=jnp.float32)


def t_dot(a, b):
    return lax.dot_general(a, b, (((0,), (0,)), ((), ())), preferred_element_type=jnp.float32)


def tile(t, size=TOK):
    return pl.ds(pl.multiple_of(t * size, size), size)


def unpack_into(packed, wide):
    c = packed.shape[-1]

    def pair(p):
        one = packed[2 * p].astype(jnp.float32)
        two = packed[2 * p + 1].astype(jnp.float32)
        rows = pl.ds(pl.multiple_of(48 * p, 48), 48)
        wide[rows, :c] = jnp.concatenate([one[:ROWS], two[:ROWS]], axis=0).astype(wide.dtype)
        wide[rows, c:] = jnp.concatenate([one[ROWS:], two[ROWS:]], axis=0).astype(wide.dtype)

    loop(N // 2, pair)


def lanes_of(h, shape):
    lane = lax.broadcasted_iota(jnp.int32, shape, 1)
    return lane < HD if h % 2 == 0 else lane >= HD


def only(h, block):
    return jnp.where(lanes_of(h, block.shape), block, jnp.zeros_like(block))


def causal(scores, offset):
    row = offset + lax.broadcasted_iota(jnp.int32, scores.shape, 0)
    col = lax.broadcasted_iota(jnp.int32, scores.shape, 1)
    return jnp.where(col <= row, scores, -1e9)


def forward_kernel(
    src_in, src_vec, src_x, src_out, src_up, src_down, src_dy,
    got_x, vec, normed, qkv, w_in, lse, got_ctx, got_out, got_up, got_down, got_dy,
    got_in, got_vec, ss, rs, own, ctx_ss, ctx_rs,
):
    f, s = place()
    sems = (ss, rs, own)
    barrier = pltpu.get_barrier_semaphore()
    expected = greet_fan(barrier, f, s) + greet_seq(barrier, f, s) + greet_rows(barrier, f, s, False)
    pl.semaphore_wait(barrier, expected)
    plan = (
        ("seq", src_x, got_x),
        ("fan_whole", src_vec, got_vec),
        ("fan", src_in, got_in),
        ("fan_whole", src_out, got_out),
        ("fan", src_up, got_up),
        ("rows", src_down, got_down),
        ("seq", src_dy, got_dy),
    )
    for k, (kind, src, dst) in enumerate(plan):
        start(kind, src, dst, sems, k, f, s)
    finish("seq", got_x, sems, 0, f, s, "recv")
    finish("fan_whole", got_vec, sems, 1, f, s, "recv")
    vec[...] = jnp.zeros_like(vec)

    def add_vec(j):
        vec[...] += got_vec[j].astype(jnp.float32)

    loop(N, add_vec)
    gain, shift = vec[0:1, :], vec[1:2, :]

    def norm_tile(t):
        unit, _ = norm_parts(got_x[t].astype(jnp.float32))
        normed[tile(t), :] = (unit * gain + shift).astype(normed.dtype)

    loop(G, norm_tile)
    finish("fan", got_in, sems, 2, f, s, "recv")
    unpack_into(got_in, w_in)
    bias = vec[pl.ds(10 + s, 1), :]

    def project(t):
        made = (dot(normed[tile(t), :], w_in[...]) + bias).astype(qkv.dtype)
        qkv[tile(t), :PAD] = (made[:, :PAD].astype(jnp.float32) * SCALE).astype(qkv.dtype)
        qkv[tile(t), PAD:] = made[:, PAD:]

    loop(G, project)
    for step, b in enumerate((3, 2, 1, 0)):
        rows, span = slice(b * TOK, (b + 1) * TOK), (b + 1) * TOK
        for pair in range(2):
            at = pair * 128
            made = None
            for h in range(2 * pair, min(2 * pair + 2, HEADS)):
                query = only(h, qkv[rows, at : at + 128])
                scores = causal(dot_t(query, qkv[:span, PAD + at : PAD + at + 128]), b * TOK)
                peak = jnp.max(scores, axis=-1, keepdims=True)
                weights = jnp.exp(scores - peak)
                total = jnp.sum(weights, axis=-1, keepdims=True)
                lse[h, rows, :] = peak + jnp.log(total)
                part = dot(weights.astype(qkv.dtype), qkv[:span, 2 * PAD + at : 2 * PAD + at + 128]) / total
                made = part if made is None else jnp.where(lanes_of(h, part.shape), part, made)
            got_ctx[s, rows, at : at + 128] = made.astype(got_ctx.dtype)

        def share(t, b=b, step=step):
            block = got_ctx.at[s, pl.ds(b * TOK, TOK)]
            send(block, block, ctx_ss.at[step], ctx_rs.at[step], f, lax.rem(s + t + 1, G))

        loop(G - 1, share)
    for step in range(G):
        three = got_ctx.at[0, pl.ds(0, 3 * TOK)]
        take(three, ctx_rs.at[step])
        take(three, ctx_ss.at[step])
    for k, (kind, src, dst) in enumerate(plan):
        if k > 2:
            finish(kind, dst, sems, k, f, s, "recv")
        finish(kind, dst, sems, k, f, s, "send")


def forward(send_in, spread, inputs, send_out, send_up, down_weight, cotangent):
    low, full = jnp.bfloat16, jnp.float32
    any_space, vmem = pl.BlockSpec(memory_space=pl.ANY), pl.BlockSpec(memory_space=pltpu.VMEM)
    shape = jax.ShapeDtypeStruct
    outs = (
        (shape((G, TOK, D), low), vmem),
        (shape((16, D), full), vmem),
        (shape((LEN, D), low), vmem),
        (shape((LEN, 3 * PAD), low), vmem),
        (shape((D, 3 * PAD), low), vmem),
        (shape((HEADS, LEN, 1), full), vmem),
        (shape((G, LEN, PAD), low), vmem),
        (shape((N, 48, 384), low), any_space),
        (shape((N, 48, 384), low), any_space),
        (shape((8, 96, D), low), any_space),
        (shape((G, TOK, D), low), any_space),
    )
    return pl.pallas_call(
        forward_kernel,
        out_shape=[o[0] for o in outs],
        in_specs=[any_space] * 7,
        out_specs=[o[1] for o in outs],
        scratch_shapes=[
            pltpu.VMEM((N, 48, 384), low),
            pltpu.VMEM((N, 16, D), low),
        ]
        + [pltpu.SemaphoreType.DMA((7,))] * 3
        + [pltpu.SemaphoreType.DMA((G,))] * 2,
        compiler_params=pltpu.CompilerParams(
            collective_id=0, has_side_effects=True, vmem_limit_bytes=48 * 2**20
        ),
    )(send_in, spread, inputs, send_out, send_up, down_weight, cotangent)


def on_device(
    inputs,
    proj_in,
    bias_query,
    bias_value,
    proj_out,
    bias_out,
    norm_gain,
    norm_shift,
    up_weight,
    up_bias,
    down_weight,
    down_bias,
    post_gain,
    post_shift,
    cotangent,
):
    low = jnp.bfloat16
    full = jnp.float32
    f, s = place()
    split = proj_in.reshape(ROWS, 3, G, OWN).transpose(2, 0, 1, 3)
    send_in = pack(pad_heads(split).reshape(G, ROWS, 3 * PAD))
    send_up = pack(up_weight.reshape(ROWS, G, FFG).transpose(1, 0, 2))
    send_out = pack(proj_out)
    vectors = jnp.stack([norm_gain, norm_shift, post_gain, post_shift, bias_out, down_bias])
    lane = jnp.arange(D)[None, :]
    zero = jnp.zeros((), low)
    spread_one = jnp.where(lane // ROWS == f, jnp.tile(vectors, (1, N)), zero)
    mine = (jnp.arange(G) == f // 8)[:, None]
    spread_up = jnp.where(mine & (lane // 96 == lax.rem(f, 8)), jnp.tile(up_bias, 8)[None, :], zero)
    query_rows, value_rows = [jnp.pad(jnp.tile(b, 8), (0, PAD - OWN)) for b in (bias_query, bias_value)]
    qkv_rows = jnp.concatenate([query_rows, jnp.zeros((PAD,), low), value_rows])[None, :]
    spread_qkv = jnp.where(mine & (lane % PAD // ROWS == lax.rem(f, 8)), qkv_rows, zero)
    spread = jnp.concatenate([spread_one, spread_up, spread_qkv, jnp.zeros((2, D), low)])
    got_x, vec, normed, qkv, w_in, lse, got_ctx, got_out, got_up, got_down, got_dy = forward(
        send_in, spread, inputs, send_out, send_up, down_weight, cotangent
    )
    w_up = unpack(got_up).reshape(D, FFG)
    w_out = unpack(got_out).reshape(D, D)
    w_down = got_down.reshape(FFG, D)
    gain_one, shift_one, gain_two, shift_two, out_shift, down_shift = [vec[i] for i in range(6)]
    up_shift = lax.dynamic_index_in_dim(vec, 6 + s, keepdims=False)

    x = got_x.reshape(LEN, D).astype(full)
    dy = got_dy.reshape(LEN, D)
    unit_one, inverse_one = norm_parts(x)
    heads = qkv.reshape(LEN, 3, PAD)[:, :, :OWN].reshape(LEN, 3, HEADS, HD).transpose(1, 2, 0, 3)
    queries, keys, values = heads[0], heads[1], heads[2]
    scores = jnp.einsum("hqd,hkd->hqk", queries, keys, preferred_element_type=full)
    mask = jnp.arange(LEN)[None, :] <= jnp.arange(LEN)[:, None]
    probs = jnp.exp(jnp.where(mask, scores, -1e9) - lse)
    probs_low = probs.astype(low)
    context = got_ctx[:, :, :OWN].transpose(1, 0, 2).reshape(LEN, D)

    residual = x + dot(context, w_out) + out_shift
    unit_two, inverse_two = norm_parts(residual)
    normed_two = (unit_two * gain_two + shift_two).astype(low)
    hidden = dot(normed_two, w_up) + up_shift
    active, pull_gelu = jax.vjp(functools.partial(jax.nn.gelu, approximate=False), hidden)
    active_low = active.astype(low)
    out_part = dot(active_low, w_down).astype(low).reshape(G, TOK, D)
    grad_down = t_dot(active_low, dy)
    d_hidden = pull_gelu(dot_t(dy, w_down))[0].astype(low)
    grad_up = t_dot(normed_two, d_hidden)
    grad_up_bias = jnp.sum(d_hidden.astype(full), axis=0)
    d_two_part = dot_t(d_hidden, w_up).astype(low).reshape(G, TOK, D)
    got_two, got_outs = exchange(2, ("seq_sum", "seq_sum"), (d_two_part, out_part))

    def own(array):
        return lax.dynamic_slice_in_dim(array, s * TOK, TOK)

    output = (own(residual) + jnp.sum(got_outs.astype(full), axis=0) + down_shift).astype(low)
    d_two = jnp.sum(got_two.astype(full), axis=0)
    unit_own, cot = own(unit_two), cotangent.astype(full)
    grad_post_gain = jnp.sum(d_two * unit_own, axis=0)
    grad_post_shift = jnp.sum(d_two, axis=0)
    d_residual = cot + norm_back(d_two, gain_two, unit_own, own(inverse_two))
    branch_own = d_residual.astype(low)
    (got_branch,) = exchange(3, ("seq",), (branch_own,))
    branch = got_branch.reshape(LEN, D)
    w_out_own = lax.dynamic_slice_in_dim(w_out, s * OWN, OWN)
    d_ctx = dot_t(branch, w_out_own).astype(low)
    grad_out = t_dot(context, pad_heads(lax.dynamic_slice_in_dim(branch, s * OWN, OWN, 1)))
    d_ctx_heads = d_ctx.reshape(LEN, HEADS, HD).transpose(1, 0, 2)
    d_values = jnp.einsum("hqk,hqd->hkd", probs_low, d_ctx_heads, preferred_element_type=full)
    d_probs = jnp.einsum("hqd,hkd->hqk", d_ctx_heads, values, preferred_element_type=full)
    inner = jnp.sum(probs * d_probs, axis=-1, keepdims=True)
    d_scores = (probs * (d_probs - inner)).astype(low)
    d_queries = jnp.einsum("hqk,hkd->hqd", d_scores, keys, preferred_element_type=full) * SCALE
    d_keys = jnp.einsum("hqk,hqd->hkd", d_scores, queries, preferred_element_type=full)
    d_proj = jnp.stack([d_queries, d_keys, d_values]).transpose(2, 0, 1, 3).reshape(LEN, 3, OWN)
    d_proj = pad_heads(d_proj).astype(low).reshape(LEN, 3 * PAD)
    grad_in = t_dot(normed, d_proj)
    d_bias = jnp.sum(d_proj.astype(full), axis=0)
    d_one_part = dot_t(d_proj, w_in).astype(low).reshape(G, TOK, D)
    (got_one,) = exchange(4, ("seq_sum",), (d_one_part,))
    d_one = jnp.sum(got_one.astype(full), axis=0)
    unit_first = own(unit_one)
    grad_input = d_residual + norm_back(d_one, gain_one, unit_first, own(inverse_one))
    zero = jnp.zeros((D,), full)
    up_rows = grad_up_bias.reshape(8, 4, ROWS).transpose(1, 0, 2).reshape(4, 8 * ROWS)
    sums = jnp.stack(
        [
            jnp.sum(d_one * unit_first, axis=0),
            jnp.sum(d_one, axis=0),
            grad_post_gain,
            grad_post_shift,
            jnp.sum(branch_own.astype(full), axis=0),
            jnp.sum(cot, axis=0),
            lax.dynamic_update_slice_in_dim(zero, d_bias[:OWN], s * OWN, 0),
            lax.dynamic_update_slice_in_dim(zero, d_bias[2 * PAD : 2 * PAD + OWN], s * OWN, 0),
        ]
    )
    sums_up = lax.dynamic_update_slice_in_dim(jnp.zeros((4, D), full), up_rows, s * OWN, 1)
    sums = jnp.pad(jnp.concatenate([sums, sums_up]), ((0, 116), (0, 0)))
    vec_blocks = sums.T.reshape(N, ROWS, 128)

    def cut(grad):
        return pack(grad.reshape(N, ROWS, -1)).astype(low)

    part_in, part_up, part_out, part_down, part_vec = exchange(
        5,
        ("fan_sum", "fan_sum", "fan_sum", "rows_sum", "fan_sum"),
        (cut(grad_in), cut(grad_up), cut(grad_out), grad_down.astype(low).reshape(8, 96, D), vec_blocks),
    )

    def halves(part):
        wide = part.astype(full).reshape(4, 2, 4, *part.shape[1:])
        wide = jnp.sum(wide, axis=(0, 2))
        mine = lax.dynamic_index_in_dim(wide, x_half(f), keepdims=False)
        other = lax.dynamic_index_in_dim(wide, 1 - x_half(f), keepdims=False)
        return jnp.stack([mine, other])

    share = (
        halves(part_in).astype(low),
        halves(part_up).astype(low),
        halves(part_out).astype(low),
        jnp.sum(part_down.astype(full), axis=0).astype(low),
        jnp.sum(part_vec, axis=0),
    )
    all_in, all_up_g, all_out, all_down, all_vec = exchange(6, ("seq",) * 5, share)

    def groups(parts):
        wide = parts.astype(full)
        swapped = jnp.concatenate([wide[2:, 1], wide[:2, 1]])
        return unpack(wide[:, 0] + swapped)

    final_in = groups(all_in).reshape(G, ROWS, 3, PAD)[..., :OWN].transpose(1, 2, 0, 3)
    final_up = groups(all_up_g).transpose(1, 0, 2).reshape(ROWS, G * FFG)
    final_out = groups(all_out)[..., :OWN].transpose(1, 0, 2).reshape(ROWS, D)
    final_down = jnp.sum(all_down.astype(full), axis=0)
    final_vec = jnp.sum(all_vec, axis=0).T
    return (
        output,
        grad_input.astype(low),
        final_in.reshape(ROWS, 3 * D),
        final_vec[6],
        final_vec[7],
        final_out,
        final_vec[4],
        final_vec[0],
        final_vec[1],
        final_up,
        final_vec[8:12].reshape(96),
        final_down,
        final_vec[5],
        final_vec[2],
        final_vec[3],
    )


def solution(mesh):
    rows, wide, flat = P(("fsdp", "seq"), None), P("fsdp", None), P("fsdp")
    return jax.shard_map(
        on_device,
        mesh=mesh,
        in_specs=(rows, wide, flat, flat, wide, flat, flat, flat, wide, flat, wide, flat, flat, flat, rows),
        out_specs=(rows, rows, wide, flat, flat, wide, flat, flat, flat, wide, flat, wide, flat, flat, flat),
        check_vma=False,
    )
```

```python
import functools
import math

import jax
import jax.numpy as jnp
from jax import lax
from jax.experimental import pallas as pl
from jax.experimental.pallas import tpu as pltpu
from jax.sharding import PartitionSpec as P

D = 768
H = 12
HD = 64
N = 32
G = 4
ROWS = 24
LEN = 1024
TOK = 256
HEADS = 3
OWN = HEADS * HD
PAD = 256
FFG = 768
epsilon = 1e-05
SCALE = 1.0 / math.sqrt(HD)
MESH = pl.DeviceIdType.MESH


def x_half(f):
    return lax.rem(f // 4, 2)


def place():
    return lax.axis_index("fsdp"), lax.axis_index("seq")


def fan_peer(f, s, t):
    peer = lax.rem(f + t, N)
    return peer, lax.rem(s + 2 * lax.abs(x_half(peer) - x_half(f)), G)


def row_server(f, s, i):
    owner = 8 * s + i
    away = lax.abs(x_half(owner) - x_half(f))
    lo = lax.rem(s // 2 + away, 2)
    return owner, 2 * lo + lax.rem(f, 2)


def row_client(f, s, m):
    group = f // 8
    away = lax.abs(s // 2 - group // 2)
    half = lax.rem(x_half(f) + away, 2)
    return (m // 2) * 8 + half * 4 + lax.rem(m, 2) * 2 + lax.rem(s, 2), group


def client_slot(f):
    return (f // 8) * 2 + lax.rem(f, 4) // 2


def send(src, dst, send_sem, recv_sem, f, s):
    pltpu.make_async_remote_copy(
        src_ref=src,
        dst_ref=dst,
        send_sem=send_sem,
        recv_sem=recv_sem,
        device_id=(f, s),
        device_id_type=MESH,
    ).start()


def take(ref, sem):
    pltpu.make_async_copy(ref, ref, sem).wait()


def loop(count, body):
    lax.fori_loop(0, count, lambda t, carry: (body(t), carry)[1], 0)


def greet(barrier, f, s):
    pl.semaphore_signal(barrier, inc=1, device_id=(f, s), device_id_type=MESH)


def greet_fan(barrier, f, s):
    loop(N - 1, lambda t: greet(barrier, *fan_peer(f, s, t + 1)))
    return N - 1


def greet_seq(barrier, f, s):
    loop(G - 1, lambda t: greet(barrier, f, lax.rem(s + t + 1, G)))
    return G - 1


def unless_self(f, s, peer, action):
    @pl.when(jnp.logical_or(peer[0] != f, peer[1] != s))
    def _():
        action(*peer)


def serves_self(f, s):
    return jnp.logical_and(f // 8 == s, row_server(f, s, lax.rem(f, 8))[1] == s)


def greet_rows(barrier, f, s, summed):
    peers = row_client if summed else row_server
    loop(8, lambda i: unless_self(f, s, peers(f, s, i), functools.partial(greet, barrier)))
    return 8 - serves_self(f, s).astype(jnp.int32)


def start_fan(kind, src, dst, sems, k, f, s):
    ss, rs, own = [group.at[k] for group in sems]
    block = {"fan": lambda pf, ps: src.at[ps], "fan_sum": lambda pf, ps: src.at[pf]}.get(kind, lambda pf, ps: src)

    def one(t):
        pf, ps = fan_peer(f, s, t + 1)
        send(block(pf, ps), dst.at[f], ss, rs, pf, ps)

    loop(N - 1, one)
    pltpu.make_async_copy(block(f, s), dst.at[f], own).start()


def start_seq(kind, src, dst, sems, k, f, s):
    ss, rs, own = [group.at[k] for group in sems]
    block = (lambda ps: src) if kind == "seq" else (lambda ps: src.at[ps])

    def one(t):
        ps = lax.rem(s + t + 1, G)
        send(block(ps), dst.at[s], ss, rs, f, ps)

    loop(G - 1, one)
    pltpu.make_async_copy(block(s), dst.at[s], own).start()


def start_rows(kind, src, dst, sems, k, f, s):
    ss, rs, own = [group.at[k] for group in sems]
    if kind == "rows":

        def one(m):
            unless_self(f, s, row_client(f, s, m), functools.partial(send, src, dst.at[lax.rem(f, 8)], ss, rs))
    else:

        def one(i):
            unless_self(
                f, s, row_server(f, s, i), functools.partial(send, src.at[i], dst.at[client_slot(f)], ss, rs)
            )

    loop(8, one)

    @pl.when(serves_self(f, s))
    def _():
        if kind == "rows":
            pltpu.make_async_copy(src, dst.at[lax.rem(f, 8)], own).start()
        else:
            pltpu.make_async_copy(src.at[lax.rem(f, 8)], dst.at[client_slot(f)], own).start()


def start(kind, *args):
    (start_fan if kind.startswith("fan") else start_seq if kind.startswith("seq") else start_rows)(kind, *args)


def finish(kind, dst, sems, k, f, s, part):
    ss, rs, own = [group.at[k] for group in sems]
    remote = rs if part == "recv" else ss
    if kind.startswith("rows"):

        @pl.when(serves_self(f, s))
        def _():
            if part == "recv":
                take(dst.at[0], own)
            take(dst.at[pl.ds(0, 7)], remote)

        @pl.when(jnp.logical_not(serves_self(f, s)))
        def _():
            take(dst, remote)
    else:
        if part == "recv":
            take(dst.at[0], own)
        take(dst.at[pl.ds(0, dst.shape[0] - 1)], remote)


def exchange_kernel(kinds, *refs):
    n = len(kinds)
    srcs, dsts, sems = refs[:n], refs[n : 2 * n], refs[2 * n :]
    f, s = place()
    barrier = pltpu.get_barrier_semaphore()
    expected = 0
    if any(k.startswith("fan") for k in kinds):
        expected += greet_fan(barrier, f, s)
    if any(k.startswith("seq") for k in kinds):
        expected += greet_seq(barrier, f, s)
    if "rows" in kinds:
        expected += greet_rows(barrier, f, s, False)
    if "rows_sum" in kinds:
        expected += greet_rows(barrier, f, s, True)
    pl.semaphore_wait(barrier, expected)
    for k, kind in enumerate(kinds):
        start(kind, srcs[k], dsts[k], sems, k, f, s)
    for k, kind in enumerate(kinds):
        finish(kind, dsts[k], sems, k, f, s, "recv")
        finish(kind, dsts[k], sems, k, f, s, "send")


def exchange(collective_id, kinds, arrays):
    shapes = []
    for kind, array in zip(kinds, arrays):
        block = array.shape if kind in ("fan_whole", "seq", "rows") else array.shape[1:]
        count = N if kind.startswith("fan") else G if kind.startswith("seq") else 8
        shapes.append(jax.ShapeDtypeStruct((count,) + block, array.dtype))
    n = len(kinds)
    return pl.pallas_call(
        functools.partial(exchange_kernel, kinds),
        out_shape=shapes,
        in_specs=[pl.BlockSpec(memory_space=pl.ANY)] * n,
        out_specs=[pl.BlockSpec(memory_space=pl.ANY)] * n,
        scratch_shapes=[pltpu.SemaphoreType.DMA((n,))] * 3,
        compiler_params=pltpu.CompilerParams(collective_id=collective_id, has_side_effects=True),
    )(*arrays)


def pack(blocks):
    c = blocks.shape[-1] // 2
    return jnp.concatenate([blocks[..., :c], blocks[..., c:]], axis=-2)


def unpack(blocks):
    return jnp.concatenate([blocks[..., :ROWS, :], blocks[..., ROWS:, :]], axis=-1)


def pad_heads(blocks):
    return jnp.pad(blocks, [(0, 0)] * (blocks.ndim - 1) + [(0, PAD - OWN)])


def norm_parts(values):
    center = jnp.mean(values, axis=-1, keepdims=True)
    centered = values - center
    spread = jnp.mean(centered * centered, axis=-1, keepdims=True)
    inverse = lax.rsqrt(spread + epsilon)
    return centered * inverse, inverse


def norm_back(grad, gain, unit, inverse):
    scaled = grad * gain
    mean_one = jnp.mean(scaled, axis=-1, keepdims=True)
    mean_two = jnp.mean(scaled * unit, axis=-1, keepdims=True)
    return inverse * (scaled - mean_one - unit * mean_two)


def dot(a, b):
    return jnp.dot(a, b, preferred_element_type=jnp.float32)


def dot_t(a, b):
    return lax.dot_general(a, b, (((1,), (1,)), ((), ())), preferred_element_type=jnp.float32)


def t_dot(a, b):
    return lax.dot_general(a, b, (((0,), (0,)), ((), ())), preferred_element_type=jnp.float32)


def tile(t, size=TOK):
    return pl.ds(pl.multiple_of(t * size, size), size)


def unpack_into(packed, wide):
    c = packed.shape[-1]

    def pair(p):
        one = packed[2 * p].astype(jnp.float32)
        two = packed[2 * p + 1].astype(jnp.float32)
        rows = pl.ds(pl.multiple_of(48 * p, 48), 48)
        wide[rows, :c] = jnp.concatenate([one[:ROWS], two[:ROWS]], axis=0).astype(wide.dtype)
        wide[rows, c:] = jnp.concatenate([one[ROWS:], two[ROWS:]], axis=0).astype(wide.dtype)

    loop(N // 2, pair)


def lanes_of(h, shape):
    lane = lax.broadcasted_iota(jnp.int32, shape, 1)
    return lane < HD if h % 2 == 0 else lane >= HD


def only(h, block):
    return jnp.where(lanes_of(h, block.shape), block, jnp.zeros_like(block))


def causal(scores, offset):
    row = offset + lax.broadcasted_iota(jnp.int32, scores.shape, 0)
    col = lax.broadcasted_iota(jnp.int32, scores.shape, 1)
    return jnp.where(col <= row, scores, -1e9)


class Ring:
    def __init__(self, src, held, sends, recvs, own, order, f, s):
        self.src, self.held, self.sends, self.recvs, self.own = src, held, sends, recvs, own
        self.order, self.f, self.s = order, f, s
        self.y, self.h, self.z = f // 8, x_half(f), lax.rem(f, 4)

    def peer(self, axis, step):
        if axis == "y":
            return lax.rem(self.y + step + 4, 4) * 8 + lax.rem(self.f, 8), self.s
        return self.f - self.z + lax.rem(self.z + step + 4, 4), self.s

    def coordinate(self, axis, step):
        return lax.rem((self.y if axis == "y" else self.z) + step + 4, 4)

    def one(self, axis, step, half=None):
        i = self.coordinate(axis, step)
        halves = slice(None) if half is None else half
        return self.held.at[i, halves, self.z] if axis == "y" else self.held.at[self.y, halves, i]

    def many(self, axis, step, half=None):
        i = self.coordinate(axis, step)
        if axis == "y":
            return self.held.at[i] if half is None else self.held.at[i, half]
        rows = slice(None) if half is None else slice(2 * half, 2 * half + 2)
        return self.held.at[rows, slice(None), i]

    def push(self, block, k, peer):
        send(block, block, self.sends.at[k], self.recvs.at[k], *peer)

    def begin(self):
        mine = self.held.at[self.y, self.h, self.z]
        other = lax.rem(self.s + 2, G)
        send(
            self.src.at[other], mine, self.sends.at[0], self.recvs.at[0], self.f + 4 - 8 * self.h, other
        )
        pltpu.make_async_copy(self.src.at[self.s], mine, self.own.at[0]).start()

    def first(self):
        mine = self.held.at[self.y, self.h, self.z]
        take(mine, self.own.at[0])
        take(mine, self.recvs.at[0])
        axis = self.order[0]
        self.push(self.one(axis, 0), 1, self.peer(axis, 1))
        self.push(self.one(axis, 0), 2, self.peer(axis, -1))

    def relay(self, part, base, axis):
        take(part(axis, -1), self.recvs.at[base])
        self.push(part(axis, -1, 0), base + 2, self.peer(axis, 1))
        take(part(axis, 1), self.recvs.at[base + 1])
        self.push(part(axis, 1, 1), base + 3, self.peer(axis, -1))

    def first_relay(self):
        self.relay(self.one, 1, self.order[0])

    def last(self):
        axis = self.order[0]
        take(self.one(axis, 2, 0), self.recvs.at[3])
        take(self.one(axis, 2, 1), self.recvs.at[4])
        axis = self.order[1]
        self.push(self.many(axis, 0), 5, self.peer(axis, 1))
        self.push(self.many(axis, 0), 6, self.peer(axis, -1))

    def last_relay(self):
        self.relay(self.many, 5, self.order[1])

    def arrive(self):
        axis = self.order[1]
        take(self.many(axis, 2, 0), self.recvs.at[7])
        take(self.many(axis, 2, 1), self.recvs.at[8])

    def drain(self):
        one, many = self.order
        take(self.held.at[self.y, self.h, self.z], self.sends.at[0])
        for k in (1, 2):
            take(self.one(one, 0), self.sends.at[k])
            take(self.one(one, 0, 0), self.sends.at[k + 2])
            take(self.many(many, 0), self.sends.at[k + 4])
            take(self.many(many, 0, 0), self.sends.at[k + 6])


class Share:
    def __init__(self, block, sends, recvs, f, s):
        self.block, self.sends, self.recvs, self.f, self.s = block, sends, recvs, f, s
        self.twin = s + 1 - 2 * lax.rem(s, 2)
        self.across = lax.rem(s + 2, G)

    def begin(self):
        mine = self.block(self.s)
        send(mine, mine, self.sends.at[1], self.recvs.at[1], self.f, self.across)
        send(mine, mine, self.sends.at[0], self.recvs.at[0], self.f, self.twin)

    def relay(self):
        theirs = self.block(self.across)
        take(theirs, self.recvs.at[1])
        send(theirs, theirs, self.sends.at[2], self.recvs.at[2], self.f, self.twin)

    def arrive(self):
        take(self.block(self.s), self.recvs.at[0])
        take(self.block(self.s), self.recvs.at[2])

    def drain(self):
        for k in range(3):
            take(self.block(self.s), self.sends.at[k])


def greet_near(barrier, f, s):
    y, h, z = f // 8, x_half(f), lax.rem(f, 4)
    greet(barrier, f + 4 - 8 * h, lax.rem(s + 2, G))
    for step in (1, 3):
        greet(barrier, lax.rem(y + step, 4) * 8 + lax.rem(f, 8), s)
        greet(barrier, f - z + lax.rem(z + step, 4), s)
    for step in (1, 2, 3):
        greet(barrier, f, lax.rem(s + step, G))
    pl.semaphore_wait(barrier, 8)


def unpack_rings(held, first, wide):
    c = held.shape[-1]

    def pair(p):
        at = (p // 4, lax.rem(p // 2, 2))
        z = 2 * lax.rem(p, 2)
        one = held[at[0], at[1], z, first : first + 48, :].astype(jnp.float32)
        two = held[at[0], at[1], z + 1, first : first + 48, :].astype(jnp.float32)
        rows = pl.ds(pl.multiple_of(48 * p, 48), 48)
        wide[rows, :c] = jnp.concatenate([one[:ROWS], two[:ROWS]], axis=0).astype(wide.dtype)
        wide[rows, c:] = jnp.concatenate([one[ROWS:], two[ROWS:]], axis=0).astype(wide.dtype)

    loop(N // 2, pair)


def spread_vectors(held, vec, f, s):
    low, full = jnp.bfloat16, jnp.float32
    row = lax.broadcasted_iota(jnp.int32, (128, D), 0)
    lane = lax.broadcasted_iota(jnp.int32, (128, D), 1)
    inside = lax.rem(lane, ROWS)
    plain = (row == inside).astype(full).astype(low)
    shifted = (row == inside + ROWS * s).astype(full).astype(low)
    owner = lax.broadcasted_iota(jnp.int32, (16, D), 1) // ROWS
    number = lax.broadcasted_iota(jnp.int32, (16, D), 0)
    vec[...] = jnp.zeros_like(vec)

    def add(j):
        block = held[j // 8, lax.rem(j // 4, 2), lax.rem(j, 4), 48:64, :128]
        straight, moved = dot(block, plain), dot(block, shifted)
        wanted = jnp.where(number < 7, j, jnp.where(j // 8 == s, lax.rem(j, 8), -1))
        vec[...] += jnp.where(owner == wanted, jnp.where(number == 6, moved, straight), 0.0)

    loop(N, add)


def forward_kernel(
    src_a, src_b, src_c, src_x, src_dy,
    got_x, vec, normed, qkv, w_in, lse, got_ctx, w_out, w_up, w_down, got_dy,
    held_a, held_b, held_c, ring_ss, ring_rs, ring_own, seq_ss, seq_rs, seq_own,
):
    f, s = place()
    greet_near(pltpu.get_barrier_semaphore(), f, s)
    ring_a, ring_b, ring_c = [
        Ring(src, held, ring_ss.at[k], ring_rs.at[k], ring_own.at[k], order, f, s)
        for k, (src, held, order) in enumerate(
            ((src_a, held_a, "yz"), (src_b, held_b, "zy"), (src_c, held_c, "yz"))
        )
    ]
    rings = (ring_a, ring_b, ring_c)
    copies = [
        pltpu.make_async_copy(src, dst.at[s], seq_own.at[k])
        for k, (src, dst) in enumerate(((src_x, got_x), (src_dy, got_dy)))
    ]
    for copy in copies:
        copy.start()
    for ring in rings:
        ring.begin()
    share_x, share_dy = [
        Share(lambda i, dst=dst: dst.at[i], seq_ss.at[k], seq_rs.at[k], f, s)
        for k, dst in enumerate((got_x, got_dy))
    ]
    copies[0].wait()
    share_x.begin()
    for ring in rings:
        ring.first()
    for ring in rings:
        ring.first_relay()
    for ring in rings:
        ring.last()
    share_x.relay()
    copies[1].wait()
    share_dy.begin()
    share_x.arrive()
    for ring in rings:
        ring.last_relay()
    ring_a.arrive()
    spread_vectors(held_a, vec, f, s)
    gain, shift = vec[0:1, :], vec[1:2, :]

    def norm_tile(t):
        unit, _ = norm_parts(got_x[t].astype(jnp.float32))
        normed[tile(t), :] = (unit * gain + shift).astype(normed.dtype)

    loop(G, norm_tile)
    unpack_rings(held_a, 0, w_in)
    bias = jnp.concatenate([vec[7:8, :PAD], jnp.zeros((1, PAD), jnp.float32), vec[8:9, :PAD]], axis=1)

    def project(t):
        made = (dot(normed[tile(t), :], w_in[...]) + bias).astype(qkv.dtype)
        qkv[tile(t), :PAD] = (made[:, :PAD].astype(jnp.float32) * SCALE).astype(qkv.dtype)
        qkv[tile(t), PAD:] = made[:, PAD:]

    loop(G, project)
    share_dy.relay()
    shares = []
    for step, b in enumerate((3, 2, 1, 0)):
        rows, span = slice(b * TOK, (b + 1) * TOK), (b + 1) * TOK
        for pair in range(2):
            at = pair * 128
            made = None
            for h in range(2 * pair, min(2 * pair + 2, HEADS)):
                query = only(h, qkv[rows, at : at + 128])
                scores = causal(dot_t(query, qkv[:span, PAD + at : PAD + at + 128]), b * TOK)
                peak = jnp.max(scores, axis=-1, keepdims=True)
                weights = jnp.exp(scores - peak)
                total = jnp.sum(weights, axis=-1, keepdims=True)
                lse[h, rows, :] = peak + jnp.log(total)
                part = dot(weights.astype(qkv.dtype), qkv[:span, 2 * PAD + at : 2 * PAD + at + 128]) / total
                made = part if made is None else jnp.where(lanes_of(h, part.shape), part, made)
            got_ctx[s, rows, at : at + 128] = made.astype(got_ctx.dtype)
        shares.append(
            Share(
                lambda i, b=b: got_ctx.at[i, pl.ds(b * TOK, TOK)], seq_ss.at[2 + step], seq_rs.at[2 + step], f, s
            )
        )
        shares[-1].begin()
        if step:
            shares[step - 1].relay()
    shares[-1].relay()
    ring_b.arrive()
    unpack_rings(held_b, 0, w_out)
    unpack_rings(held_b, 48, w_up)
    ring_c.arrive()
    unpack_rings(held_c, 0, w_down)
    share_dy.arrive()
    for share in shares:
        share.arrive()
    for share in [share_x, share_dy] + shares:
        share.drain()
    for ring in rings:
        ring.drain()


def forward(src_a, src_b, src_c, inputs, cotangent):
    low, full = jnp.bfloat16, jnp.float32
    any_space, vmem = pl.BlockSpec(memory_space=pl.ANY), pl.BlockSpec(memory_space=pltpu.VMEM)
    shape = jax.ShapeDtypeStruct
    outs = (
        shape((G, TOK, D), low),
        shape((16, D), full),
        shape((LEN, D), low),
        shape((LEN, 3 * PAD), low),
        shape((D, 3 * PAD), low),
        shape((HEADS, LEN, 1), full),
        shape((G, LEN, PAD), low),
        shape((D, D), low),
        shape((D, FFG), low),
        shape((FFG, D), low),
        shape((G, TOK, D), low),
    )
    return pl.pallas_call(
        forward_kernel,
        out_shape=outs,
        in_specs=[any_space] * 5,
        out_specs=[vmem] * len(outs),
        scratch_shapes=[pltpu.VMEM((4, 2, 4, rows, 384), low) for rows in (64, 96, 48)]
        + [pltpu.SemaphoreType.DMA((3, 9))] * 2
        + [pltpu.SemaphoreType.DMA((3, 1))]
        + [pltpu.SemaphoreType.DMA((6, 3))] * 2
        + [pltpu.SemaphoreType.DMA((2,))],
        compiler_params=pltpu.CompilerParams(
            collective_id=0, has_side_effects=True, vmem_limit_bytes=48 * 2**20
        ),
    )(src_a, src_b, src_c, inputs, cotangent)


def on_device(
    inputs,
    proj_in,
    bias_query,
    bias_value,
    proj_out,
    bias_out,
    norm_gain,
    norm_shift,
    up_weight,
    up_bias,
    down_weight,
    down_bias,
    post_gain,
    post_shift,
    cotangent,
):
    low = jnp.bfloat16
    full = jnp.float32
    f, s = place()
    split = proj_in.reshape(ROWS, 3, G, OWN).transpose(2, 0, 1, 3)
    send_in = pack(pad_heads(split).reshape(G, ROWS, 3 * PAD))
    units = up_weight.reshape(ROWS, N, G, ROWS).transpose(2, 0, 1, 3).reshape(G, ROWS, FFG)
    send_out = jnp.broadcast_to(pack(proj_out)[None], (G, 48, 384))
    vectors = jnp.stack(
        [norm_gain, norm_shift, post_gain, post_shift, bias_out, down_bias, jnp.zeros_like(bias_out), bias_query, bias_value]
    )
    compact = jnp.pad(vectors, ((0, 7), (0, 384 - ROWS)))
    compact = compact + jnp.pad(up_bias[None], ((6, 9), (0, 384 - 96)))
    src_a = jnp.concatenate([send_in, jnp.broadcast_to(compact[None], (G, 16, 384))], axis=1)
    src_b = jnp.concatenate([send_out, pack(units)], axis=1)
    src_c = pack(down_weight.reshape(G, ROWS, D))
    got_x, vec, normed, qkv, w_in, lse, got_ctx, w_out, w_up, w_down, got_dy = forward(
        src_a, src_b, src_c, inputs, cotangent
    )
    gain_one, shift_one, gain_two, shift_two, out_shift, down_shift = [vec[i] for i in range(6)]
    up_shift = vec[6]

    x = got_x.reshape(LEN, D).astype(full)
    dy = got_dy.reshape(LEN, D)
    unit_one, inverse_one = norm_parts(x)
    heads = qkv.reshape(LEN, 3, PAD)[:, :, :OWN].reshape(LEN, 3, HEADS, HD).transpose(1, 2, 0, 3)
    queries, keys, values = heads[0], heads[1], heads[2]
    scores = jnp.einsum("hqd,hkd->hqk", queries, keys, preferred_element_type=full)
    mask = jnp.arange(LEN)[None, :] <= jnp.arange(LEN)[:, None]
    probs = jnp.exp(jnp.where(mask, scores, -1e9) - lse)
    probs_low = probs.astype(low)
    context = got_ctx[:, :, :OWN].transpose(1, 0, 2).reshape(LEN, D)

    residual = x + dot(context, w_out) + out_shift
    unit_two, inverse_two = norm_parts(residual)
    normed_two = (unit_two * gain_two + shift_two).astype(low)
    hidden = dot(normed_two, w_up) + up_shift
    active, pull_gelu = jax.vjp(functools.partial(jax.nn.gelu, approximate=False), hidden)
    active_low = active.astype(low)
    out_part = dot(active_low, w_down).astype(low).reshape(G, TOK, D)
    grad_down = t_dot(active_low, dy)
    d_hidden = pull_gelu(dot_t(dy, w_down))[0].astype(low)
    grad_up = t_dot(normed_two, d_hidden)
    grad_up_bias = jnp.sum(d_hidden.astype(full), axis=0)
    d_two_part = dot_t(d_hidden, w_up).astype(low).reshape(G, TOK, D)
    got_two, got_outs = exchange(2, ("seq_sum", "seq_sum"), (d_two_part, out_part))

    def own(array):
        return lax.dynamic_slice_in_dim(array, s * TOK, TOK)

    output = (own(residual) + jnp.sum(got_outs.astype(full), axis=0) + down_shift).astype(low)
    d_two = jnp.sum(got_two.astype(full), axis=0)
    unit_own, cot = own(unit_two), cotangent.astype(full)
    grad_post_gain = jnp.sum(d_two * unit_own, axis=0)
    grad_post_shift = jnp.sum(d_two, axis=0)
    d_residual = cot + norm_back(d_two, gain_two, unit_own, own(inverse_two))
    branch_own = d_residual.astype(low)
    (got_branch,) = exchange(3, ("seq",), (branch_own,))
    branch = got_branch.reshape(LEN, D)
    w_out_own = lax.dynamic_slice_in_dim(w_out, s * OWN, OWN)
    d_ctx = dot_t(branch, w_out_own).astype(low)
    grad_out = t_dot(context, pad_heads(lax.dynamic_slice_in_dim(branch, s * OWN, OWN, 1)))
    d_ctx_heads = d_ctx.reshape(LEN, HEADS, HD).transpose(1, 0, 2)
    d_values = jnp.einsum("hqk,hqd->hkd", probs_low, d_ctx_heads, preferred_element_type=full)
    d_probs = jnp.einsum("hqd,hkd->hqk", d_ctx_heads, values, preferred_element_type=full)
    inner = jnp.sum(probs * d_probs, axis=-1, keepdims=True)
    d_scores = (probs * (d_probs - inner)).astype(low)
    d_queries = jnp.einsum("hqk,hkd->hqd", d_scores, keys, preferred_element_type=full) * SCALE
    d_keys = jnp.einsum("hqk,hqd->hkd", d_scores, queries, preferred_element_type=full)
    d_proj = jnp.stack([d_queries, d_keys, d_values]).transpose(2, 0, 1, 3).reshape(LEN, 3, OWN)
    d_proj = pad_heads(d_proj).astype(low).reshape(LEN, 3 * PAD)
    grad_in = t_dot(normed, d_proj)
    d_bias = jnp.sum(d_proj.astype(full), axis=0)
    d_one_part = dot_t(d_proj, w_in).astype(low).reshape(G, TOK, D)
    (got_one,) = exchange(4, ("seq_sum",), (d_one_part,))
    d_one = jnp.sum(got_one.astype(full), axis=0)
    unit_first = own(unit_one)
    grad_input = d_residual + norm_back(d_one, gain_one, unit_first, own(inverse_one))
    zero = jnp.zeros((D,), full)
    sums = jnp.stack(
        [
            jnp.sum(d_one * unit_first, axis=0),
            jnp.sum(d_one, axis=0),
            grad_post_gain,
            grad_post_shift,
            jnp.sum(branch_own.astype(full), axis=0),
            jnp.sum(cot, axis=0),
            lax.dynamic_update_slice_in_dim(zero, d_bias[:OWN], s * OWN, 0),
            lax.dynamic_update_slice_in_dim(zero, d_bias[2 * PAD : 2 * PAD + OWN], s * OWN, 0),
        ]
    )
    sums_up = lax.dynamic_update_slice_in_dim(jnp.zeros((4, D), full), grad_up_bias[None], s, 0)
    sums = jnp.pad(jnp.concatenate([sums, sums_up]), ((0, 116), (0, 0)))
    vec_blocks = sums.T.reshape(N, ROWS, 128)

    def cut(grad):
        return pack(grad.reshape(N, ROWS, -1)).astype(low)

    part_in, part_up, part_out, part_down, part_vec = exchange(
        5,
        ("fan_sum",) * 5,
        (cut(grad_in), cut(grad_up), cut(grad_out), cut(grad_down), vec_blocks),
    )

    def halves(part):
        wide = part.astype(full).reshape(4, 2, 4, *part.shape[1:])
        wide = jnp.sum(wide, axis=(0, 2))
        mine = lax.dynamic_index_in_dim(wide, x_half(f), keepdims=False)
        other = lax.dynamic_index_in_dim(wide, 1 - x_half(f), keepdims=False)
        return jnp.stack([mine, other])

    share = (
        halves(part_in).astype(low),
        halves(part_up).astype(low),
        halves(part_out).astype(low),
        halves(part_down).astype(low),
        jnp.sum(part_vec, axis=0),
    )
    all_in, all_up_g, all_out, all_down, all_vec = exchange(6, ("seq",) * 5, share)

    def groups(parts):
        wide = parts.astype(full)
        swapped = jnp.concatenate([wide[2:, 1], wide[:2, 1]])
        return unpack(wide[:, 0] + swapped)

    final_in = groups(all_in).reshape(G, ROWS, 3, PAD)[..., :OWN].transpose(1, 2, 0, 3)
    final_up = groups(all_up_g).reshape(G, ROWS, N, ROWS).transpose(1, 2, 0, 3).reshape(ROWS, G * FFG)
    final_out = groups(all_out)[..., :OWN].transpose(1, 0, 2).reshape(ROWS, D)
    final_down = groups(all_down).reshape(96, D)
    final_vec = jnp.sum(all_vec, axis=0).T
    return (
        output,
        grad_input.astype(low),
        final_in.reshape(ROWS, 3 * D),
        final_vec[6],
        final_vec[7],
        final_out,
        final_vec[4],
        final_vec[0],
        final_vec[1],
        final_up,
        final_vec[8:12].reshape(96),
        final_down,
        final_vec[5],
        final_vec[2],
        final_vec[3],
    )


def solution(mesh):
    rows, wide, flat = P(("fsdp", "seq"), None), P("fsdp", None), P("fsdp")
    return jax.shard_map(
        on_device,
        mesh=mesh,
        in_specs=(rows, wide, flat, flat, wide, flat, flat, flat, wide, flat, wide, flat, flat, flat, rows),
        out_specs=(rows, rows, wide, flat, flat, wide, flat, flat, flat, wide, flat, wide, flat, flat, flat),
        check_vma=False,
    )
```

```python
import functools
import math

import jax
import jax.numpy as jnp
from jax import lax
from jax.experimental import pallas as pl
from jax.experimental.pallas import tpu as pltpu
from jax.sharding import PartitionSpec as P

D = 768
H = 12
HD = 64
N = 32
G = 4
ROWS = 24
LEN = 1024
TOK = 256
HEADS = 3
OWN = HEADS * HD
PAD = 256
FFG = 768
epsilon = 1e-05
SCALE = 1.0 / math.sqrt(HD)
MESH = pl.DeviceIdType.MESH


def x_half(f):
    return lax.rem(f // 4, 2)


def place():
    return lax.axis_index("fsdp"), lax.axis_index("seq")


def send(src, dst, send_sem, recv_sem, f, s):
    pltpu.make_async_remote_copy(
        src_ref=src,
        dst_ref=dst,
        send_sem=send_sem,
        recv_sem=recv_sem,
        device_id=(f, s),
        device_id_type=MESH,
    ).start()


def take(ref, sem):
    pltpu.make_async_copy(ref, ref, sem).wait()


def loop(count, body):
    lax.fori_loop(0, count, lambda t, carry: (body(t), carry)[1], 0)


def greet(barrier, f, s):
    pl.semaphore_signal(barrier, inc=1, device_id=(f, s), device_id_type=MESH)


def pack(blocks):
    c = blocks.shape[-1] // 2
    return jnp.concatenate([blocks[..., :c], blocks[..., c:]], axis=-2)


def unpack(blocks):
    return jnp.concatenate([blocks[..., :ROWS, :], blocks[..., ROWS:, :]], axis=-1)


def pad_heads(blocks):
    return jnp.pad(blocks, [(0, 0)] * (blocks.ndim - 1) + [(0, PAD - OWN)])


def norm_parts(values):
    center = jnp.mean(values, axis=-1, keepdims=True)
    centered = values - center
    spread = jnp.mean(centered * centered, axis=-1, keepdims=True)
    inverse = lax.rsqrt(spread + epsilon)
    return centered * inverse, inverse


def norm_back(grad, gain, unit, inverse):
    scaled = grad * gain
    mean_one = jnp.mean(scaled, axis=-1, keepdims=True)
    mean_two = jnp.mean(scaled * unit, axis=-1, keepdims=True)
    return inverse * (scaled - mean_one - unit * mean_two)


def dot(a, b):
    return jnp.dot(a, b, preferred_element_type=jnp.float32)


def dot_t(a, b):
    return lax.dot_general(a, b, (((1,), (1,)), ((), ())), preferred_element_type=jnp.float32)


def t_dot(a, b):
    return lax.dot_general(a, b, (((0,), (0,)), ((), ())), preferred_element_type=jnp.float32)


def tile(t, size=TOK):
    return pl.ds(pl.multiple_of(t * size, size), size)


def lanes_of(h, shape):
    lane = lax.broadcasted_iota(jnp.int32, shape, 1)
    return lane < HD if h % 2 == 0 else lane >= HD


def only(h, block):
    return jnp.where(lanes_of(h, block.shape), block, jnp.zeros_like(block))


def causal(scores, offset):
    row = offset + lax.broadcasted_iota(jnp.int32, scores.shape, 0)
    col = lax.broadcasted_iota(jnp.int32, scores.shape, 1)
    return jnp.where(col <= row, scores, -1e9)


class Ring:
    def __init__(self, src, held, sends, recvs, own, order, f, s):
        self.src, self.held, self.sends, self.recvs, self.own = src, held, sends, recvs, own
        self.order, self.f, self.s = order, f, s
        self.y, self.h, self.z = f // 8, x_half(f), lax.rem(f, 4)

    def peer(self, axis, step):
        if axis == "y":
            return lax.rem(self.y + step + 4, 4) * 8 + lax.rem(self.f, 8), self.s
        return self.f - self.z + lax.rem(self.z + step + 4, 4), self.s

    def coordinate(self, axis, step):
        return lax.rem((self.y if axis == "y" else self.z) + step + 4, 4)

    def one(self, axis, step, half=None):
        i = self.coordinate(axis, step)
        halves = slice(None) if half is None else half
        return self.held.at[i, halves, self.z] if axis == "y" else self.held.at[self.y, halves, i]

    def many(self, axis, step, half=None):
        i = self.coordinate(axis, step)
        if axis == "y":
            return self.held.at[i] if half is None else self.held.at[i, half]
        rows = slice(None) if half is None else slice(2 * half, 2 * half + 2)
        return self.held.at[rows, slice(None), i]

    def push(self, block, k, peer):
        send(block, block, self.sends.at[k], self.recvs.at[k], *peer)

    def begin(self):
        mine = self.held.at[self.y, self.h, self.z]
        other = lax.rem(self.s + 2, G)
        send(
            self.src.at[other], mine, self.sends.at[0], self.recvs.at[0], self.f + 4 - 8 * self.h, other
        )
        pltpu.make_async_copy(self.src.at[self.s], mine, self.own.at[0]).start()

    def first(self):
        mine = self.held.at[self.y, self.h, self.z]
        take(mine, self.own.at[0])
        take(mine, self.recvs.at[0])
        axis = self.order[0]
        self.push(self.one(axis, 0), 1, self.peer(axis, 1))
        self.push(self.one(axis, 0), 2, self.peer(axis, -1))

    def relay(self, part, base, axis):
        take(part(axis, -1), self.recvs.at[base])
        self.push(part(axis, -1, 0), base + 2, self.peer(axis, 1))
        take(part(axis, 1), self.recvs.at[base + 1])
        self.push(part(axis, 1, 1), base + 3, self.peer(axis, -1))

    def first_relay(self):
        self.relay(self.one, 1, self.order[0])

    def last(self):
        axis = self.order[0]
        take(self.one(axis, 2, 0), self.recvs.at[3])
        take(self.one(axis, 2, 1), self.recvs.at[4])
        axis = self.order[1]
        self.push(self.many(axis, 0), 5, self.peer(axis, 1))
        self.push(self.many(axis, 0), 6, self.peer(axis, -1))

    def last_relay(self):
        self.relay(self.many, 5, self.order[1])

    def arrive(self):
        axis = self.order[1]
        take(self.many(axis, 2, 0), self.recvs.at[7])
        take(self.many(axis, 2, 1), self.recvs.at[8])

    def drain(self):
        one, many = self.order
        take(self.held.at[self.y, self.h, self.z], self.sends.at[0])
        for k in (1, 2):
            take(self.one(one, 0), self.sends.at[k])
            take(self.one(one, 0, 0), self.sends.at[k + 2])
            take(self.many(many, 0), self.sends.at[k + 4])
            take(self.many(many, 0, 0), self.sends.at[k + 6])


class Share:
    def __init__(self, block, sends, recvs, f, s):
        self.block, self.sends, self.recvs, self.f, self.s = block, sends, recvs, f, s
        self.twin = s + 1 - 2 * lax.rem(s, 2)
        self.across = lax.rem(s + 2, G)

    def begin(self):
        mine = self.block(self.s)
        send(mine, mine, self.sends.at[1], self.recvs.at[1], self.f, self.across)
        send(mine, mine, self.sends.at[0], self.recvs.at[0], self.f, self.twin)

    def relay(self):
        theirs = self.block(self.across)
        take(theirs, self.recvs.at[1])
        send(theirs, theirs, self.sends.at[2], self.recvs.at[2], self.f, self.twin)

    def arrive(self):
        take(self.block(self.s), self.recvs.at[0])
        take(self.block(self.s), self.recvs.at[2])

    def drain(self):
        for k in range(3):
            take(self.block(self.s), self.sends.at[k])


def greet_near(barrier, f, s):
    y, h, z = f // 8, x_half(f), lax.rem(f, 4)
    greet(barrier, f + 4 - 8 * h, lax.rem(s + 2, G))
    greet(barrier, f + 4 - 8 * h, s)
    for step in (1, 3):
        greet(barrier, lax.rem(y + step, 4) * 8 + lax.rem(f, 8), s)
        greet(barrier, f - z + lax.rem(z + step, 4), s)
    for step in (1, 2, 3):
        greet(barrier, f, lax.rem(s + step, G))
    pl.semaphore_wait(barrier, 9)


def unpack_rings(held, first, wide):
    c = held.shape[-1]

    def pair(p):
        at = (p // 4, lax.rem(p // 2, 2))
        z = 2 * lax.rem(p, 2)
        one = held[at[0], at[1], z, first : first + 48, :].astype(jnp.float32)
        two = held[at[0], at[1], z + 1, first : first + 48, :].astype(jnp.float32)
        rows = pl.ds(pl.multiple_of(48 * p, 48), 48)
        wide[rows, :c] = jnp.concatenate([one[:ROWS], two[:ROWS]], axis=0).astype(wide.dtype)
        wide[rows, c:] = jnp.concatenate([one[ROWS:], two[ROWS:]], axis=0).astype(wide.dtype)

    loop(N // 2, pair)


def spread_vectors(held, vec, f, s):
    low, full = jnp.bfloat16, jnp.float32
    row = lax.broadcasted_iota(jnp.int32, (128, D), 0)
    lane = lax.broadcasted_iota(jnp.int32, (128, D), 1)
    inside = lax.rem(lane, ROWS)
    plain = (row == inside).astype(full).astype(low)
    shifted = (row == inside + ROWS * s).astype(full).astype(low)
    owner = lax.broadcasted_iota(jnp.int32, (16, D), 1) // ROWS
    number = lax.broadcasted_iota(jnp.int32, (16, D), 0)
    vec[...] = jnp.zeros_like(vec)

    def add(j):
        block = held[j // 8, lax.rem(j // 4, 2), lax.rem(j, 4), 48:64, :128]
        straight, moved = dot(block, plain), dot(block, shifted)
        wanted = jnp.where(number < 7, j, jnp.where(j // 8 == s, lax.rem(j, 8), -1))
        vec[...] += jnp.where(owner == wanted, jnp.where(number == 6, moved, straight), 0.0)

    loop(N, add)


class RingSum:
    def __init__(self, part, inbox, total, sends, recvs, order, f, s):
        self.part, self.inbox, self.total = part, inbox, total
        self.sends, self.recvs, self.f, self.s = sends, recvs, f, s
        self.line = Ring(None, part, None, None, None, order, f, s)
        self.order = order

    def push(self, block, inbox, k, peer):
        send(block, inbox, self.sends.at[k], self.recvs.at[k], *peer)

    def add(self, block, *inboxes):
        total = block[...].astype(jnp.float32)
        for inbox in inboxes:
            total = total + inbox[...].astype(jnp.float32)
        block[...] = total.astype(block.dtype)

    def stage(self, section, axis, far, near, base):
        line = self.line
        self.push(section(axis, 2, 0), far.at[0], base, line.peer(axis, 1))
        self.push(section(axis, 2, 1), far.at[1], base + 1, line.peer(axis, -1))
        yield
        take(far.at[0], self.recvs.at[base])
        self.add(section(axis, 1, 0), far.at[0])
        self.push(section(axis, 1), near.at[0], base + 2, line.peer(axis, 1))
        take(far.at[1], self.recvs.at[base + 1])
        self.add(section(axis, -1, 1), far.at[1])
        self.push(section(axis, -1), near.at[1], base + 3, line.peer(axis, -1))
        yield
        take(near.at[0], self.recvs.at[base + 2])
        take(near.at[1], self.recvs.at[base + 3])
        self.add(section(axis, 0), near.at[0], near.at[1])

    def steps(self):
        line = self.line
        far_many, near_many, far_one, near_one, beyond = self.inbox
        yield from self.stage(line.many, self.order[1], far_many, near_many, 0)
        yield from self.stage(line.one, self.order[0], far_one, near_one, 4)
        self.push(
            self.part.at[line.y, 1 - line.h, line.z], beyond, 8, (self.f + 4 - 8 * line.h, self.s)
        )
        yield
        take(beyond, self.recvs.at[8])
        mine = self.part[line.y, line.h, line.z].astype(jnp.float32)
        self.total[self.s] = (mine + beyond[...].astype(jnp.float32)).astype(self.total.dtype)

    def drain(self):
        far_many, near_many, far_one, near_one, beyond = self.inbox
        for k, ref in enumerate((far_many, far_many, near_many, near_many, far_one, far_one, near_one, near_one)):
            take(ref.at[0], self.sends.at[k])
        take(beyond, self.sends.at[8])


def ring_inbox(order, rows):
    many = (4, 2) if order[1] == "z" else (2, 4)
    half = (2, 2) if order[1] == "z" else (4,)
    block = (rows, 384)
    return [(2,) + half + block, (2,) + many + block, (2,) + block, (2, 2) + block, block]


class SeqSum:
    def __init__(self, part, twins, crossed, sends, recvs, f, s):
        self.part, self.twins, self.crossed = part, twins, crossed
        self.sends, self.recvs, self.f, self.s = sends, recvs, f, s
        self.twin = s + 1 - 2 * lax.rem(s, 2)
        self.across = lax.rem(s + 2, G)
        self.far_twin = 3 - s

    def ready(self, t):
        @pl.when(t == self.far_twin)
        def _():
            send(
                self.part.at[self.far_twin], self.twins.at[0], self.sends.at[0], self.recvs.at[0], self.f, self.twin
            )

        @pl.when(t == self.twin)
        def _():
            send(self.part.at[self.twin], self.twins.at[1], self.sends.at[2], self.recvs.at[2], self.f, self.twin)

    def relay(self, t):
        @pl.when(t == self.across)
        def _():
            take(self.twins.at[0], self.recvs.at[0])
            both = self.part[self.across].astype(jnp.float32) + self.twins[0].astype(jnp.float32)
            self.part[self.across] = both.astype(self.part.dtype)
            send(
                self.part.at[self.across], self.crossed, self.sends.at[1], self.recvs.at[1], self.f, self.across
            )

    def total(self):
        take(self.crossed, self.recvs.at[1])
        take(self.crossed, self.recvs.at[2])
        mine = self.part[self.s].astype(jnp.float32) + self.twins[1].astype(jnp.float32)
        return mine + self.crossed[...].astype(jnp.float32)

    def drain(self):
        for k in range(3):
            take(self.crossed, self.sends.at[k])


def cut_grad(left, right, part, first, chunks):
    low = part.dtype

    def chunk(c):
        columns = pl.ds(pl.multiple_of(c * 384, 128), 384)
        made = t_dot(left[:, columns], right[...])
        for i in range(16):
            block = made[i * ROWS : (i + 1) * ROWS]
            packed = jnp.concatenate([block[:, :384], block[:, 384:]], axis=0).astype(low)
            part[2 * c + i // 8, (i // 4) % 2, i % 4, first : first + 48, :] = packed

    loop(chunks, chunk)


def column_sum(values):
    return jnp.sum(values, axis=0, keepdims=True)


RING_PLAN = (("yz", 48), ("zy", 48), ("yz", 16), ("yz", 32), ("zy", 32))


def layer_kernel(*refs):
    (
        src_a, src_b, src_c, src_x, src_dy,
        output, grad_input, fin_up, fin_down, fin_out, fin_a, fin_b,
        got_x, vec, normed, qkv, w_in, lse, got_ctx, w_out, w_up, w_down, got_dy,
        held_a, held_b, held_c,
        residual, normed_two, active, d_hidden, branch, d_ctx, d_proj, d_key, d_value, d_res, sums, grad_in,
        out_part, out_twins, out_crossed, two_part, two_twins, two_crossed, one_part, one_twins, one_crossed,
        part_up, part_down, part_out, part_a, part_b,
        *inboxes,
        ring_ss, ring_rs, ring_own, seq_ss, seq_rs, seq_own, sum_ss, sum_rs, part_ss, part_rs,
    ) = refs
    low, full = jnp.bfloat16, jnp.float32
    f, s = place()
    greet_near(pltpu.get_barrier_semaphore(), f, s)
    ring_a, ring_b, ring_c = [
        Ring(src, held, ring_ss.at[k], ring_rs.at[k], ring_own.at[k], order, f, s)
        for k, (src, held, order) in enumerate(
            ((src_a, held_a, "yz"), (src_b, held_b, "zy"), (src_c, held_c, "yz"))
        )
    ]
    rings = (ring_a, ring_b, ring_c)
    copies = [
        pltpu.make_async_copy(src, dst.at[s], seq_own.at[k])
        for k, (src, dst) in enumerate(((src_x, got_x), (src_dy, got_dy)))
    ]
    for copy in copies:
        copy.start()
    for ring in rings:
        ring.begin()
    share_x, share_dy = [
        Share(lambda i, dst=dst: dst.at[i], seq_ss.at[k], seq_rs.at[k], f, s)
        for k, dst in enumerate((got_x, got_dy))
    ]
    copies[0].wait()
    share_x.begin()
    for ring in rings:
        ring.first()
    for ring in rings:
        ring.first_relay()
    for ring in rings:
        ring.last()
    share_x.relay()
    copies[1].wait()
    share_dy.begin()
    share_x.arrive()
    for ring in rings:
        ring.last_relay()
    ring_a.arrive()
    spread_vectors(held_a, vec, f, s)
    gain, shift = vec[0:1, :], vec[1:2, :]

    def norm_tile(t):
        unit, _ = norm_parts(got_x[t].astype(jnp.float32))
        normed[tile(t), :] = (unit * gain + shift).astype(normed.dtype)

    loop(G, norm_tile)
    unpack_rings(held_a, 0, w_in)
    bias = jnp.concatenate([vec[7:8, :PAD], jnp.zeros((1, PAD), jnp.float32), vec[8:9, :PAD]], axis=1)

    def project(t):
        made = (dot(normed[tile(t), :], w_in[...]) + bias).astype(qkv.dtype)
        qkv[tile(t), :PAD] = (made[:, :PAD].astype(jnp.float32) * SCALE).astype(qkv.dtype)
        qkv[tile(t), PAD:] = made[:, PAD:]

    loop(G, project)
    share_dy.relay()
    shares = []
    for step, b in enumerate((3, 2, 1, 0)):
        rows, span = slice(b * TOK, (b + 1) * TOK), (b + 1) * TOK
        for pair in range(2):
            at = pair * 128
            made = None
            for h in range(2 * pair, min(2 * pair + 2, HEADS)):
                query = only(h, qkv[rows, at : at + 128])
                scores = causal(dot_t(query, qkv[:span, PAD + at : PAD + at + 128]), b * TOK)
                peak = jnp.max(scores, axis=-1, keepdims=True)
                weights = jnp.exp(scores - peak)
                total = jnp.sum(weights, axis=-1, keepdims=True)
                lse[h, rows, :] = peak + jnp.log(total)
                part = dot(weights.astype(qkv.dtype), qkv[:span, 2 * PAD + at : 2 * PAD + at + 128]) / total
                made = part if made is None else jnp.where(lanes_of(h, part.shape), part, made)
            got_ctx[s, rows, at : at + 128] = made.astype(got_ctx.dtype)
        shares.append(
            Share(
                lambda i, b=b: got_ctx.at[i, pl.ds(b * TOK, TOK)], seq_ss.at[2 + step], seq_rs.at[2 + step], f, s
            )
        )
        shares[-1].begin()
        if step:
            shares[step - 1].relay()
    shares[-1].relay()
    ring_b.arrive()
    unpack_rings(held_b, 0, w_out)
    unpack_rings(held_b, 48, w_up)
    ring_c.arrive()
    unpack_rings(held_c, 0, w_down)
    share_dy.arrive()
    for share in shares:
        share.arrive()

    sum_out = SeqSum(out_part, out_twins, out_crossed, part_ss.at[0], part_rs.at[0], f, s)
    sum_two = SeqSum(two_part, two_twins, two_crossed, part_ss.at[1], part_rs.at[1], f, s)
    sum_one = SeqSum(one_part, one_twins, one_crossed, part_ss.at[2], part_rs.at[2], f, s)
    sums[...] = jnp.zeros_like(sums)
    gain_two, shift_two = vec[2:3, :], vec[3:4, :]

    def turn(i):
        return jnp.where(i == 0, 3 - s, jnp.where(i == 1, lax.rem(s + 2, G), jnp.where(i == 2, sum_two.twin, s)))

    def feed(i):
        t = turn(i)
        rows = tile(t)
        value = got_x[t].astype(full) + vec[4:5, :]
        for g in range(G):
            value = value + dot(got_ctx[g, rows, :OWN], w_out[g * OWN : (g + 1) * OWN, :])
        residual[rows, :] = value
        unit, _ = norm_parts(value)
        normed_low = (unit * gain_two + shift_two).astype(low)
        normed_two[rows, :] = normed_low
        hidden = dot(normed_low, w_up[...]) + vec[6:7, :]
        cdf = 0.5 * (1.0 + lax.erf(hidden * math.sqrt(0.5)))
        active_low = (hidden * cdf).astype(low)
        active[rows, :] = active_low
        slope = cdf + hidden * jnp.exp(-0.5 * hidden * hidden) * (1.0 / math.sqrt(2.0 * math.pi))
        dy = got_dy[t]
        d_low = (dot_t(dy, w_down[...]) * slope).astype(low)
        d_hidden[rows, :] = d_low
        d_two = dot_t(d_low, w_up[...])
        two_part[t] = d_two.astype(low)
        sum_two.ready(t)
        sums[2:3, :] += column_sum(d_two * unit)
        sums[3:4, :] += column_sum(d_two)
        sums[8:9, :] += column_sum(d_low.astype(full))
        out_part[t] = dot(active_low, w_down[...]).astype(low)
        sum_out.ready(t)

        @pl.when(i > 1)
        def _():
            sum_two.relay(turn(i - 1))
            sum_out.relay(turn(i - 1))

    loop(G, feed)

    inbox = [inboxes[5 * k : 5 * k + 5] for k in range(5)]
    totals = (fin_up, fin_down, fin_out, fin_a, fin_b)
    parts = (part_up, part_down, part_out, part_a, part_b)
    adders = [
        RingSum(parts[k], inbox[k], totals[k], sum_ss.at[k], sum_rs.at[k], RING_PLAN[k][0], f, s) for k in range(5)
    ]
    finals = [
        Share(lambda i, k=k: totals[k].at[i], seq_ss.at[7 + k], seq_rs.at[7 + k], f, s) for k in range(5)
    ]

    def life(k):
        yield from adders[k].steps()
        finals[k].begin()
        yield
        finals[k].relay()
        yield
        finals[k].arrive()

    lives = [life(k) for k in range(5)]

    def advance(*which):
        for k in which:
            next(lives[k], None)

    cut_grad(normed_two, d_hidden, part_up, 0, 2)
    advance(0)
    flat_dy = [got_dy[t] for t in range(G)]
    dy_all = jnp.concatenate(flat_dy, axis=0)

    def chunk_down(c):
        columns = pl.ds(pl.multiple_of(c * 384, 128), 384)
        made = t_dot(active[:, columns], dy_all)
        for i in range(16):
            block = made[i * ROWS : (i + 1) * ROWS]
            packed = jnp.concatenate([block[:, :384], block[:, 384:]], axis=0).astype(low)
            part_down[2 * c + i // 8, (i // 4) % 2, i % 4] = packed

    loop(2, chunk_down)
    advance(1)

    mine = tile(s)
    own_res = residual[mine, :]
    unit, inverse = norm_parts(own_res)
    own_dy = got_dy[s].astype(full)
    d_own = own_dy + norm_back(sum_two.total(), gain_two, unit, inverse)
    d_res[...] = d_own
    branch[s] = d_own.astype(low)
    share_branch = Share(lambda i: branch.at[i], seq_ss.at[6], seq_rs.at[6], f, s)
    share_branch.begin()
    sums[4:5, :] += column_sum(d_own.astype(low).astype(full))
    sums[5:6, :] += column_sum(own_dy)
    advance(0, 1)
    share_branch.relay()
    output[...] = (own_res + sum_out.total() + vec[5:6, :]).astype(low)
    d_key[...] = jnp.zeros_like(d_key)
    d_value[...] = jnp.zeros_like(d_value)
    share_branch.arrive()

    own_rows = pl.ds(pl.multiple_of(s * OWN, 64), OWN)
    pick = lax.broadcasted_iota(jnp.int32, (D, PAD), 0) == lax.broadcasted_iota(jnp.int32, (D, PAD), 1) + s * OWN
    pick = jnp.logical_and(pick, lax.broadcasted_iota(jnp.int32, (D, PAD), 1) < OWN)
    pick = pick.astype(full).astype(low)
    picked = [dot(branch[t], pick).astype(low) for t in range(G)]
    picked = jnp.concatenate(picked, axis=0)

    def cut_out(g):
        made = t_dot(got_ctx[g], picked)
        for i in range(8):
            one, two, three = [made[i * ROWS + 8 * r : i * ROWS + 8 * r + 8] for r in range(3)]
            upper = jnp.concatenate([one, two[:, :128]], axis=1)
            lower = jnp.concatenate([two[:, 128:], three], axis=1)
            part_out[g, i // 4, i % 4] = jnp.concatenate([upper, lower], axis=0).astype(low)

    loop(G, cut_out)
    advance(2)
    for b in (3, 2, 1, 0):
        rows, span = slice(b * TOK, (b + 1) * TOK), (b + 1) * TOK
        made = dot_t(branch[b], w_out[own_rows, :])
        d_block = jnp.concatenate([made, jnp.zeros((TOK, PAD - OWN), full)], axis=1).astype(low)
        for pair in range(2):
            at = pair * 128
            d_query = None
            for h in range(2 * pair, min(2 * pair + 2, HEADS)):
                query = only(h, qkv[rows, at : at + 128])
                key = qkv[:span, PAD + at : PAD + at + 128]
                grad = only(h, d_block[:, at : at + 128])
                probs = jnp.exp(causal(dot_t(query, key), b * TOK) - lse[h, rows, :])
                d_value[:span, at : at + 128] += t_dot(probs.astype(low), grad)
                d_probs = dot_t(grad, qkv[:span, 2 * PAD + at : 2 * PAD + at + 128])
                inner = jnp.sum(probs * d_probs, axis=-1, keepdims=True)
                d_scores = (probs * (d_probs - inner)).astype(low)
                d_key[:span, at : at + 128] += t_dot(d_scores, query)
                part = dot(d_scores, key) * SCALE
                d_query = part if d_query is None else jnp.where(lanes_of(h, part.shape), part, d_query)
            if pair:
                d_query = only(0, d_query)
            d_proj[rows, at : at + 128] = d_query.astype(low)
            advance(0, 1, 2)
        d_proj[rows, PAD : 2 * PAD] = d_key[rows, :].astype(low)
        d_proj[rows, 2 * PAD :] = d_value[rows, :].astype(low)
        d_one = dot_t(d_proj[rows, :], w_in[...])
        one_part[b] = d_one.astype(low)
        sum_one.ready(b)
        unit, _ = norm_parts(got_x[b].astype(full))
        sums[0:1, :] += column_sum(d_one * unit)
        sums[1:2, :] += column_sum(d_one)
        if b < 3:
            sum_one.relay(b + 1)
    sum_one.relay(0)

    sums[6:7, :PAD] = column_sum(d_proj[:, :PAD].astype(full))
    sums[7:8, :PAD] = column_sum(d_proj[:, 2 * PAD :].astype(full))
    lane = lax.broadcasted_iota(jnp.int32, (16, D), 1) // ROWS
    number = lax.broadcasted_iota(jnp.int32, (16, D), 0)
    up_row = jnp.broadcast_to(sums[8:9, :], (16, D))
    plain = jnp.where(number < 8, sums[...], jnp.where(number == 8 + s, up_row, 0.0))
    compact = lax.rem(lax.broadcasted_iota(jnp.int32, (D, 128), 0), ROWS) == lax.broadcasted_iota(
        jnp.int32, (D, 128), 1
    )
    compact = compact.astype(full).astype(low)
    pad_lanes = jnp.zeros((16, 256), low)

    def cut_in(c):
        columns = pl.ds(pl.multiple_of(c * 384, 128), 384)
        made = t_dot(normed[:, columns], d_proj[...])
        for i in range(16):
            block = made[i * ROWS : (i + 1) * ROWS]
            packed = jnp.concatenate([block[:, :384], block[:, 384:]], axis=0)
            at = (2 * c + i // 8, (i // 4) % 2, i % 4)
            part_a[at[0], at[1], at[2]] = packed[:32].astype(low)
            part_b[at[0], at[1], at[2], :16, :] = packed[32:].astype(low)
            owner = 16 * c + i
            wanted = jnp.where(jnp.logical_or(number == 6, number == 7), owner - 8 * s, owner)
            few = dot(jnp.where(lane == wanted, plain, 0.0).astype(low), compact).astype(low)
            part_b[at[0], at[1], at[2], 16:, :] = jnp.concatenate([few, pad_lanes], axis=1)

    loop(2, cut_in)
    advance(3, 4)
    advance(0, 1, 2)
    unit, inverse = norm_parts(got_x[s].astype(full))
    grad_input[...] = (d_res[...] + norm_back(sum_one.total(), gain, unit, inverse)).astype(low)
    for _ in range(8):
        advance(3, 4)
    for k in (0, 1, 2, 3, 4):
        for _ in lives[k]:
            pass
    for share in [share_x, share_dy, share_branch] + shares + finals:
        share.drain()
    for ring in rings:
        ring.drain()
    for adder in adders + [sum_out, sum_two, sum_one]:
        adder.drain()


def layer(src_a, src_b, src_c, inputs, cotangent):
    low, full = jnp.bfloat16, jnp.float32
    any_space, vmem = pl.BlockSpec(memory_space=pl.ANY), pl.BlockSpec(memory_space=pltpu.VMEM)
    outs = [jax.ShapeDtypeStruct((TOK, D), low)] * 2
    outs += [jax.ShapeDtypeStruct((G, rows, 384), low) for _, rows in RING_PLAN]
    seq_part = [pltpu.VMEM((G, TOK, D), low), pltpu.VMEM((2, TOK, D), low), pltpu.VMEM((TOK, D), low)]
    return pl.pallas_call(
        layer_kernel,
        out_shape=outs,
        in_specs=[any_space] * 5,
        out_specs=[vmem] * len(outs),
        scratch_shapes=[
            pltpu.VMEM((G, TOK, D), low),
            pltpu.VMEM((16, D), full),
            pltpu.VMEM((LEN, D), low),
            pltpu.VMEM((LEN, 3 * PAD), low),
            pltpu.VMEM((D, 3 * PAD), low),
            pltpu.VMEM((HEADS, LEN, 1), full),
            pltpu.VMEM((G, LEN, PAD), low),
            pltpu.VMEM((D, D), low),
            pltpu.VMEM((D, FFG), low),
            pltpu.VMEM((FFG, D), low),
            pltpu.VMEM((G, TOK, D), low),
        ]
        + [pltpu.VMEM((4, 2, 4, rows, 384), low) for rows in (64, 96, 48)]
        + [
            pltpu.VMEM((LEN, D), full),
            pltpu.VMEM((LEN, D), low),
            pltpu.VMEM((LEN, FFG), low),
            pltpu.VMEM((LEN, FFG), low),
            pltpu.VMEM((G, TOK, D), low),
            pltpu.VMEM((16, PAD), low),
            pltpu.VMEM((LEN, 3 * PAD), low),
            pltpu.VMEM((LEN, PAD), full),
            pltpu.VMEM((LEN, PAD), full),
            pltpu.VMEM((TOK, D), full),
            pltpu.VMEM((16, D), full),
            pltpu.VMEM((16, D), full),
        ]
        + seq_part * 3
        + [pltpu.VMEM((4, 2, 4, rows, 384), low) for _, rows in RING_PLAN]
        + [pltpu.VMEM(shape, low) for order, rows in RING_PLAN for shape in ring_inbox(order, rows)]
        + [pltpu.SemaphoreType.DMA((3, 9))] * 2
        + [pltpu.SemaphoreType.DMA((3, 1))]
        + [pltpu.SemaphoreType.DMA((12, 3))] * 2
        + [pltpu.SemaphoreType.DMA((2,))]
        + [pltpu.SemaphoreType.DMA((5, 9))] * 2
        + [pltpu.SemaphoreType.DMA((3, 3))] * 2,
        compiler_params=pltpu.CompilerParams(
            collective_id=0, has_side_effects=True, vmem_limit_bytes=62 * 2**20
        ),
    )(src_a, src_b, src_c, inputs, cotangent)


def on_device(
    inputs,
    proj_in,
    bias_query,
    bias_value,
    proj_out,
    bias_out,
    norm_gain,
    norm_shift,
    up_weight,
    up_bias,
    down_weight,
    down_bias,
    post_gain,
    post_shift,
    cotangent,
):
    low = jnp.bfloat16
    full = jnp.float32
    f, s = place()
    split = proj_in.reshape(ROWS, 3, G, OWN).transpose(2, 0, 1, 3)
    send_in = pack(pad_heads(split).reshape(G, ROWS, 3 * PAD))
    units = up_weight.reshape(ROWS, N, G, ROWS).transpose(2, 0, 1, 3).reshape(G, ROWS, FFG)
    send_out = jnp.broadcast_to(pack(proj_out)[None], (G, 48, 384))
    vectors = jnp.stack(
        [norm_gain, norm_shift, post_gain, post_shift, bias_out, down_bias, jnp.zeros_like(bias_out), bias_query, bias_value]
    )
    compact = jnp.pad(vectors, ((0, 7), (0, 384 - ROWS)))
    compact = compact + jnp.pad(up_bias[None], ((6, 9), (0, 384 - 96)))
    src_a = jnp.concatenate([send_in, jnp.broadcast_to(compact[None], (G, 16, 384))], axis=1)
    src_b = jnp.concatenate([send_out, pack(units)], axis=1)
    src_c = pack(down_weight.reshape(G, ROWS, D))
    output, grad_input, all_up, all_down, all_out, all_a, all_b = layer(src_a, src_b, src_c, inputs, cotangent)
    split_in = jnp.concatenate([all_a, all_b[:, :16]], axis=1)
    final_in = unpack(split_in.astype(full)).reshape(G, ROWS, 3, PAD)[..., :OWN].transpose(1, 2, 0, 3)
    final_up = unpack(all_up.astype(full)).reshape(G, ROWS, N, ROWS).transpose(1, 2, 0, 3).reshape(ROWS, G * FFG)
    upper, lower = all_out[:, :8].astype(full), all_out[:, 8:].astype(full)
    second = jnp.concatenate([upper[..., PAD:], lower[..., :128]], axis=-1)
    out_blocks = jnp.concatenate([upper[..., :PAD], second, lower[..., 128:]], axis=1)
    final_out = out_blocks[..., :OWN].transpose(1, 0, 2).reshape(ROWS, D)
    final_down = unpack(all_down.astype(full)).reshape(96, D)
    final_vec = jnp.sum(all_b[:, 16:, :ROWS].astype(full), axis=0)
    return (
        output,
        grad_input,
        final_in.reshape(ROWS, 3 * D),
        final_vec[6],
        final_vec[7],
        final_out,
        final_vec[4],
        final_vec[0],
        final_vec[1],
        final_up,
        final_vec[8:12].reshape(96),
        final_down,
        final_vec[5],
        final_vec[2],
        final_vec[3],
    )


def solution(mesh):
    rows, wide, flat = P(("fsdp", "seq"), None), P("fsdp", None), P("fsdp")
    return jax.shard_map(
        on_device,
        mesh=mesh,
        in_specs=(rows, wide, flat, flat, wide, flat, flat, flat, wide, flat, wide, flat, flat, flat, rows),
        out_specs=(rows, rows, wide, flat, flat, wide, flat, flat, flat, wide, flat, wide, flat, flat, flat),
        check_vma=False,
    )
```

```python
import functools
import math

import jax
import jax.numpy as jnp
from jax import lax
from jax.experimental import pallas as pl
from jax.experimental.pallas import tpu as pltpu
from jax.sharding import PartitionSpec as P

D = 768
H = 12
HD = 64
N = 32
G = 4
ROWS = 24
LEN = 1024
TOK = 256
HEADS = 3
OWN = HEADS * HD
PAD = 256
FFG = 768
epsilon = 1e-05
SCALE = 1.0 / math.sqrt(HD)
MESH = pl.DeviceIdType.MESH


def x_half(f):
    return lax.rem(f // 4, 2)


def place():
    return lax.axis_index("fsdp"), lax.axis_index("seq")


def send(src, dst, send_sem, recv_sem, f, s):
    pltpu.make_async_remote_copy(
        src_ref=src,
        dst_ref=dst,
        send_sem=send_sem,
        recv_sem=recv_sem,
        device_id=(f, s),
        device_id_type=MESH,
    ).start()


def take(ref, sem):
    pltpu.make_async_copy(ref, ref, sem).wait()


def loop(count, body):
    lax.fori_loop(0, count, lambda t, carry: (body(t), carry)[1], 0)


def greet(barrier, f, s):
    pl.semaphore_signal(barrier, inc=1, device_id=(f, s), device_id_type=MESH)


def pack(blocks):
    c = blocks.shape[-1] // 2
    return jnp.concatenate([blocks[..., :c], blocks[..., c:]], axis=-2)


def unpack(blocks):
    return jnp.concatenate([blocks[..., :ROWS, :], blocks[..., ROWS:, :]], axis=-1)


def pad_heads(blocks):
    return jnp.pad(blocks, [(0, 0)] * (blocks.ndim - 1) + [(0, PAD - OWN)])


def norm_parts(values):
    center = jnp.mean(values, axis=-1, keepdims=True)
    centered = values - center
    spread = jnp.mean(centered * centered, axis=-1, keepdims=True)
    inverse = lax.rsqrt(spread + epsilon)
    return centered * inverse, inverse


def norm_back(grad, gain, unit, inverse):
    scaled = grad * gain
    mean_one = jnp.mean(scaled, axis=-1, keepdims=True)
    mean_two = jnp.mean(scaled * unit, axis=-1, keepdims=True)
    return inverse * (scaled - mean_one - unit * mean_two)


def dot(a, b):
    return jnp.dot(a, b, preferred_element_type=jnp.float32)


def dot_t(a, b):
    return lax.dot_general(a, b, (((1,), (1,)), ((), ())), preferred_element_type=jnp.float32)


def t_dot(a, b):
    return lax.dot_general(a, b, (((0,), (0,)), ((), ())), preferred_element_type=jnp.float32)


def tile(t, size=TOK):
    return pl.ds(pl.multiple_of(t * size, size), size)


def lanes_of(h, shape):
    lane = lax.broadcasted_iota(jnp.int32, shape, 1)
    return lane < HD if h % 2 == 0 else lane >= HD


def only(h, block):
    return jnp.where(lanes_of(h, block.shape), block, jnp.zeros_like(block))


def causal(scores, offset):
    row = offset + lax.broadcasted_iota(jnp.int32, scores.shape, 0)
    col = lax.broadcasted_iota(jnp.int32, scores.shape, 1)
    return jnp.where(col <= row, scores, -1e9)


class Ring:
    def __init__(self, src, held, sends, recvs, order, f, s):
        self.src, self.held, self.sends, self.recvs = src, held, sends, recvs
        self.order, self.f, self.s = order, f, s
        self.y, self.h, self.z = f // 8, x_half(f), lax.rem(f, 4)

    def peer(self, axis, step):
        if axis == "y":
            return lax.rem(self.y + step + 4, 4) * 8 + lax.rem(self.f, 8), self.s
        return self.f - self.z + lax.rem(self.z + step + 4, 4), self.s

    def coordinate(self, axis, step):
        return lax.rem((self.y if axis == "y" else self.z) + step + 4, 4)

    def plane(self, t):
        h = lax.rem(self.h + t // 4, 2)
        if self.order[0] == "y":
            return lax.rem(self.y + t, 4) * 8 + h * 4 + self.z, t // 4
        return self.y * 8 + h * 4 + lax.rem(self.z + t, 4), t // 4

    def many(self, axis, step, half=None):
        i = self.coordinate(axis, step)
        if axis == "y":
            return self.held.at[i] if half is None else self.held.at[i, half]
        rows = slice(None) if half is None else slice(2 * half, 2 * half + 2)
        return self.held.at[rows, slice(None), i]

    def push(self, block, k, peer):
        send(block, block, self.sends.at[k], self.recvs.at[k], *peer)

    def begin(self):
        mine = self.held.at[self.y, self.h, self.z]

        def one(t, k):
            peer, away = self.plane(t)
            group = lax.rem(self.s + 2 * away, G)
            send(self.src.at[group], mine, self.sends.at[k], self.recvs.at[0], peer, group)

        loop(4, lambda t: one(t + 4, 0))
        loop(3, lambda t: one(t + 1, 7))
        pltpu.make_async_copy(self.src.at[self.s], mine, self.recvs.at[0]).start()

    def last(self):
        axis = self.order[1]
        take(self.many(axis, 0), self.recvs.at[0])
        for k, (part, step) in enumerate(((0, 1), (1, -1), (1, 1), (0, -1))):
            self.push(self.many(axis, 0, part), 1 + k, self.peer(axis, step))

    def last_relay(self):
        axis = self.order[1]
        for k, step in enumerate((1, -1)):
            part = self.many(axis, -step, k)
            take(part, self.recvs.at[1 + k])
            self.push(part, 5 + k, self.peer(axis, step))

    def arrive(self):
        for k in (3, 4, 5, 6):
            take(self.many(self.order[1], 0, 0), self.recvs.at[k])

    def drain(self):
        half = self.many(self.order[1], 0, 0)
        take(half, self.sends.at[0])
        take(self.held.at[0, 0, pl.ds(0, 3)], self.sends.at[7])
        for k in range(1, 7):
            take(half, self.sends.at[k])


class Share:
    def __init__(self, block, sends, recvs, f, s):
        self.block, self.sends, self.recvs, self.f, self.s = block, sends, recvs, f, s
        self.twin = s + 1 - 2 * lax.rem(s, 2)
        self.across = lax.rem(s + 2, G)

    def begin(self):
        self.begin_across()
        self.begin_twin()

    def begin_all(self):
        self.begin()
        mine = self.block(self.s)
        send(mine, mine, self.sends.at[2], self.recvs.at[2], self.f, 3 - self.s)

    def begin_across(self):
        mine = self.block(self.s)
        send(mine, mine, self.sends.at[1], self.recvs.at[1], self.f, self.across)

    def begin_twin(self):
        mine = self.block(self.s)
        send(mine, mine, self.sends.at[0], self.recvs.at[0], self.f, self.twin)

    def relay(self):
        theirs = self.block(self.across)
        take(theirs, self.recvs.at[1])
        send(theirs, theirs, self.sends.at[2], self.recvs.at[2], self.f, self.twin)

    def arrive(self):
        take(self.block(self.s), self.recvs.at[0])
        take(self.block(self.s), self.recvs.at[2])

    def arrive_all(self):
        self.arrive()
        take(self.block(self.s), self.recvs.at[1])

    def drain(self):
        for k in range(3):
            take(self.block(self.s), self.sends.at[k])


def greet_near(barrier, f, s):
    y, h, z = f // 8, x_half(f), lax.rem(f, 4)
    other = 1 - h

    def line(t):
        column, row = lax.rem(y + t, 4) * 8, lax.rem(z + t, 4)

        @pl.when(t > 0)
        def _():
            greet(barrier, column + h * 4 + z, s)
            greet(barrier, y * 8 + h * 4 + row, s)
            greet(barrier, f, lax.rem(s + t, G))
            for k in (0, 2):
                greet(barrier, y * 8 + other * 4 + row, lax.rem(s + k, G))

        for k in (0, 2):
            greet(barrier, column + other * 4 + z, lax.rem(s + k, G))

    loop(4, line)
    pl.semaphore_wait(barrier, 23)


def unpack_rings(pieces, wide):
    c = wide.shape[-1] // 2

    def block(y, h, z):
        parts = [held[y, h, z, first : first + rows, :].astype(jnp.float32) for held, first, rows in pieces]
        return parts[0] if len(parts) == 1 else jnp.concatenate(parts, axis=0)

    def pair(p):
        at = (p // 4, lax.rem(p // 2, 2))
        z = 2 * lax.rem(p, 2)
        one, two = block(*at, z), block(*at, z + 1)
        rows = pl.ds(pl.multiple_of(48 * p, 48), 48)
        wide[rows, :c] = jnp.concatenate([one[:ROWS], two[:ROWS]], axis=0).astype(wide.dtype)
        wide[rows, c:] = jnp.concatenate([one[ROWS:], two[ROWS:]], axis=0).astype(wide.dtype)

    loop(N // 2, pair)


def vector_masks(s):
    low, full = jnp.bfloat16, jnp.float32
    row = lax.broadcasted_iota(jnp.int32, (128, D), 0)
    inside = lax.rem(lax.broadcasted_iota(jnp.int32, (128, D), 1), ROWS)
    return (row == inside).astype(full).astype(low), (row == inside + ROWS * s).astype(full).astype(low)


def spread_vectors(blocks, masks, s):
    flat = blocks.reshape(N * 16, 128)
    straight, moved = [dot(flat, mask).reshape(N, 16, D) for mask in masks]
    owner = lax.broadcasted_iota(jnp.int32, (N, 16, D), 2) // ROWS
    number = lax.broadcasted_iota(jnp.int32, (N, 16, D), 1)
    j = lax.broadcasted_iota(jnp.int32, (N, 16, D), 0)
    wanted = jnp.where(number < 7, j, jnp.where(j // 8 == s, j - 8 * s, -1))
    return jnp.sum(jnp.where(owner == wanted, jnp.where(number == 6, moved, straight), 0.0), axis=0)


class RingSum:
    def __init__(self, part, inbox, total, sends, recvs, order, f, s):
        self.part, self.inbox, self.total = part, inbox, total
        self.sends, self.recvs, self.f, self.s = sends, recvs, f, s
        self.line = Ring(None, part, None, None, order, f, s)
        self.order = order

    def push(self, block, inbox, k, peer):
        send(block, inbox, self.sends.at[k], self.recvs.at[k], *peer)

    def add(self, block, *inboxes):
        total = block[...].astype(jnp.float32)
        for inbox in inboxes:
            total = total + inbox[...].astype(jnp.float32)
        block[...] = total.astype(block.dtype)

    def steps(self):
        line, axis = self.line, self.order[1]
        far, plain, added, direct = self.inbox
        sides = ((0, 1), (1, -1))
        for k, step in sides:
            self.push(line.many(axis, 2, k), far.at[k], k, line.peer(axis, step))
        for k, step in sides:
            self.push(line.many(axis, step, 1 - k), plain.at[k], 2 + k, line.peer(axis, step))
        yield
        for k, step in sides:
            take(far.at[k], self.recvs.at[k])
            self.add(line.many(axis, step, k), far.at[k])
            self.push(line.many(axis, step, k), added.at[k], 4 + k, line.peer(axis, step))
        yield
        for k, step in sides:
            take(plain.at[1 - k], self.recvs.at[3 - k])
            take(added.at[k], self.recvs.at[4 + k])
            self.add(line.many(axis, 0, k), added.at[k], plain.at[1 - k])
        first = line.y if self.order[0] == "y" else line.z
        slot = 2 * first + line.h

        def one(t):
            peer, _ = line.plane(t + 1)
            block = self.part.at[peer // 8, x_half(peer), lax.rem(peer, 4)]
            send(block, direct.at[slot], self.sends.at[6], self.recvs.at[6], peer, self.s)

        loop(7, one)
        direct[slot] = self.part[line.y, line.h, line.z]
        yield
        take(direct.at[pl.ds(0, 7)], self.recvs.at[6])
        self.total[self.s] = jnp.sum(direct[...].astype(jnp.float32), axis=0).astype(self.total.dtype)

    def drain(self):
        far, plain, added, direct = self.inbox
        for k, ref in enumerate((far, far, plain, plain, added, added)):
            take(ref.at[0], self.sends.at[k])
        take(direct.at[pl.ds(0, 7)], self.sends.at[6])


def ring_inbox(order, rows):
    half = (2, 2) if order[1] == "z" else (4,)
    block = (rows, 384)
    return [(2,) + half + block] * 3 + [(8,) + block]


class SeqSum:
    def __init__(self, part, twins, crossed, sends, recvs, f, s):
        self.part, self.twins, self.crossed = part, twins, crossed
        self.sends, self.recvs, self.f, self.s = sends, recvs, f, s
        self.twin = s + 1 - 2 * lax.rem(s, 2)
        self.across = lax.rem(s + 2, G)
        self.far_twin = 3 - s

    def ready(self, t):
        @pl.when(t == self.far_twin)
        def _():
            send(
                self.part.at[self.far_twin], self.twins.at[0], self.sends.at[0], self.recvs.at[0], self.f, self.twin
            )

        @pl.when(t == self.twin)
        def _():
            send(self.part.at[self.twin], self.twins.at[1], self.sends.at[2], self.recvs.at[2], self.f, self.twin)

    def relay(self, t):
        @pl.when(t == self.across)
        def _():
            take(self.twins.at[0], self.recvs.at[0])
            both = self.part[self.across].astype(jnp.float32) + self.twins[0].astype(jnp.float32)
            self.part[self.across] = both.astype(self.part.dtype)
            send(
                self.part.at[self.across], self.crossed, self.sends.at[1], self.recvs.at[1], self.f, self.across
            )

    def total(self):
        take(self.crossed, self.recvs.at[1])
        take(self.crossed, self.recvs.at[2])
        mine = self.part[self.s].astype(jnp.float32) + self.twins[1].astype(jnp.float32)
        return mine + self.crossed[...].astype(jnp.float32)

    def drain(self):
        for k in range(3):
            take(self.crossed, self.sends.at[k])


def cut_grad(left, right, part, first, chunks):
    low = part.dtype

    def chunk(c):
        columns = pl.ds(pl.multiple_of(c * 384, 128), 384)
        made = t_dot(left[:, columns], right[...])
        for i in range(16):
            block = made[i * ROWS : (i + 1) * ROWS]
            packed = jnp.concatenate([block[:, :384], block[:, 384:]], axis=0).astype(low)
            part[2 * c + i // 8, (i // 4) % 2, i % 4, first : first + 48, :] = packed

    loop(chunks, chunk)


def column_sum(values):
    return jnp.sum(values, axis=0, keepdims=True)


GATHER_PLAN = (("yz", 32), ("zy", 32), ("yz", 80), ("zy", 64))
RING_PLAN = (("yz", 48), ("zy", 48), ("yz", 16), ("yz", 32), ("zy", 32))


def layer_kernel(*refs):
    (
        src_a, src_b, src_c, src_d, src_x, src_dy,
        output, grad_input, fin_up, fin_down, fin_out, fin_a, fin_b,
        got_x, vec, normed, qkv, w_in, lse, got_ctx, w_out, w_up, w_down, got_dy,
        held_a, held_b, held_c, held_d,
        residual, normed_two, active, d_hidden, branch, d_ctx, d_proj, d_key, d_value, d_res, sums, grad_in,
        out_part, out_twins, out_crossed, two_part, two_twins, two_crossed, one_part, one_twins, one_crossed,
        part_up, part_down, part_out, part_a, part_b,
        *inboxes,
        ring_ss, ring_rs, seq_ss, seq_rs, seq_own, sum_ss, sum_rs, part_ss, part_rs,
    ) = refs
    low, full = jnp.bfloat16, jnp.float32
    f, s = place()
    greet_near(pltpu.get_barrier_semaphore(), f, s)
    sources = (src_a, src_b, src_c, src_d)
    helds = (held_a, held_b, held_c, held_d)
    rings = [
        Ring(sources[k], helds[k], ring_ss.at[k], ring_rs.at[k], GATHER_PLAN[k][0], f, s)
        for k in range(4)
    ]
    early, late = rings[:2], rings[2:]
    copies = [
        pltpu.make_async_copy(src, dst.at[s], seq_own.at[k])
        for k, (src, dst) in enumerate(((src_x, got_x), (src_dy, got_dy)))
    ]
    for copy in copies:
        copy.start()
    for ring in rings:
        ring.begin()
    share_x, share_dy = [
        Share(lambda i, dst=dst: dst.at[i], seq_ss.at[k], seq_rs.at[k], f, s)
        for k, dst in enumerate((got_x, got_dy))
    ]
    copies[0].wait()
    share_x.begin()
    masks = vector_masks(s)
    for ring in early:
        ring.last()
    for ring in early:
        ring.last_relay()
    share_x.relay()
    copies[1].wait()
    share_dy.begin()
    for ring in late:
        ring.last()
    share_x.arrive()
    rings[1].arrive()
    vec[...] = spread_vectors(held_b[:, :, :, 16:, :128], masks, s)
    gain, shift = vec[0:1, :], vec[1:2, :]

    def norm_tile(t):
        unit, _ = norm_parts(got_x[t].astype(jnp.float32))
        normed[tile(t), :] = (unit * gain + shift).astype(normed.dtype)

    loop(G, norm_tile)
    rings[0].arrive()
    unpack_rings(((held_a, 0, 32), (held_b, 0, 16)), w_in)
    bias = jnp.concatenate([vec[7:8, :PAD], jnp.zeros((1, PAD), jnp.float32), vec[8:9, :PAD]], axis=1)

    def project(t):
        made = (dot(normed[tile(t), :], w_in[...]) + bias).astype(qkv.dtype)
        qkv[tile(t), :PAD] = (made[:, :PAD].astype(jnp.float32) * SCALE).astype(qkv.dtype)
        qkv[tile(t), PAD:] = made[:, PAD:]

    loop(G, project)
    half = s // 2
    shares = [
        Share(lambda i, b=b: got_ctx.at[i, pl.ds(b * TOK, TOK)], seq_ss.at[2 + b], seq_rs.at[2 + b], f, s)
        for b in range(G)
    ]
    for b in (1, 0, 3, 2):
        rows, span = slice(b * TOK, (b + 1) * TOK), (b + 1) * TOK
        for pair in range(2):
            at = pair * 128
            made = None
            for h in range(2 * pair, min(2 * pair + 2, HEADS)):
                query = only(h, qkv[rows, at : at + 128])
                scores = causal(dot_t(query, qkv[:span, PAD + at : PAD + at + 128]), b * TOK)
                peak = jnp.max(scores, axis=-1, keepdims=True)
                weights = jnp.exp(scores - peak)
                total = jnp.sum(weights, axis=-1, keepdims=True)
                lse[h, rows, :] = peak + jnp.log(total)
                part = dot(weights.astype(qkv.dtype), qkv[:span, 2 * PAD + at : 2 * PAD + at + 128]) / total
                made = part if made is None else jnp.where(lanes_of(h, part.shape), part, made)
            got_ctx[s, rows, at : at + 128] = made.astype(got_ctx.dtype)
        shares[b].begin_twin()
        if b > 1:
            shares[b].begin_across()
        else:
            pl.when(half == 0)(shares[b].begin_across)

    @pl.when(half == 1)
    def _():
        shares[1].begin_across()
        shares[0].begin_across()

    for ring in late:
        ring.last_relay()
    share_dy.relay()
    for ring in late:
        ring.arrive()
    unpack_rings(((held_c, 0, 48),), w_out)
    unpack_rings(((held_c, 48, 32), (held_d, 0, 16)), w_up)
    unpack_rings(((held_d, 16, 48),), w_down)
    share_dy.arrive()

    sum_out = SeqSum(out_part, out_twins, out_crossed, part_ss.at[0], part_rs.at[0], f, s)
    sum_two = SeqSum(two_part, two_twins, two_crossed, part_ss.at[1], part_rs.at[1], f, s)
    sum_one = SeqSum(one_part, one_twins, one_crossed, part_ss.at[2], part_rs.at[2], f, s)
    sums[...] = jnp.zeros_like(sums)
    gain_two, shift_two = vec[2:3, :], vec[3:4, :]

    def turn(i):
        return lax.rem(7 - 2 * half - i, G)

    def context_at(t, action):
        for b in range(G):
            pl.when(t == b)(functools.partial(action, shares[b]))

    def land(share):
        share.relay()
        share.arrive()

    def feed(i):
        t = turn(i)
        context_at(t, land)
        rows = tile(t)
        value = got_x[t].astype(full) + vec[4:5, :]
        for g in range(G):
            value = value + dot(got_ctx[g, rows, :OWN], w_out[g * OWN : (g + 1) * OWN, :])
        residual[rows, :] = value
        unit, _ = norm_parts(value)
        normed_low = (unit * gain_two + shift_two).astype(low)
        normed_two[rows, :] = normed_low
        hidden = dot(normed_low, w_up[...]) + vec[6:7, :]
        cdf = 0.5 * (1.0 + lax.erf(hidden * math.sqrt(0.5)))
        active_low = (hidden * cdf).astype(low)
        active[rows, :] = active_low
        slope = cdf + hidden * jnp.exp(-0.5 * hidden * hidden) * (1.0 / math.sqrt(2.0 * math.pi))
        dy = got_dy[t]
        d_low = (dot_t(dy, w_down[...]) * slope).astype(low)
        d_hidden[rows, :] = d_low
        d_two = dot_t(d_low, w_up[...])
        two_part[t] = d_two.astype(low)
        sum_two.ready(t)
        sums[2:3, :] += column_sum(d_two * unit)
        sums[3:4, :] += column_sum(d_two)
        sums[8:9, :] += column_sum(d_low.astype(full))
        out_part[t] = dot(active_low, w_down[...]).astype(low)
        sum_out.ready(t)

        @pl.when(i > 0)
        def _():
            sum_two.relay(turn(i - 1))

    loop(G, feed)

    inbox = [inboxes[4 * k : 4 * k + 4] for k in range(5)]
    totals = (fin_up, fin_down, fin_out, fin_a, fin_b)
    parts = (part_up, part_down, part_out, part_a, part_b)
    adders = [
        RingSum(parts[k], inbox[k], totals[k], sum_ss.at[k], sum_rs.at[k], RING_PLAN[k][0], f, s) for k in range(5)
    ]
    finals = [
        Share(lambda i, k=k: totals[k].at[i], seq_ss.at[7 + k], seq_rs.at[7 + k], f, s) for k in range(5)
    ]

    def life(k):
        yield from adders[k].steps()
        finals[k].begin_all()
        yield
        finals[k].arrive_all()

    lives = [life(k) for k in range(5)]

    def advance(*which):
        for k in which:
            next(lives[k], None)

    cut_grad(normed_two, d_hidden, part_up, 0, 2)

    mine = tile(s)
    own_res = residual[mine, :]
    unit, inverse = norm_parts(own_res)
    own_dy = got_dy[s].astype(full)
    d_own = own_dy + norm_back(sum_two.total(), gain_two, unit, inverse)
    d_res[...] = d_own
    branch[s] = d_own.astype(low)
    share_branch = Share(lambda i: branch.at[i], seq_ss.at[6], seq_rs.at[6], f, s)
    share_branch.begin()
    advance(0)
    sums[4:5, :] += column_sum(d_own.astype(low).astype(full))
    sums[5:6, :] += column_sum(own_dy)
    dy_all = jnp.concatenate([got_dy[t] for t in range(G)], axis=0)

    def chunk_down(c):
        columns = pl.ds(pl.multiple_of(c * 384, 128), 384)
        made = t_dot(active[:, columns], dy_all)
        for i in range(16):
            block = made[i * ROWS : (i + 1) * ROWS]
            packed = jnp.concatenate([block[:, :384], block[:, 384:]], axis=0).astype(low)
            part_down[2 * c + i // 8, (i // 4) % 2, i % 4] = packed

    loop(2, chunk_down)
    advance(1)
    d_key[...] = jnp.zeros_like(d_key)
    d_value[...] = jnp.zeros_like(d_value)
    share_branch.relay()
    for t in range(G):
        sum_out.relay(t)
    share_branch.arrive()
    advance(0, 1)

    own_rows = pl.ds(pl.multiple_of(s * OWN, 64), OWN)
    pick = lax.broadcasted_iota(jnp.int32, (D, PAD), 0) == lax.broadcasted_iota(jnp.int32, (D, PAD), 1) + s * OWN
    pick = jnp.logical_and(pick, lax.broadcasted_iota(jnp.int32, (D, PAD), 1) < OWN)
    pick = pick.astype(full).astype(low)
    picked = [dot(branch[t], pick).astype(low) for t in range(G)]
    picked = jnp.concatenate(picked, axis=0)

    def cut_out(g):
        made = t_dot(got_ctx[g], picked)
        for i in range(8):
            one, two, three = [made[i * ROWS + 8 * r : i * ROWS + 8 * r + 8] for r in range(3)]
            upper = jnp.concatenate([one, two[:, :128]], axis=1)
            lower = jnp.concatenate([two[:, 128:], three], axis=1)
            part_out[g, i // 4, i % 4] = jnp.concatenate([upper, lower], axis=0).astype(low)

    loop(G, cut_out)
    advance(2)
    for b in (3, 2, 1, 0):
        rows, span = slice(b * TOK, (b + 1) * TOK), (b + 1) * TOK
        made = dot_t(branch[b], w_out[own_rows, :])
        d_block = jnp.concatenate([made, jnp.zeros((TOK, PAD - OWN), full)], axis=1).astype(low)
        for pair in range(2):
            at = pair * 128
            d_query = None
            for h in range(2 * pair, min(2 * pair + 2, HEADS)):
                query = only(h, qkv[rows, at : at + 128])
                key = qkv[:span, PAD + at : PAD + at + 128]
                grad = only(h, d_block[:, at : at + 128])
                probs = jnp.exp(causal(dot_t(query, key), b * TOK) - lse[h, rows, :])
                d_value[:span, at : at + 128] += t_dot(probs.astype(low), grad)
                d_probs = dot_t(grad, qkv[:span, 2 * PAD + at : 2 * PAD + at + 128])
                inner = jnp.sum(probs * d_probs, axis=-1, keepdims=True)
                d_scores = (probs * (d_probs - inner)).astype(low)
                d_key[:span, at : at + 128] += t_dot(d_scores, query)
                part = dot(d_scores, key) * SCALE
                d_query = part if d_query is None else jnp.where(lanes_of(h, part.shape), part, d_query)
            if pair:
                d_query = only(0, d_query)
            d_proj[rows, at : at + 128] = d_query.astype(low)
        if b != 1:
            advance(0, 1, 2) if b != 2 else advance(2)
        d_proj[rows, PAD : 2 * PAD] = d_key[rows, :].astype(low)
        d_proj[rows, 2 * PAD :] = d_value[rows, :].astype(low)
        d_one = dot_t(d_proj[rows, :], w_in[...])
        one_part[b] = d_one.astype(low)
        sum_one.ready(b)
        unit, _ = norm_parts(got_x[b].astype(full))
        sums[0:1, :] += column_sum(d_one * unit)
        sums[1:2, :] += column_sum(d_one)
        if b < 3:
            sum_one.relay(b + 1)
    sum_one.relay(0)

    sums[6:7, :PAD] = column_sum(d_proj[:, :PAD].astype(full))
    sums[7:8, :PAD] = column_sum(d_proj[:, 2 * PAD :].astype(full))
    lane = lax.broadcasted_iota(jnp.int32, (16, D), 1) // ROWS
    number = lax.broadcasted_iota(jnp.int32, (16, D), 0)
    up_row = jnp.broadcast_to(sums[8:9, :], (16, D))
    plain = jnp.where(number < 8, sums[...], jnp.where(number == 8 + s, up_row, 0.0))
    compact = lax.rem(lax.broadcasted_iota(jnp.int32, (D, 128), 0), ROWS) == lax.broadcasted_iota(
        jnp.int32, (D, 128), 1
    )
    compact = compact.astype(full).astype(low)
    pad_lanes = jnp.zeros((16, 256), low)

    def cut_in(c):
        columns = pl.ds(pl.multiple_of(c * 384, 128), 384)
        made = t_dot(normed[:, columns], d_proj[...])
        for i in range(16):
            block = made[i * ROWS : (i + 1) * ROWS]
            packed = jnp.concatenate([block[:, :384], block[:, 384:]], axis=0)
            at = (2 * c + i // 8, (i // 4) % 2, i % 4)
            part_a[at[0], at[1], at[2]] = packed[:32].astype(low)
            part_b[at[0], at[1], at[2], :16, :] = packed[32:].astype(low)
            owner = 16 * c + i
            wanted = jnp.where(jnp.logical_or(number == 6, number == 7), owner - 8 * s, owner)
            few = dot(jnp.where(lane == wanted, plain, 0.0).astype(low), compact).astype(low)
            part_b[at[0], at[1], at[2], 16:, :] = jnp.concatenate([few, pad_lanes], axis=1)

    loop(2, cut_in)
    advance(3, 4)
    output[...] = (own_res + sum_out.total() + vec[5:6, :]).astype(low)
    advance(3, 4)
    advance(0, 1, 2)
    advance(3, 4)
    unit, inverse = norm_parts(got_x[s].astype(full))
    grad_input[...] = (d_res[...] + norm_back(sum_one.total(), gain, unit, inverse)).astype(low)
    advance(3, 4)
    for k in (0, 1, 2, 3, 4):
        for _ in lives[k]:
            pass
    for share in [share_x, share_dy, share_branch] + shares + finals:
        share.drain()
    for ring in rings:
        ring.drain()
    for adder in adders + [sum_out, sum_two, sum_one]:
        adder.drain()


def layer(*sources):
    low, full = jnp.bfloat16, jnp.float32
    any_space, vmem = pl.BlockSpec(memory_space=pl.ANY), pl.BlockSpec(memory_space=pltpu.VMEM)
    outs = [jax.ShapeDtypeStruct((TOK, D), low)] * 2
    outs += [jax.ShapeDtypeStruct((G, rows, 384), low) for _, rows in RING_PLAN]
    seq_part = [pltpu.VMEM((G, TOK, D), low), pltpu.VMEM((2, TOK, D), low), pltpu.VMEM((TOK, D), low)]
    return pl.pallas_call(
        layer_kernel,
        out_shape=outs,
        in_specs=[any_space] * 6,
        out_specs=[vmem] * len(outs),
        scratch_shapes=[
            pltpu.VMEM((G, TOK, D), low),
            pltpu.VMEM((16, D), full),
            pltpu.VMEM((LEN, D), low),
            pltpu.VMEM((LEN, 3 * PAD), low),
            pltpu.VMEM((D, 3 * PAD), low),
            pltpu.VMEM((HEADS, LEN, 1), full),
            pltpu.VMEM((G, LEN, PAD), low),
            pltpu.VMEM((D, D), low),
            pltpu.VMEM((D, FFG), low),
            pltpu.VMEM((FFG, D), low),
            pltpu.VMEM((G, TOK, D), low),
        ]
        + [pltpu.VMEM((4, 2, 4, rows, 384), low) for _, rows in GATHER_PLAN]
        + [
            pltpu.VMEM((LEN, D), full),
            pltpu.VMEM((LEN, D), low),
            pltpu.VMEM((LEN, FFG), low),
            pltpu.VMEM((LEN, FFG), low),
            pltpu.VMEM((G, TOK, D), low),
            pltpu.VMEM((16, PAD), low),
            pltpu.VMEM((LEN, 3 * PAD), low),
            pltpu.VMEM((LEN, PAD), full),
            pltpu.VMEM((LEN, PAD), full),
            pltpu.VMEM((TOK, D), full),
            pltpu.VMEM((16, D), full),
            pltpu.VMEM((16, D), full),
        ]
        + seq_part * 3
        + [pltpu.VMEM((4, 2, 4, rows, 384), low) for _, rows in RING_PLAN]
        + [pltpu.VMEM(shape, low) for order, rows in RING_PLAN for shape in ring_inbox(order, rows)]
        + [pltpu.SemaphoreType.DMA((4, 9))] * 2
        + [pltpu.SemaphoreType.DMA((12, 3))] * 2
        + [pltpu.SemaphoreType.DMA((2,))]
        + [pltpu.SemaphoreType.DMA((5, 9))] * 2
        + [pltpu.SemaphoreType.DMA((3, 3))] * 2,
        compiler_params=pltpu.CompilerParams(
            collective_id=0, has_side_effects=True, vmem_limit_bytes=62 * 2**20
        ),
    )(*sources)


def on_device(
    inputs,
    proj_in,
    bias_query,
    bias_value,
    proj_out,
    bias_out,
    norm_gain,
    norm_shift,
    up_weight,
    up_bias,
    down_weight,
    down_bias,
    post_gain,
    post_shift,
    cotangent,
):
    low = jnp.bfloat16
    full = jnp.float32
    f, s = place()
    split = proj_in.reshape(ROWS, 3, G, OWN).transpose(2, 0, 1, 3)
    send_in = pack(pad_heads(split).reshape(G, ROWS, 3 * PAD))
    units = up_weight.reshape(ROWS, N, G, ROWS).transpose(2, 0, 1, 3).reshape(G, ROWS, FFG)
    send_out = jnp.broadcast_to(pack(proj_out)[None], (G, 48, 384))
    vectors = jnp.stack(
        [norm_gain, norm_shift, post_gain, post_shift, bias_out, down_bias, jnp.zeros_like(bias_out), bias_query, bias_value]
    )
    compact = jnp.pad(vectors, ((0, 7), (0, 384 - ROWS)))
    compact = compact + jnp.pad(up_bias[None], ((6, 9), (0, 384 - 96)))
    send_up = pack(units)
    compact = jnp.broadcast_to(compact[None], (G, 16, 384))
    src_a = send_in[:, :32]
    src_b = jnp.concatenate([send_in[:, 32:], compact], axis=1)
    src_c = jnp.concatenate([send_out, send_up[:, :32]], axis=1)
    src_d = jnp.concatenate([send_up[:, 32:], pack(down_weight.reshape(G, ROWS, D))], axis=1)
    output, grad_input, all_up, all_down, all_out, all_a, all_b = layer(
        src_a, src_b, src_c, src_d, inputs, cotangent
    )
    split_in = jnp.concatenate([all_a, all_b[:, :16]], axis=1)
    final_in = unpack(split_in.astype(full)).reshape(G, ROWS, 3, PAD)[..., :OWN].transpose(1, 2, 0, 3)
    final_up = unpack(all_up.astype(full)).reshape(G, ROWS, N, ROWS).transpose(1, 2, 0, 3).reshape(ROWS, G * FFG)
    upper, lower = all_out[:, :8].astype(full), all_out[:, 8:].astype(full)
    second = jnp.concatenate([upper[..., PAD:], lower[..., :128]], axis=-1)
    out_blocks = jnp.concatenate([upper[..., :PAD], second, lower[..., 128:]], axis=1)
    final_out = out_blocks[..., :OWN].transpose(1, 0, 2).reshape(ROWS, D)
    final_down = unpack(all_down.astype(full)).reshape(96, D)
    final_vec = jnp.sum(all_b[:, 16:, :ROWS].astype(full), axis=0)
    return (
        output,
        grad_input,
        final_in.reshape(ROWS, 3 * D),
        final_vec[6],
        final_vec[7],
        final_out,
        final_vec[4],
        final_vec[0],
        final_vec[1],
        final_up,
        final_vec[8:12].reshape(96),
        final_down,
        final_vec[5],
        final_vec[2],
        final_vec[3],
    )


def solution(mesh):
    rows, wide, flat = P(("fsdp", "seq"), None), P("fsdp", None), P("fsdp")
    return jax.shard_map(
        on_device,
        mesh=mesh,
        in_specs=(rows, wide, flat, flat, wide, flat, flat, flat, wide, flat, wide, flat, flat, flat, rows),
        out_specs=(rows, rows, wide, flat, flat, wide, flat, flat, flat, wide, flat, wide, flat, flat, flat),
        check_vma=False,
    )
```

```python
import functools
import math

import jax
import jax.numpy as jnp
from jax import lax
from jax.experimental import pallas as pl
from jax.experimental.pallas import tpu as pltpu
from jax.sharding import PartitionSpec as P

D = 768
H = 12
HD = 64
N = 32
G = 4
ROWS = 24
LEN = 1024
TOK = 256
HEADS = 3
OWN = HEADS * HD
PAD = 256
FFG = 768
epsilon = 1e-05
SCALE = 1.0 / math.sqrt(HD)
MESH = pl.DeviceIdType.MESH


def x_half(f):
    return lax.rem(f // 4, 2)


def place():
    return lax.axis_index("fsdp"), lax.axis_index("seq")


def send(src, dst, send_sem, recv_sem, f, s):
    pltpu.make_async_remote_copy(
        src_ref=src,
        dst_ref=dst,
        send_sem=send_sem,
        recv_sem=recv_sem,
        device_id=(f, s),
        device_id_type=MESH,
    ).start()


def take(ref, sem):
    pltpu.make_async_copy(ref, ref, sem).wait()


def loop(count, body):
    lax.fori_loop(0, count, lambda t, carry: (body(t), carry)[1], 0)


def greet(barrier, f, s):
    pl.semaphore_signal(barrier, inc=1, device_id=(f, s), device_id_type=MESH)


def pack(blocks):
    c = blocks.shape[-1] // 2
    return jnp.concatenate([blocks[..., :c], blocks[..., c:]], axis=-2)


def unpack(blocks):
    return jnp.concatenate([blocks[..., :ROWS, :], blocks[..., ROWS:, :]], axis=-1)


def pad_heads(blocks):
    return jnp.pad(blocks, [(0, 0)] * (blocks.ndim - 1) + [(0, PAD - OWN)])


def norm_parts(values):
    center = jnp.mean(values, axis=-1, keepdims=True)
    centered = values - center
    spread = jnp.mean(centered * centered, axis=-1, keepdims=True)
    inverse = lax.rsqrt(spread + epsilon)
    return centered * inverse, inverse


def norm_back(grad, gain, unit, inverse):
    scaled = grad * gain
    mean_one = jnp.mean(scaled, axis=-1, keepdims=True)
    mean_two = jnp.mean(scaled * unit, axis=-1, keepdims=True)
    return inverse * (scaled - mean_one - unit * mean_two)


def dot(a, b):
    return jnp.dot(a, b, preferred_element_type=jnp.float32)


def dot_t(a, b):
    return lax.dot_general(a, b, (((1,), (1,)), ((), ())), preferred_element_type=jnp.float32)


def t_dot(a, b):
    return lax.dot_general(a, b, (((0,), (0,)), ((), ())), preferred_element_type=jnp.float32)


def tile(t, size=TOK):
    return pl.ds(pl.multiple_of(t * size, size), size)


def lanes_of(h, shape):
    lane = lax.broadcasted_iota(jnp.int32, shape, 1)
    return lane < HD if h % 2 == 0 else lane >= HD


def only(h, block):
    return jnp.where(lanes_of(h, block.shape), block, jnp.zeros_like(block))


def causal(scores, offset):
    row = offset + lax.broadcasted_iota(jnp.int32, scores.shape, 0)
    col = lax.broadcasted_iota(jnp.int32, scores.shape, 1)
    return jnp.where(col <= row, scores, -1e9)


class Ring:
    def __init__(self, src, held, sends, recvs, order, f, s):
        self.src, self.held, self.sends, self.recvs = src, held, sends, recvs
        self.order, self.f, self.s = order, f, s
        self.y, self.h, self.z = f // 8, x_half(f), lax.rem(f, 4)

    def peer(self, axis, step):
        if axis == "y":
            return lax.rem(self.y + step + 4, 4) * 8 + lax.rem(self.f, 8), self.s
        return self.f - self.z + lax.rem(self.z + step + 4, 4), self.s

    def coordinate(self, axis, step):
        return lax.rem((self.y if axis == "y" else self.z) + step + 4, 4)

    def plane(self, t):
        h = lax.rem(self.h + t // 4, 2)
        if self.order[0] == "y":
            return lax.rem(self.y + t, 4) * 8 + h * 4 + self.z, t // 4
        return self.y * 8 + h * 4 + lax.rem(self.z + t, 4), t // 4

    def many(self, axis, step, half=None):
        i = self.coordinate(axis, step)
        if axis == "y":
            return self.held.at[i] if half is None else self.held.at[i, half]
        rows = slice(None) if half is None else slice(2 * half, 2 * half + 2)
        return self.held.at[rows, slice(None), i]

    def push(self, block, k, peer):
        send(block, block, self.sends.at[k], self.recvs.at[k], *peer)

    def begin(self):
        mine = self.held.at[self.y, self.h, self.z]

        def one(t, k):
            peer, away = self.plane(t)
            group = lax.rem(self.s + 2 * away, G)
            send(self.src.at[group], mine, self.sends.at[k], self.recvs.at[0], peer, group)

        loop(4, lambda t: one(t + 4, 0))
        loop(3, lambda t: one(t + 1, 7))
        pltpu.make_async_copy(self.src.at[self.s], mine, self.recvs.at[0]).start()

    def last(self):
        axis = self.order[1]
        take(self.many(axis, 0), self.recvs.at[0])
        for k, (part, step) in enumerate(((0, 1), (1, -1), (1, 1), (0, -1))):
            self.push(self.many(axis, 0, part), 1 + k, self.peer(axis, step))

    def last_relay(self):
        axis = self.order[1]
        for k, step in enumerate((1, -1)):
            part = self.many(axis, -step, k)
            take(part, self.recvs.at[1 + k])
            self.push(part, 5 + k, self.peer(axis, step))

    def arrive(self):
        for k in (3, 4, 5, 6):
            take(self.many(self.order[1], 0, 0), self.recvs.at[k])

    def drain(self):
        half = self.many(self.order[1], 0, 0)
        take(half, self.sends.at[0])
        take(self.held.at[0, 0, pl.ds(0, 3)], self.sends.at[7])
        for k in range(1, 7):
            take(half, self.sends.at[k])


class Share:
    def __init__(self, block, sends, recvs, f, s):
        self.block, self.sends, self.recvs, self.f, self.s = block, sends, recvs, f, s
        self.twin = s + 1 - 2 * lax.rem(s, 2)
        self.across = lax.rem(s + 2, G)

    def begin(self):
        self.begin_across()
        self.begin_twin()

    def begin_all(self):
        self.begin()
        mine = self.block(self.s)
        send(mine, mine, self.sends.at[2], self.recvs.at[2], self.f, 3 - self.s)

    def begin_across(self):
        mine = self.block(self.s)
        send(mine, mine, self.sends.at[1], self.recvs.at[1], self.f, self.across)

    def begin_twin(self):
        mine = self.block(self.s)
        send(mine, mine, self.sends.at[0], self.recvs.at[0], self.f, self.twin)

    def relay(self):
        theirs = self.block(self.across)
        take(theirs, self.recvs.at[1])
        send(theirs, theirs, self.sends.at[2], self.recvs.at[2], self.f, self.twin)

    def arrive(self):
        take(self.block(self.s), self.recvs.at[0])
        take(self.block(self.s), self.recvs.at[2])

    def arrive_all(self):
        self.arrive()
        take(self.block(self.s), self.recvs.at[1])

    def drain(self):
        for k in range(3):
            take(self.block(self.s), self.sends.at[k])


def greet_near(barrier, f, s):
    y, h, z = f // 8, x_half(f), lax.rem(f, 4)
    other = 1 - h

    def line(t):
        column, row = lax.rem(y + t, 4) * 8, lax.rem(z + t, 4)

        @pl.when(t > 0)
        def _():
            greet(barrier, column + h * 4 + z, s)
            greet(barrier, y * 8 + h * 4 + row, s)
            greet(barrier, f, lax.rem(s + t, G))
            greet(barrier, y * 8 + other * 4 + row, lax.rem(s + 2, G))

        greet(barrier, column + other * 4 + z, lax.rem(s + 2, G))

    loop(4, line)
    pl.semaphore_wait(barrier, 16)


def unpack_rings(pieces, wide):
    c = wide.shape[-1] // 2

    def block(y, h, z):
        parts = [held[y, h, z, first : first + rows, :].astype(jnp.float32) for held, first, rows in pieces]
        return parts[0] if len(parts) == 1 else jnp.concatenate(parts, axis=0)

    def pair(p):
        at = (p // 4, lax.rem(p // 2, 2))
        z = 2 * lax.rem(p, 2)
        one, two = block(*at, z), block(*at, z + 1)
        rows = pl.ds(pl.multiple_of(48 * p, 48), 48)
        wide[rows, :c] = jnp.concatenate([one[:ROWS], two[:ROWS]], axis=0).astype(wide.dtype)
        wide[rows, c:] = jnp.concatenate([one[ROWS:], two[ROWS:]], axis=0).astype(wide.dtype)

    loop(N // 2, pair)


def vector_masks(s):
    low, full = jnp.bfloat16, jnp.float32
    row = lax.broadcasted_iota(jnp.int32, (128, D), 0)
    inside = lax.rem(lax.broadcasted_iota(jnp.int32, (128, D), 1), ROWS)
    return (row == inside).astype(full).astype(low), (row == inside + ROWS * s).astype(full).astype(low)


def spread_vectors(blocks, masks, s):
    flat = blocks.reshape(N * 16, 128)
    straight, moved = [dot(flat, mask).reshape(N, 16, D) for mask in masks]
    owner = lax.broadcasted_iota(jnp.int32, (N, 16, D), 2) // ROWS
    number = lax.broadcasted_iota(jnp.int32, (N, 16, D), 1)
    j = lax.broadcasted_iota(jnp.int32, (N, 16, D), 0)
    wanted = jnp.where(number < 7, j, jnp.where(j // 8 == s, j - 8 * s, -1))
    return jnp.sum(jnp.where(owner == wanted, jnp.where(number == 6, moved, straight), 0.0), axis=0)


class RingSum:
    def __init__(self, part, inbox, total, sends, recvs, order, f, s):
        self.part, self.inbox, self.total = part, inbox, total
        self.sends, self.recvs, self.f, self.s = sends, recvs, f, s
        self.line = Ring(None, part, None, None, order, f, s)
        self.order = order

    def push(self, block, inbox, k, peer):
        send(block, inbox, self.sends.at[k], self.recvs.at[k], *peer)

    def add(self, block, *inboxes):
        total = block[...].astype(jnp.float32)
        for inbox in inboxes:
            total = total + inbox[...].astype(jnp.float32)
        block[...] = total.astype(block.dtype)

    def steps(self):
        line, axis = self.line, self.order[1]
        far, plain, added, direct = self.inbox
        sides = ((0, 1), (1, -1))
        for k, step in sides:
            self.push(line.many(axis, 2, k), far.at[k], k, line.peer(axis, step))
        for k, step in sides:
            self.push(line.many(axis, step, 1 - k), plain.at[k], 2 + k, line.peer(axis, step))
        yield
        for k, step in sides:
            take(far.at[k], self.recvs.at[k])
            self.add(line.many(axis, step, k), far.at[k])
            self.push(line.many(axis, step, k), added.at[k], 4 + k, line.peer(axis, step))
        yield
        for k, step in sides:
            take(plain.at[1 - k], self.recvs.at[3 - k])
            take(added.at[k], self.recvs.at[4 + k])
            self.add(line.many(axis, 0, k), added.at[k], plain.at[1 - k])
        first = line.y if self.order[0] == "y" else line.z
        slot = 2 * first + line.h

        def one(t):
            peer, away = line.plane(t + 1)
            block = self.part.at[peer // 8, x_half(peer), lax.rem(peer, 4)]
            group = lax.rem(self.s + 2 * away, G)
            send(block, direct.at[slot], self.sends.at[6], self.recvs.at[6], peer, group)

        loop(7, one)
        direct[slot] = self.part[line.y, line.h, line.z]
        yield
        take(direct.at[pl.ds(0, 7)], self.recvs.at[6])
        halves = direct[...].astype(jnp.float32).reshape(4, 2, *direct.shape[1:])
        halves = jnp.sum(halves, axis=0).astype(self.total.dtype)
        lower = line.h == 0
        self.total[self.s, 0] = jnp.where(lower, halves[0], halves[1])
        self.total[self.s, 1] = jnp.where(lower, halves[1], halves[0])

    def drain(self):
        far, plain, added, direct = self.inbox
        for k, ref in enumerate((far, far, plain, plain, added, added)):
            take(ref.at[0], self.sends.at[k])
        take(direct.at[pl.ds(0, 7)], self.sends.at[6])


def joined(total, g):
    return total[g, 0].astype(jnp.float32) + total[(g + 2) % G, 1].astype(jnp.float32)


def ring_inbox(order, rows):
    half = (2, 2) if order[1] == "z" else (4,)
    block = (rows, 384)
    return [(2,) + half + block] * 3 + [(8,) + block]


class SeqSum:
    def __init__(self, part, twins, crossed, sends, recvs, f, s):
        self.part, self.twins, self.crossed = part, twins, crossed
        self.sends, self.recvs, self.f, self.s = sends, recvs, f, s
        self.twin = s + 1 - 2 * lax.rem(s, 2)
        self.across = lax.rem(s + 2, G)
        self.far_twin = 3 - s

    def ready(self, t):
        @pl.when(t == self.far_twin)
        def _():
            send(
                self.part.at[self.far_twin], self.twins.at[0], self.sends.at[0], self.recvs.at[0], self.f, self.twin
            )

        @pl.when(t == self.twin)
        def _():
            send(self.part.at[self.twin], self.twins.at[1], self.sends.at[2], self.recvs.at[2], self.f, self.twin)

    def relay(self, t):
        @pl.when(t == self.across)
        def _():
            take(self.twins.at[0], self.recvs.at[0])
            both = self.part[self.across].astype(jnp.float32) + self.twins[0].astype(jnp.float32)
            self.part[self.across] = both.astype(self.part.dtype)
            send(
                self.part.at[self.across], self.crossed, self.sends.at[1], self.recvs.at[1], self.f, self.across
            )

    def total(self):
        take(self.crossed, self.recvs.at[1])
        take(self.crossed, self.recvs.at[2])
        mine = self.part[self.s].astype(jnp.float32) + self.twins[1].astype(jnp.float32)
        return mine + self.crossed[...].astype(jnp.float32)

    def drain(self):
        for k in range(3):
            take(self.crossed, self.sends.at[k])


def cut_grad(left, right, part, first, chunks):
    low = part.dtype

    def chunk(c):
        columns = pl.ds(pl.multiple_of(c * 384, 128), 384)
        made = t_dot(left[:, columns], right[...])
        for i in range(16):
            block = made[i * ROWS : (i + 1) * ROWS]
            packed = jnp.concatenate([block[:, :384], block[:, 384:]], axis=0).astype(low)
            part[2 * c + i // 8, (i // 4) % 2, i % 4, first : first + 48, :] = packed

    loop(chunks, chunk)


def column_sum(values):
    return jnp.sum(values, axis=0, keepdims=True)


GATHER_PLAN = (("yz", 32), ("zy", 32), ("yz", 80), ("zy", 64))
RING_PLAN = (("yz", 48), ("zy", 48), ("zy", 16), ("yz", 32), ("zy", 16), ("yz", 16))


def layer_kernel(*refs):
    (
        src_a, src_b, src_c, src_d, src_x, src_dy,
        output, grad_input, out_in, out_out, out_up, out_down, out_vec,
        fin_up, fin_down, fin_out, fin_a, fin_b, fin_vec,
        got_x, vec, normed, qkv, w_in, lse, got_ctx, w_out, w_up, w_down, got_dy,
        held_a, held_b, held_c, held_d,
        residual, normed_two, active, d_hidden, branch, d_send, d_ctx, d_proj, d_key, d_value, d_res, sums,
        out_part, out_twins, out_crossed, two_part, two_twins, two_crossed, one_part, one_twins, one_crossed,
        part_up, part_down, part_out, part_a, part_b, part_vec,
        *inboxes,
        ring_ss, ring_rs, seq_ss, seq_rs, seq_own, sum_ss, sum_rs, part_ss, part_rs,
    ) = refs
    low, full = jnp.bfloat16, jnp.float32
    f, s = place()
    greet_near(pltpu.get_barrier_semaphore(), f, s)
    sources = (src_a, src_b, src_c, src_d)
    helds = (held_a, held_b, held_c, held_d)
    rings = [
        Ring(sources[k], helds[k], ring_ss.at[k], ring_rs.at[k], GATHER_PLAN[k][0], f, s)
        for k in range(4)
    ]
    early, late = rings[:2], rings[2:]
    copies = [
        pltpu.make_async_copy(src, dst.at[s], seq_own.at[k])
        for k, (src, dst) in enumerate(((src_x, got_x), (src_dy, got_dy)))
    ]
    for copy in copies:
        copy.start()
    for ring in rings:
        ring.begin()
    share_x, share_dy = [
        Share(lambda i, dst=dst: dst.at[i], seq_ss.at[k], seq_rs.at[k], f, s)
        for k, dst in enumerate((got_x, got_dy))
    ]
    copies[0].wait()
    share_x.begin()
    masks = vector_masks(s)
    for ring in early:
        ring.last()
    for ring in early:
        ring.last_relay()
    share_x.relay()
    copies[1].wait()
    share_dy.begin()
    for ring in late:
        ring.last()
    share_x.arrive()
    rings[1].arrive()
    vec[...] = spread_vectors(held_b[:, :, :, 16:, :128], masks, s)
    gain, shift = vec[0:1, :], vec[1:2, :]

    def norm_tile(t):
        unit, _ = norm_parts(got_x[t].astype(jnp.float32))
        normed[tile(t), :] = (unit * gain + shift).astype(normed.dtype)

    loop(G, norm_tile)
    rings[0].arrive()
    unpack_rings(((held_a, 0, 32), (held_b, 0, 16)), w_in)
    bias = jnp.concatenate([vec[7:8, :PAD], jnp.zeros((1, PAD), jnp.float32), vec[8:9, :PAD]], axis=1)

    def project(t):
        made = (dot(normed[tile(t), :], w_in[...]) + bias).astype(qkv.dtype)
        qkv[tile(t), :PAD] = (made[:, :PAD].astype(jnp.float32) * SCALE).astype(qkv.dtype)
        qkv[tile(t), PAD:] = made[:, PAD:]

    loop(G, project)
    half = s // 2
    shares = [
        Share(lambda i, b=b: got_ctx.at[i, pl.ds(b * TOK, TOK)], seq_ss.at[2 + b], seq_rs.at[2 + b], f, s)
        for b in range(G)
    ]
    for b in (1, 0, 3, 2):
        rows, span = slice(b * TOK, (b + 1) * TOK), (b + 1) * TOK
        for pair in range(2):
            at = pair * 128
            made = None
            for h in range(2 * pair, min(2 * pair + 2, HEADS)):
                query = only(h, qkv[rows, at : at + 128])
                scores = causal(dot_t(query, qkv[:span, PAD + at : PAD + at + 128]), b * TOK)
                peak = jnp.max(scores, axis=-1, keepdims=True)
                weights = jnp.exp(scores - peak)
                total = jnp.sum(weights, axis=-1, keepdims=True)
                lse[h, rows, :] = peak + jnp.log(total)
                part = dot(weights.astype(qkv.dtype), qkv[:span, 2 * PAD + at : 2 * PAD + at + 128]) / total
                made = part if made is None else jnp.where(lanes_of(h, part.shape), part, made)
            got_ctx[s, rows, at : at + 128] = made.astype(got_ctx.dtype)
        shares[b].begin_twin()
        if b > 1:
            shares[b].begin_across()
        else:
            pl.when(half == 0)(shares[b].begin_across)

    @pl.when(half == 1)
    def _():
        shares[1].begin_across()
        shares[0].begin_across()

    for ring in late:
        ring.last_relay()
    share_dy.relay()
    for ring in late:
        ring.arrive()
    unpack_rings(((held_c, 0, 48),), w_out)
    unpack_rings(((held_c, 48, 32), (held_d, 0, 16)), w_up)
    unpack_rings(((held_d, 16, 48),), w_down)
    share_dy.arrive()

    sum_out = SeqSum(out_part, out_twins, out_crossed, part_ss.at[0], part_rs.at[0], f, s)
    sum_two = SeqSum(two_part, two_twins, two_crossed, part_ss.at[1], part_rs.at[1], f, s)
    sum_one = SeqSum(one_part, one_twins, one_crossed, part_ss.at[2], part_rs.at[2], f, s)
    sums[...] = jnp.zeros_like(sums)
    gain_two, shift_two = vec[2:3, :], vec[3:4, :]

    def turn(i):
        return lax.rem(7 - 2 * half - i, G)

    def context_at(t, action):
        for b in range(G):
            pl.when(t == b)(functools.partial(action, shares[b]))

    def land(share):
        share.relay()
        share.arrive()

    def feed(i):
        t = turn(i)
        context_at(t, land)
        rows = tile(t)
        value = got_x[t].astype(full) + vec[4:5, :]
        for g in range(G):
            value = value + dot(got_ctx[g, rows, :OWN], w_out[g * OWN : (g + 1) * OWN, :])
        residual[rows, :] = value
        unit, _ = norm_parts(value)
        normed_low = (unit * gain_two + shift_two).astype(low)
        normed_two[rows, :] = normed_low
        hidden = dot(normed_low, w_up[...]) + vec[6:7, :]
        cdf = 0.5 * (1.0 + lax.erf(hidden * math.sqrt(0.5)))
        active_low = (hidden * cdf).astype(low)
        active[rows, :] = active_low
        slope = cdf + hidden * jnp.exp(-0.5 * hidden * hidden) * (1.0 / math.sqrt(2.0 * math.pi))
        dy = got_dy[t]
        d_low = (dot_t(dy, w_down[...]) * slope).astype(low)
        d_hidden[rows, :] = d_low
        d_two = dot_t(d_low, w_up[...])
        two_part[t] = d_two.astype(low)
        sum_two.ready(t)
        sums[2:3, :] += column_sum(d_two * unit)
        sums[3:4, :] += column_sum(d_two)
        sums[8:9, :] += column_sum(d_low.astype(full))
        out_part[t] = dot(active_low, w_down[...]).astype(low)
        sum_out.ready(t)

        @pl.when(i > 0)
        def _():
            sum_two.relay(turn(i - 1))

    loop(G, feed)

    inbox = [inboxes[4 * k : 4 * k + 4] for k in range(6)]
    totals = (fin_up, fin_down, fin_out, fin_a, fin_b, fin_vec)
    parts = (part_up, part_down, part_out, part_a, part_b, part_vec)
    adders = [
        RingSum(parts[k], inbox[k], totals[k], sum_ss.at[k], sum_rs.at[k], RING_PLAN[k][0], f, s) for k in range(6)
    ]
    finals = [
        Share(lambda i, k=k: totals[k].at[i], seq_ss.at[7 + k], seq_rs.at[7 + k], f, s) for k in range(6)
    ]

    def life(k):
        yield from adders[k].steps()
        finals[k].begin_all()
        yield
        finals[k].arrive_all()

    lives = [life(k) for k in range(6)]

    def advance(*which):
        for k in which:
            next(lives[k], None)

    cut_grad(normed_two, d_hidden, part_up, 0, 2)

    mine = tile(s)
    own_res = residual[mine, :]
    unit, inverse = norm_parts(own_res)
    own_dy = got_dy[s].astype(full)
    d_own = own_dy + norm_back(sum_two.total(), gain_two, unit, inverse)
    d_res[...] = d_own
    own_branch = d_own.astype(low)
    branch[s] = own_branch
    for g in range(G):
        made = dot_t(own_branch, w_out[g * OWN : (g + 1) * OWN, :])
        d_send[g] = jnp.concatenate([made, jnp.zeros((TOK, PAD - OWN), full)], axis=1).astype(low)
    for k, peer in enumerate((sum_two.across, sum_two.far_twin, sum_two.twin)):
        send(d_send.at[peer], d_ctx.at[s], seq_ss.at[13, k], seq_rs.at[13, k], f, peer)
    d_ctx[s] = d_send[s]
    share_branch = Share(lambda i: branch.at[i], seq_ss.at[6], seq_rs.at[6], f, s)
    share_branch.begin()
    advance(0)
    sums[4:5, :] += column_sum(d_own.astype(low).astype(full))
    sums[5:6, :] += column_sum(own_dy)
    dy_all = jnp.concatenate([got_dy[t] for t in range(G)], axis=0)

    def chunk_down(c):
        columns = pl.ds(pl.multiple_of(c * 384, 128), 384)
        made = t_dot(active[:, columns], dy_all)
        for i in range(16):
            block = made[i * ROWS : (i + 1) * ROWS]
            packed = jnp.concatenate([block[:, :384], block[:, 384:]], axis=0).astype(low)
            part_down[2 * c + i // 8, (i // 4) % 2, i % 4] = packed

    loop(2, chunk_down)
    advance(1)
    d_key[...] = jnp.zeros_like(d_key)
    d_value[...] = jnp.zeros_like(d_value)
    for k in range(3):
        take(d_ctx.at[0], seq_rs.at[13, k])
    advance(0)

    for b in (3, 2, 1, 0):
        rows, span = slice(b * TOK, (b + 1) * TOK), (b + 1) * TOK
        d_block = d_ctx[b]
        for pair in range(2):
            at = pair * 128
            d_query = None
            for h in range(2 * pair, min(2 * pair + 2, HEADS)):
                query = only(h, qkv[rows, at : at + 128])
                key = qkv[:span, PAD + at : PAD + at + 128]
                grad = only(h, d_block[:, at : at + 128])
                probs = jnp.exp(causal(dot_t(query, key), b * TOK) - lse[h, rows, :])
                d_value[:span, at : at + 128] += t_dot(probs.astype(low), grad)
                d_probs = dot_t(grad, qkv[:span, 2 * PAD + at : 2 * PAD + at + 128])
                inner = jnp.sum(probs * d_probs, axis=-1, keepdims=True)
                d_scores = (probs * (d_probs - inner)).astype(low)
                d_key[:span, at : at + 128] += t_dot(d_scores, query)
                part = dot(d_scores, key) * SCALE
                d_query = part if d_query is None else jnp.where(lanes_of(h, part.shape), part, d_query)
            if pair:
                d_query = only(0, d_query)
            d_proj[rows, at : at + 128] = d_query.astype(low)
        d_proj[rows, PAD : 2 * PAD] = d_key[rows, :].astype(low)
        d_proj[rows, 2 * PAD :] = d_value[rows, :].astype(low)
        if b == 3:
            advance(1)
        if b == 2:
            advance(0)
            for t in range(G):
                sum_out.relay(t)

    def cut_in(c):
        columns = pl.ds(pl.multiple_of(c * 384, 128), 384)
        made = t_dot(normed[:, columns], d_proj[...])
        for i in range(16):
            block = made[i * ROWS : (i + 1) * ROWS]
            packed = jnp.concatenate([block[:, :384], block[:, 384:]], axis=0)
            at = (2 * c + i // 8, (i // 4) % 2, i % 4)
            part_a[at[0], at[1], at[2]] = packed[:32].astype(low)
            part_b[at[0], at[1], at[2]] = packed[32:].astype(low)

    loop(2, cut_in)
    advance(3, 4)
    advance(1)

    def feed_back(i):
        t = turn(i)
        d_one = dot_t(d_proj[tile(t), :], w_in[...])
        one_part[t] = d_one.astype(low)
        sum_one.ready(t)
        unit, _ = norm_parts(got_x[t].astype(full))
        sums[0:1, :] += column_sum(d_one * unit)
        sums[1:2, :] += column_sum(d_one)

        @pl.when(i > 0)
        def _():
            sum_one.relay(turn(i - 1))

    share_branch.relay()
    loop(G, feed_back)
    advance(0)
    sums[6:7, :PAD] = column_sum(d_proj[:, :PAD].astype(full))
    sums[7:8, :PAD] = column_sum(d_proj[:, 2 * PAD :].astype(full))
    lane = lax.broadcasted_iota(jnp.int32, (16, D), 1) // ROWS
    number = lax.broadcasted_iota(jnp.int32, (16, D), 0)
    up_row = jnp.broadcast_to(sums[8:9, :], (16, D))
    plain = jnp.where(number < 8, sums[...], jnp.where(number == 8 + s, up_row, 0.0))
    compact = lax.rem(lax.broadcasted_iota(jnp.int32, (D, 128), 0), ROWS) == lax.broadcasted_iota(
        jnp.int32, (D, 128), 1
    )
    compact = compact.astype(full).astype(low)
    pad_lanes = jnp.zeros((16, 256), low)
    def cut_vec(g):
        for i in range(8):
            owner = 8 * g + i
            wanted = jnp.where(jnp.logical_or(number == 6, number == 7), owner - 8 * s, owner)
            few = dot(jnp.where(lane == wanted, plain, 0.0).astype(low), compact).astype(low)
            part_vec[g, i // 4, i % 4] = jnp.concatenate([few, pad_lanes], axis=1)

    loop(G, cut_vec)
    advance(5)
    pick_row = lax.broadcasted_iota(jnp.int32, (D, PAD), 0)
    pick_lane = lax.broadcasted_iota(jnp.int32, (D, PAD), 1)
    pick = jnp.where(pick_lane < OWN, pick_lane + s * OWN, -1) == pick_row
    pick = pick.astype(full).astype(low)
    share_branch.arrive()
    picked = jnp.concatenate([dot(branch[t], pick).astype(low) for t in range(G)], axis=0)

    def cut_out(g):
        made = t_dot(got_ctx[g], picked)
        for i in range(8):
            one, two, three = [made[i * ROWS + 8 * r : i * ROWS + 8 * r + 8] for r in range(3)]
            upper = jnp.concatenate([one, two[:, :128]], axis=1)
            lower = jnp.concatenate([two[:, 128:], three], axis=1)
            part_out[g, i // 4, i % 4] = jnp.concatenate([upper, lower], axis=0).astype(low)

    loop(G, cut_out)
    advance(2)
    advance(3, 4)
    advance(1)
    output[...] = (own_res + sum_out.total() + vec[5:6, :]).astype(low)
    place_row = lax.broadcasted_iota(jnp.int32, (PAD, D), 0)
    place_lane = lax.broadcasted_iota(jnp.int32, (PAD, D), 1)
    places = [
        (jnp.where(place_row < OWN, place_row + g * OWN, -1) == place_lane).astype(full).astype(low)
        for g in range(G)
    ]
    advance(5)
    advance(3, 4)
    advance(0)
    advance(2)
    advance(1)
    def place_up(g):
        n = lax.broadcasted_iota(jnp.int32, (1, 1536), 1)
        inside = lax.rem(n, 96) - ROWS * g
        source = jnp.where(jnp.logical_and(inside >= 0, inside < ROWS), n // 96 * ROWS + inside, -1)
        places = lax.broadcasted_iota(jnp.int32, (384, 1536), 0) == source
        made = dot(joined(fin_up, g).astype(low), places.astype(full).astype(low))
        out_up[:, :1536] += made[:ROWS]
        out_up[:, 1536:] += made[ROWS:]

    out_up[...] = jnp.zeros_like(out_up)
    loop(G, place_up)
    for g in range(G):
        block = joined(fin_down, g)
        out_down[g * ROWS : (g + 1) * ROWS, :384] = block[:ROWS]
        out_down[g * ROWS : (g + 1) * ROWS, 384:] = block[ROWS:]
    advance(5)
    advance(2)
    advance(3, 4)
    unit, inverse = norm_parts(got_x[s].astype(full))
    grad_input[...] = (d_res[...] + norm_back(sum_one.total(), gain, unit, inverse)).astype(low)
    advance(5, 2)
    advance(3, 4)
    total_in = jnp.zeros((3 * ROWS, D), full)
    for g in range(G):
        block = jnp.concatenate([joined(fin_a, g), joined(fin_b, g)], axis=0)
        wide = jnp.concatenate([block[:ROWS], block[ROWS:]], axis=1)
        tall = jnp.concatenate([wide[:, k * PAD : (k + 1) * PAD] for k in range(3)], axis=0)
        total_in = total_in + dot(tall.astype(low), places[g])
    for k in range(3):
        out_in[:, k * D : (k + 1) * D] = total_in[k * ROWS : (k + 1) * ROWS]
    advance(5, 2)
    total_out = jnp.zeros((ROWS, D), full)
    total_vec = jnp.zeros((16, 128), full)
    for g in range(G):
        both = joined(fin_out, g)
        upper, lower = both[:8], both[8:]
        middle = jnp.concatenate([upper[:, PAD:], lower[:, :128]], axis=1)
        block = jnp.concatenate([upper[:, :PAD], middle, lower[:, 128:]], axis=0)
        total_out = total_out + dot(block.astype(low), places[g])
        total_vec = total_vec + joined(fin_vec, g)[:, :128]
    out_out[...] = total_out
    out_vec[...] = total_vec
    for k in range(6):
        for _ in lives[k]:
            pass
    for share in [share_x, share_dy, share_branch] + shares + finals:
        share.drain()
    for k in range(3):
        take(d_send.at[0], seq_ss.at[13, k])
    for ring in rings:
        ring.drain()
    for adder in adders + [sum_out, sum_two, sum_one]:
        adder.drain()


def layer(*sources):
    low, full = jnp.bfloat16, jnp.float32
    any_space, vmem = pl.BlockSpec(memory_space=pl.ANY), pl.BlockSpec(memory_space=pltpu.VMEM)
    outs = [jax.ShapeDtypeStruct((TOK, D), low)] * 2
    outs += [
        jax.ShapeDtypeStruct(shape, full)
        for shape in ((ROWS, 3 * D), (ROWS, D), (ROWS, G * FFG), (G * ROWS, D), (16, 128))
    ]
    seq_part = [pltpu.VMEM((G, TOK, D), low), pltpu.VMEM((2, TOK, D), low), pltpu.VMEM((TOK, D), low)]
    return pl.pallas_call(
        layer_kernel,
        out_shape=outs,
        in_specs=[any_space] * 6,
        out_specs=[vmem] * len(outs),
        scratch_shapes=[pltpu.VMEM((G, 2, rows, 384), low) for _, rows in RING_PLAN]
        + [
            pltpu.VMEM((G, TOK, D), low),
            pltpu.VMEM((16, D), full),
            pltpu.VMEM((LEN, D), low),
            pltpu.VMEM((LEN, 3 * PAD), low),
            pltpu.VMEM((D, 3 * PAD), low),
            pltpu.VMEM((HEADS, LEN, 1), full),
            pltpu.VMEM((G, LEN, PAD), low),
            pltpu.VMEM((D, D), low),
            pltpu.VMEM((D, FFG), low),
            pltpu.VMEM((FFG, D), low),
            pltpu.VMEM((G, TOK, D), low),
        ]
        + [pltpu.VMEM((4, 2, 4, rows, 384), low) for _, rows in GATHER_PLAN]
        + [
            pltpu.VMEM((LEN, D), full),
            pltpu.VMEM((LEN, D), low),
            pltpu.VMEM((LEN, FFG), low),
            pltpu.VMEM((LEN, FFG), low),
            pltpu.VMEM((G, TOK, D), low),
            pltpu.VMEM((G, TOK, PAD), low),
            pltpu.VMEM((G, TOK, PAD), low),
            pltpu.VMEM((LEN, 3 * PAD), low),
            pltpu.VMEM((LEN, PAD), full),
            pltpu.VMEM((LEN, PAD), full),
            pltpu.VMEM((TOK, D), full),
            pltpu.VMEM((16, D), full),
        ]
        + seq_part * 3
        + [pltpu.VMEM((4, 2, 4, rows, 384), low) for _, rows in RING_PLAN]
        + [pltpu.VMEM(shape, low) for order, rows in RING_PLAN for shape in ring_inbox(order, rows)]
        + [pltpu.SemaphoreType.DMA((4, 9))] * 2
        + [pltpu.SemaphoreType.DMA((14, 3))] * 2
        + [pltpu.SemaphoreType.DMA((2,))]
        + [pltpu.SemaphoreType.DMA((6, 9))] * 2
        + [pltpu.SemaphoreType.DMA((3, 3))] * 2,
        compiler_params=pltpu.CompilerParams(
            collective_id=0, has_side_effects=True, vmem_limit_bytes=62 * 2**20
        ),
    )(*sources)


def on_device(
    inputs,
    proj_in,
    bias_query,
    bias_value,
    proj_out,
    bias_out,
    norm_gain,
    norm_shift,
    up_weight,
    up_bias,
    down_weight,
    down_bias,
    post_gain,
    post_shift,
    cotangent,
):
    low = jnp.bfloat16
    full = jnp.float32
    f, s = place()
    split = proj_in.reshape(ROWS, 3, G, OWN).transpose(2, 0, 1, 3)
    send_in = pack(pad_heads(split).reshape(G, ROWS, 3 * PAD))
    units = up_weight.reshape(ROWS, N, G, ROWS).transpose(2, 0, 1, 3).reshape(G, ROWS, FFG)
    send_out = jnp.broadcast_to(pack(proj_out)[None], (G, 48, 384))
    vectors = jnp.stack(
        [norm_gain, norm_shift, post_gain, post_shift, bias_out, down_bias, jnp.zeros_like(bias_out), bias_query, bias_value]
    )
    compact = jnp.pad(vectors, ((0, 7), (0, 384 - ROWS)))
    compact = compact + jnp.pad(up_bias[None], ((6, 9), (0, 384 - 96)))
    send_up = pack(units)
    compact = jnp.broadcast_to(compact[None], (G, 16, 384))
    src_a = send_in[:, :32]
    src_b = jnp.concatenate([send_in[:, 32:], compact], axis=1)
    src_c = jnp.concatenate([send_out, send_up[:, :32]], axis=1)
    src_d = jnp.concatenate([send_up[:, 32:], pack(down_weight.reshape(G, ROWS, D))], axis=1)
    output, grad_input, final_in, final_out, final_up, final_down, final_vec = layer(
        src_a, src_b, src_c, src_d, inputs, cotangent
    )
    final_vec = final_vec[:, :ROWS]
    return (
        output,
        grad_input,
        final_in,
        final_vec[6],
        final_vec[7],
        final_out,
        final_vec[4],
        final_vec[0],
        final_vec[1],
        final_up,
        final_vec[8:12].reshape(96),
        final_down,
        final_vec[5],
        final_vec[2],
        final_vec[3],
    )


def solution(mesh):
    rows, wide, flat = P(("fsdp", "seq"), None), P("fsdp", None), P("fsdp")
    return jax.shard_map(
        on_device,
        mesh=mesh,
        in_specs=(rows, wide, flat, flat, wide, flat, flat, flat, wide, flat, wide, flat, flat, flat, rows),
        out_specs=(rows, rows, wide, flat, flat, wide, flat, flat, flat, wide, flat, wide, flat, flat, flat),
        check_vma=False,
    )
```

```python
import functools
import math

import jax
import jax.numpy as jnp
from jax import lax
from jax.experimental import pallas as pl
from jax.experimental.pallas import tpu as pltpu
from jax.sharding import PartitionSpec as P

D = 768
H = 12
HD = 64
N = 32
G = 4
ROWS = 24
LEN = 1024
TOK = 256
HEADS = 3
OWN = HEADS * HD
PAD = 256
FFG = 768
epsilon = 1e-05
SCALE = 1.0 / math.sqrt(HD)
MESH = pl.DeviceIdType.MESH


def x_half(f):
    return lax.rem(f // 4, 2)


def place():
    return lax.axis_index("fsdp"), lax.axis_index("seq")


def send(src, dst, send_sem, recv_sem, f, s):
    pltpu.make_async_remote_copy(
        src_ref=src,
        dst_ref=dst,
        send_sem=send_sem,
        recv_sem=recv_sem,
        device_id=(f, s),
        device_id_type=MESH,
    ).start()


def take(ref, sem):
    pltpu.make_async_copy(ref, ref, sem).wait()


def loop(count, body):
    lax.fori_loop(0, count, lambda t, carry: (body(t), carry)[1], 0)


def greet(barrier, f, s):
    pl.semaphore_signal(barrier, inc=1, device_id=(f, s), device_id_type=MESH)


def pack(blocks):
    c = blocks.shape[-1] // 2
    return jnp.concatenate([blocks[..., :c], blocks[..., c:]], axis=-2)


def unpack(blocks):
    return jnp.concatenate([blocks[..., :ROWS, :], blocks[..., ROWS:, :]], axis=-1)


def pad_heads(blocks):
    return jnp.pad(blocks, [(0, 0)] * (blocks.ndim - 1) + [(0, PAD - OWN)])


def norm_parts(values):
    center = jnp.mean(values, axis=-1, keepdims=True)
    centered = values - center
    spread = jnp.mean(centered * centered, axis=-1, keepdims=True)
    inverse = lax.rsqrt(spread + epsilon)
    return centered * inverse, inverse


def norm_back(grad, gain, unit, inverse):
    scaled = grad * gain
    mean_one = jnp.mean(scaled, axis=-1, keepdims=True)
    mean_two = jnp.mean(scaled * unit, axis=-1, keepdims=True)
    return inverse * (scaled - mean_one - unit * mean_two)


def dot(a, b):
    return jnp.dot(a, b, preferred_element_type=jnp.float32)


def dot_t(a, b):
    return lax.dot_general(a, b, (((1,), (1,)), ((), ())), preferred_element_type=jnp.float32)


def t_dot(a, b):
    return lax.dot_general(a, b, (((0,), (0,)), ((), ())), preferred_element_type=jnp.float32)


def tile(t, size=TOK):
    return pl.ds(pl.multiple_of(t * size, size), size)


def lanes_of(h, shape):
    lane = lax.broadcasted_iota(jnp.int32, shape, 1)
    return lane < HD if h % 2 == 0 else lane >= HD


def only(h, block):
    return jnp.where(lanes_of(h, block.shape), block, jnp.zeros_like(block))


def causal(scores, offset):
    row = offset + lax.broadcasted_iota(jnp.int32, scores.shape, 0)
    col = lax.broadcasted_iota(jnp.int32, scores.shape, 1)
    return jnp.where(col <= row, scores, -1e9)


class Ring:
    def __init__(self, src, held, sends, recvs, order, f, s):
        self.src, self.held, self.sends, self.recvs = src, held, sends, recvs
        self.order, self.f, self.s = order, f, s
        self.y, self.h, self.z = f // 8, x_half(f), lax.rem(f, 4)

    def peer(self, axis, step):
        if axis == "y":
            return lax.rem(self.y + step + 4, 4) * 8 + lax.rem(self.f, 8), self.s
        return self.f - self.z + lax.rem(self.z + step + 4, 4), self.s

    def coordinate(self, axis, step):
        return lax.rem((self.y if axis == "y" else self.z) + step + 4, 4)

    def plane(self, t):
        h = lax.rem(self.h + t // 4, 2)
        if self.order[0] == "y":
            return lax.rem(self.y + t, 4) * 8 + h * 4 + self.z, t // 4
        return self.y * 8 + h * 4 + lax.rem(self.z + t, 4), t // 4

    def many(self, axis, step, half=None):
        i = self.coordinate(axis, step)
        if axis == "y":
            return self.held.at[i] if half is None else self.held.at[i, half]
        rows = slice(None) if half is None else slice(2 * half, 2 * half + 2)
        return self.held.at[rows, slice(None), i]

    def push(self, block, k, peer):
        send(block, block, self.sends.at[k], self.recvs.at[k], *peer)

    def begin(self):
        mine = self.held.at[self.y, self.h, self.z]

        def one(t, k):
            peer, away = self.plane(t)
            group = lax.rem(self.s + 2 * away, G)
            send(self.src.at[group], mine, self.sends.at[k], self.recvs.at[0], peer, group)

        loop(4, lambda t: one(t + 4, 0))
        loop(3, lambda t: one(t + 1, 7))
        pltpu.make_async_copy(self.src.at[self.s], mine, self.recvs.at[0]).start()

    def last(self):
        axis = self.order[1]
        take(self.many(axis, 0), self.recvs.at[0])
        for k, (part, step) in enumerate(((0, 1), (1, -1), (1, 1), (0, -1))):
            self.push(self.many(axis, 0, part), 1 + k, self.peer(axis, step))

    def last_relay(self):
        axis = self.order[1]
        for k, step in enumerate((1, -1)):
            part = self.many(axis, -step, k)
            take(part, self.recvs.at[1 + k])
            self.push(part, 5 + k, self.peer(axis, step))

    def arrive(self):
        for k in (3, 4, 5, 6):
            take(self.many(self.order[1], 0, 0), self.recvs.at[k])

    def drain(self):
        half = self.many(self.order[1], 0, 0)
        take(half, self.sends.at[0])
        take(self.held.at[0, 0, pl.ds(0, 3)], self.sends.at[7])
        for k in range(1, 7):
            take(half, self.sends.at[k])


class Share:
    def __init__(self, block, sends, recvs, f, s):
        self.block, self.sends, self.recvs, self.f, self.s = block, sends, recvs, f, s
        self.twin = s + 1 - 2 * lax.rem(s, 2)
        self.across = lax.rem(s + 2, G)

    def begin(self):
        self.begin_across()
        self.begin_twin()

    def begin_all(self):
        self.begin()
        mine = self.block(self.s)
        send(mine, mine, self.sends.at[2], self.recvs.at[2], self.f, 3 - self.s)

    def begin_across(self):
        mine = self.block(self.s)
        send(mine, mine, self.sends.at[1], self.recvs.at[1], self.f, self.across)

    def begin_twin(self):
        mine = self.block(self.s)
        send(mine, mine, self.sends.at[0], self.recvs.at[0], self.f, self.twin)

    def relay(self):
        theirs = self.block(self.across)
        take(theirs, self.recvs.at[1])
        send(theirs, theirs, self.sends.at[2], self.recvs.at[2], self.f, self.twin)

    def arrive(self):
        take(self.block(self.s), self.recvs.at[0])
        take(self.block(self.s), self.recvs.at[2])

    def arrive_all(self):
        self.arrive()
        take(self.block(self.s), self.recvs.at[1])

    def drain(self):
        for k in range(3):
            take(self.block(self.s), self.sends.at[k])


def greet_near(barrier, f, s):
    y, h, z = f // 8, x_half(f), lax.rem(f, 4)
    other = 1 - h

    def line(t):
        column, row = lax.rem(y + t, 4) * 8, lax.rem(z + t, 4)

        @pl.when(t > 0)
        def _():
            greet(barrier, column + h * 4 + z, s)
            greet(barrier, y * 8 + h * 4 + row, s)
            greet(barrier, f, lax.rem(s + t, G))
            greet(barrier, y * 8 + other * 4 + row, lax.rem(s + 2, G))

        greet(barrier, column + other * 4 + z, lax.rem(s + 2, G))

    loop(4, line)
    pl.semaphore_wait(barrier, 16)


def unpack_rings(pieces, wide):
    c = wide.shape[-1] // 2

    def block(y, h, z):
        parts = [held[y, h, z, first : first + rows, :].astype(jnp.float32) for held, first, rows in pieces]
        return parts[0] if len(parts) == 1 else jnp.concatenate(parts, axis=0)

    def pair(p):
        at = (p // 4, lax.rem(p // 2, 2))
        z = 2 * lax.rem(p, 2)
        one, two = block(*at, z), block(*at, z + 1)
        rows = pl.ds(pl.multiple_of(48 * p, 48), 48)
        wide[rows, :c] = jnp.concatenate([one[:ROWS], two[:ROWS]], axis=0).astype(wide.dtype)
        wide[rows, c:] = jnp.concatenate([one[ROWS:], two[ROWS:]], axis=0).astype(wide.dtype)

    loop(N // 2, pair)


def vector_masks(s):
    low, full = jnp.bfloat16, jnp.float32
    row = lax.broadcasted_iota(jnp.int32, (128, D), 0)
    inside = lax.rem(lax.broadcasted_iota(jnp.int32, (128, D), 1), ROWS)
    return (row == inside).astype(full).astype(low), (row == inside + ROWS * s).astype(full).astype(low)


def spread_vectors(blocks, masks, s):
    flat = blocks.reshape(N * 16, 128)
    straight, moved = [dot(flat, mask).reshape(N, 16, D) for mask in masks]
    owner = lax.broadcasted_iota(jnp.int32, (N, 16, D), 2) // ROWS
    number = lax.broadcasted_iota(jnp.int32, (N, 16, D), 1)
    j = lax.broadcasted_iota(jnp.int32, (N, 16, D), 0)
    wanted = jnp.where(number < 7, j, jnp.where(j // 8 == s, j - 8 * s, -1))
    return jnp.sum(jnp.where(owner == wanted, jnp.where(number == 6, moved, straight), 0.0), axis=0)


class RingSum:
    def __init__(self, part, inbox, total, sends, recvs, order, f, s):
        self.part, self.inbox, self.total = part, inbox, total
        self.sends, self.recvs, self.f, self.s = sends, recvs, f, s
        self.line = Ring(None, part, None, None, order, f, s)
        self.order = order

    def push(self, block, inbox, k, peer):
        send(block, inbox, self.sends.at[k], self.recvs.at[k], *peer)

    def add(self, block, *inboxes):
        total = block[...].astype(jnp.float32)
        for inbox in inboxes:
            total = total + inbox[...].astype(jnp.float32)
        block[...] = total.astype(block.dtype)

    def steps(self):
        line, axis = self.line, self.order[1]
        far, plain, added, direct = self.inbox
        sides = ((0, 1), (1, -1))
        for k, step in sides:
            self.push(line.many(axis, 2, k), far.at[k], k, line.peer(axis, step))
        for k, step in sides:
            self.push(line.many(axis, step, 1 - k), plain.at[k], 2 + k, line.peer(axis, step))
        yield
        for k, step in sides:
            take(far.at[k], self.recvs.at[k])
            self.add(line.many(axis, step, k), far.at[k])
            self.push(line.many(axis, step, k), added.at[k], 4 + k, line.peer(axis, step))
        yield
        for k, step in sides:
            take(plain.at[1 - k], self.recvs.at[3 - k])
            take(added.at[k], self.recvs.at[4 + k])
            self.add(line.many(axis, 0, k), added.at[k], plain.at[1 - k])
        first = line.y if self.order[0] == "y" else line.z
        slot = 2 * first + line.h

        def one(t):
            peer, away = line.plane(t + 1)
            block = self.part.at[peer // 8, x_half(peer), lax.rem(peer, 4)]
            group = lax.rem(self.s + 2 * away, G)
            send(block, direct.at[slot], self.sends.at[6], self.recvs.at[6], peer, group)

        loop(7, one)
        direct[slot] = self.part[line.y, line.h, line.z]
        yield
        take(direct.at[pl.ds(0, 7)], self.recvs.at[6])
        halves = direct[...].astype(jnp.float32).reshape(4, 2, *direct.shape[1:])
        halves = jnp.sum(halves, axis=0).astype(self.total.dtype)
        lower = line.h == 0
        self.total[self.s, 0] = jnp.where(lower, halves[0], halves[1])
        self.total[self.s, 1] = jnp.where(lower, halves[1], halves[0])

    def drain(self):
        far, plain, added, direct = self.inbox
        for k, ref in enumerate((far, far, plain, plain, added, added)):
            take(ref.at[0], self.sends.at[k])
        take(direct.at[pl.ds(0, 7)], self.sends.at[6])


def joined(total, g):
    return total[g, 0].astype(jnp.float32) + total[(g + 2) % G, 1].astype(jnp.float32)


def ring_inbox(order, rows):
    half = (2, 2) if order[1] == "z" else (4,)
    block = (rows, 384)
    return [(2,) + half + block] * 3 + [(8,) + block]


class SeqSum:
    def __init__(self, part, twins, crossed, sends, recvs, f, s):
        self.part, self.twins, self.crossed = part, twins, crossed
        self.sends, self.recvs, self.f, self.s = sends, recvs, f, s
        self.twin = s + 1 - 2 * lax.rem(s, 2)
        self.across = lax.rem(s + 2, G)
        self.far_twin = 3 - s

    def ready(self, t):
        @pl.when(t == self.far_twin)
        def _():
            send(
                self.part.at[self.far_twin], self.twins.at[0], self.sends.at[0], self.recvs.at[0], self.f, self.twin
            )

        @pl.when(t == self.twin)
        def _():
            send(self.part.at[self.twin], self.twins.at[1], self.sends.at[2], self.recvs.at[2], self.f, self.twin)

    def relay(self, t):
        @pl.when(t == self.across)
        def _():
            take(self.twins.at[0], self.recvs.at[0])
            both = self.part[self.across].astype(jnp.float32) + self.twins[0].astype(jnp.float32)
            self.part[self.across] = both.astype(self.part.dtype)
            send(
                self.part.at[self.across], self.crossed, self.sends.at[1], self.recvs.at[1], self.f, self.across
            )

    def total(self):
        take(self.crossed, self.recvs.at[1])
        take(self.crossed, self.recvs.at[2])
        mine = self.part[self.s].astype(jnp.float32) + self.twins[1].astype(jnp.float32)
        return mine + self.crossed[...].astype(jnp.float32)

    def drain(self):
        for k in range(3):
            take(self.crossed, self.sends.at[k])


def cut_grad(left, right, part, first, chunks):
    low = part.dtype

    def chunk(c):
        columns = pl.ds(pl.multiple_of(c * 384, 128), 384)
        made = t_dot(left[:, columns], right[...])
        for i in range(16):
            block = made[i * ROWS : (i + 1) * ROWS]
            packed = jnp.concatenate([block[:, :384], block[:, 384:]], axis=0).astype(low)
            part[2 * c + i // 8, (i // 4) % 2, i % 4, first : first + 48, :] = packed

    loop(chunks, chunk)


def column_sum(values):
    return jnp.sum(values, axis=0, keepdims=True)


GATHER_PLAN = (("yz", 32), ("zy", 32), ("yz", 80), ("zy", 64))
RING_PLAN = (("yz", 48), ("zy", 48), ("zy", 16), ("yz", 32), ("zy", 16), ("yz", 16))


def layer_kernel(*refs):
    (
        src_a, src_b, src_c, src_d, src_x, src_dy,
        out_rows, out_wide, out_down, out_vec,
        fin_up, fin_down, fin_out, fin_a, fin_b, fin_vec,
        got_x, vec, normed, qkv, w_in, lse, got_ctx, w_out, w_up, w_down, got_dy,
        held_a, held_b, held_c, held_d,
        residual, normed_two, active, d_hidden, branch, d_send, d_ctx, d_proj, d_key, d_value, d_res, sums,
        out_part, out_twins, out_crossed, two_part, two_twins, two_crossed, one_part, one_twins, one_crossed,
        part_up, part_down, part_out, part_a, part_b, part_vec,
        *inboxes,
        ring_ss, ring_rs, seq_ss, seq_rs, seq_own, sum_ss, sum_rs, part_ss, part_rs,
    ) = refs
    low, full = jnp.bfloat16, jnp.float32
    f, s = place()
    greet_near(pltpu.get_barrier_semaphore(), f, s)
    sources = (src_a, src_b, src_c, src_d)
    helds = (held_a, held_b, held_c, held_d)
    rings = [
        Ring(sources[k], helds[k], ring_ss.at[k], ring_rs.at[k], GATHER_PLAN[k][0], f, s)
        for k in range(4)
    ]
    early, late = rings[:2], rings[2:]
    copies = [
        pltpu.make_async_copy(src, dst.at[s], seq_own.at[k])
        for k, (src, dst) in enumerate(((src_x, got_x), (src_dy, got_dy)))
    ]
    for copy in copies:
        copy.start()
    for ring in rings:
        ring.begin()
    share_x, share_dy = [
        Share(lambda i, dst=dst: dst.at[i], seq_ss.at[k], seq_rs.at[k], f, s)
        for k, dst in enumerate((got_x, got_dy))
    ]
    copies[0].wait()
    share_x.begin()
    masks = vector_masks(s)
    for ring in early:
        ring.last()
    for ring in early:
        ring.last_relay()
    share_x.relay()
    copies[1].wait()
    share_dy.begin()
    for ring in late:
        ring.last()
    share_x.arrive()
    rings[1].arrive()
    vec[...] = spread_vectors(held_b[:, :, :, 16:, :128], masks, s)
    gain, shift = vec[0:1, :], vec[1:2, :]

    def norm_tile(t):
        unit, _ = norm_parts(got_x[t].astype(jnp.float32))
        normed[tile(t), :] = (unit * gain + shift).astype(normed.dtype)

    loop(G, norm_tile)
    rings[0].arrive()
    unpack_rings(((held_a, 0, 32), (held_b, 0, 16)), w_in)
    bias = jnp.concatenate([vec[7:8, :PAD], jnp.zeros((1, PAD), jnp.float32), vec[8:9, :PAD]], axis=1)

    def project(t):
        made = (dot(normed[tile(t), :], w_in[...]) + bias).astype(qkv.dtype)
        qkv[tile(t), :PAD] = (made[:, :PAD].astype(jnp.float32) * SCALE).astype(qkv.dtype)
        qkv[tile(t), PAD:] = made[:, PAD:]

    loop(G, project)
    half = s // 2
    shares = [
        Share(lambda i, b=b: got_ctx.at[i, pl.ds(b * TOK, TOK)], seq_ss.at[2 + b], seq_rs.at[2 + b], f, s)
        for b in range(G)
    ]
    for b in (1, 0, 3, 2):
        rows, span = slice(b * TOK, (b + 1) * TOK), (b + 1) * TOK
        for pair in range(2):
            at = pair * 128
            made = None
            for h in range(2 * pair, min(2 * pair + 2, HEADS)):
                query = only(h, qkv[rows, at : at + 128])
                scores = causal(dot_t(query, qkv[:span, PAD + at : PAD + at + 128]), b * TOK)
                peak = jnp.max(scores, axis=-1, keepdims=True)
                weights = jnp.exp(scores - peak)
                total = jnp.sum(weights, axis=-1, keepdims=True)
                lse[h, rows, :] = peak + jnp.log(total)
                part = dot(weights.astype(qkv.dtype), qkv[:span, 2 * PAD + at : 2 * PAD + at + 128]) / total
                made = part if made is None else jnp.where(lanes_of(h, part.shape), part, made)
            got_ctx[s, rows, at : at + 128] = made.astype(got_ctx.dtype)
        shares[b].begin_twin()
        if b > 1:
            shares[b].begin_across()
        else:
            pl.when(half == 0)(shares[b].begin_across)

    @pl.when(half == 1)
    def _():
        shares[1].begin_across()
        shares[0].begin_across()

    for ring in late:
        ring.last_relay()
    share_dy.relay()
    for ring in late:
        ring.arrive()
    unpack_rings(((held_c, 0, 48),), w_out)
    unpack_rings(((held_c, 48, 32), (held_d, 0, 16)), w_up)
    unpack_rings(((held_d, 16, 48),), w_down)
    share_dy.arrive()

    sum_out = SeqSum(out_part, out_twins, out_crossed, part_ss.at[0], part_rs.at[0], f, s)
    sum_two = SeqSum(two_part, two_twins, two_crossed, part_ss.at[1], part_rs.at[1], f, s)
    sum_one = SeqSum(one_part, one_twins, one_crossed, part_ss.at[2], part_rs.at[2], f, s)
    sums[...] = jnp.zeros_like(sums)
    gain_two, shift_two = vec[2:3, :], vec[3:4, :]

    def turn(i):
        return lax.rem(7 - 2 * half - i, G)

    def context_at(t, action):
        for b in range(G):
            pl.when(t == b)(functools.partial(action, shares[b]))

    def land(share):
        share.relay()
        share.arrive()

    def feed(i):
        t = turn(i)
        context_at(t, land)
        rows = tile(t)
        value = got_x[t].astype(full) + vec[4:5, :]
        for g in range(G):
            value = value + dot(got_ctx[g, rows, :OWN], w_out[g * OWN : (g + 1) * OWN, :])
        residual[rows, :] = value
        unit, _ = norm_parts(value)
        normed_low = (unit * gain_two + shift_two).astype(low)
        normed_two[rows, :] = normed_low
        hidden = dot(normed_low, w_up[...]) + vec[6:7, :]
        cdf = 0.5 * (1.0 + lax.erf(hidden * math.sqrt(0.5)))
        active_low = (hidden * cdf).astype(low)
        active[rows, :] = active_low
        slope = cdf + hidden * jnp.exp(-0.5 * hidden * hidden) * (1.0 / math.sqrt(2.0 * math.pi))
        dy = got_dy[t]
        d_low = (dot_t(dy, w_down[...]) * slope).astype(low)
        d_hidden[rows, :] = d_low
        d_two = dot_t(d_low, w_up[...])
        two_part[t] = d_two.astype(low)
        sum_two.ready(t)
        sums[2:3, :] += column_sum(d_two * unit)
        sums[3:4, :] += column_sum(d_two)
        sums[8:9, :] += column_sum(d_low.astype(full))
        out_part[t] = dot(active_low, w_down[...]).astype(low)
        sum_out.ready(t)

        @pl.when(i > 0)
        def _():
            sum_two.relay(turn(i - 1))

    loop(G, feed)

    inbox = [inboxes[4 * k : 4 * k + 4] for k in range(6)]
    totals = (fin_up, fin_down, fin_out, fin_a, fin_b, fin_vec)
    parts = (part_up, part_down, part_out, part_a, part_b, part_vec)
    adders = [
        RingSum(parts[k], inbox[k], totals[k], sum_ss.at[k], sum_rs.at[k], RING_PLAN[k][0], f, s) for k in range(6)
    ]
    finals = [
        Share(lambda i, k=k: totals[k].at[i], seq_ss.at[7 + k], seq_rs.at[7 + k], f, s) for k in range(6)
    ]

    def life(k):
        yield from adders[k].steps()
        finals[k].begin_all()
        yield
        finals[k].arrive_all()

    lives = [life(k) for k in range(6)]

    def advance(*which):
        for k in which:
            next(lives[k], None)

    cut_grad(normed_two, d_hidden, part_up, 0, 2)

    mine = tile(s)
    own_res = residual[mine, :]
    unit, inverse = norm_parts(own_res)
    own_dy = got_dy[s].astype(full)
    d_own = own_dy + norm_back(sum_two.total(), gain_two, unit, inverse)
    d_res[...] = d_own
    own_branch = d_own.astype(low)
    branch[s] = own_branch
    for g in range(G):
        made = dot_t(own_branch, w_out[g * OWN : (g + 1) * OWN, :])
        d_send[g] = jnp.concatenate([made, jnp.zeros((TOK, PAD - OWN), full)], axis=1).astype(low)
    for k, peer in enumerate((sum_two.across, sum_two.far_twin, sum_two.twin)):
        send(d_send.at[peer], d_ctx.at[s], seq_ss.at[13, k], seq_rs.at[13, k], f, peer)
    d_ctx[s] = d_send[s]
    share_branch = Share(lambda i: branch.at[i], seq_ss.at[6], seq_rs.at[6], f, s)
    share_branch.begin()
    advance(0)
    sums[4:5, :] += column_sum(d_own.astype(low).astype(full))
    sums[5:6, :] += column_sum(own_dy)
    dy_all = jnp.concatenate([got_dy[t] for t in range(G)], axis=0)

    def chunk_down(c):
        columns = pl.ds(pl.multiple_of(c * 384, 128), 384)
        made = t_dot(active[:, columns], dy_all)
        for i in range(16):
            block = made[i * ROWS : (i + 1) * ROWS]
            packed = jnp.concatenate([block[:, :384], block[:, 384:]], axis=0).astype(low)
            part_down[2 * c + i // 8, (i // 4) % 2, i % 4] = packed

    loop(2, chunk_down)
    advance(1)
    d_key[...] = jnp.zeros_like(d_key)
    d_value[...] = jnp.zeros_like(d_value)
    for k in range(3):
        take(d_ctx.at[0], seq_rs.at[13, k])
    advance(0)

    for b in (3, 2, 1, 0):
        rows, span = slice(b * TOK, (b + 1) * TOK), (b + 1) * TOK
        d_block = d_ctx[b]
        for pair in range(2):
            at = pair * 128
            d_query = None
            for h in range(2 * pair, min(2 * pair + 2, HEADS)):
                query = only(h, qkv[rows, at : at + 128])
                key = qkv[:span, PAD + at : PAD + at + 128]
                grad = only(h, d_block[:, at : at + 128])
                probs = jnp.exp(causal(dot_t(query, key), b * TOK) - lse[h, rows, :])
                d_value[:span, at : at + 128] += t_dot(probs.astype(low), grad)
                d_probs = dot_t(grad, qkv[:span, 2 * PAD + at : 2 * PAD + at + 128])
                inner = jnp.sum(probs * d_probs, axis=-1, keepdims=True)
                d_scores = (probs * (d_probs - inner)).astype(low)
                d_key[:span, at : at + 128] += t_dot(d_scores, query)
                part = dot(d_scores, key) * SCALE
                d_query = part if d_query is None else jnp.where(lanes_of(h, part.shape), part, d_query)
            if pair:
                d_query = only(0, d_query)
            d_proj[rows, at : at + 128] = d_query.astype(low)
        d_proj[rows, PAD : 2 * PAD] = d_key[rows, :].astype(low)
        d_proj[rows, 2 * PAD :] = d_value[rows, :].astype(low)
        if b == 3:
            advance(1)
        if b == 2:
            advance(0)
            for t in range(G):
                sum_out.relay(t)

    def cut_in(c):
        columns = pl.ds(pl.multiple_of(c * 384, 128), 384)
        made = t_dot(normed[:, columns], d_proj[...])
        for i in range(16):
            block = made[i * ROWS : (i + 1) * ROWS]
            packed = jnp.concatenate([block[:, :384], block[:, 384:]], axis=0)
            at = (2 * c + i // 8, (i // 4) % 2, i % 4)
            part_a[at[0], at[1], at[2]] = packed[:32].astype(low)
            part_b[at[0], at[1], at[2]] = packed[32:].astype(low)

    loop(2, cut_in)
    advance(3, 4)
    advance(1)

    def feed_back(i):
        t = turn(i)
        d_one = dot_t(d_proj[tile(t), :], w_in[...])
        one_part[t] = d_one.astype(low)
        sum_one.ready(t)
        unit, _ = norm_parts(got_x[t].astype(full))
        sums[0:1, :] += column_sum(d_one * unit)
        sums[1:2, :] += column_sum(d_one)

        @pl.when(i > 0)
        def _():
            sum_one.relay(turn(i - 1))

    share_branch.relay()
    loop(G, feed_back)
    advance(0)
    sums[6:7, :PAD] = column_sum(d_proj[:, :PAD].astype(full))
    sums[7:8, :PAD] = column_sum(d_proj[:, 2 * PAD :].astype(full))
    lane = lax.broadcasted_iota(jnp.int32, (16, D), 1) // ROWS
    number = lax.broadcasted_iota(jnp.int32, (16, D), 0)
    up_row = jnp.broadcast_to(sums[8:9, :], (16, D))
    plain = jnp.where(number < 8, sums[...], jnp.where(number == 8 + s, up_row, 0.0))
    compact = lax.rem(lax.broadcasted_iota(jnp.int32, (D, 128), 0), ROWS) == lax.broadcasted_iota(
        jnp.int32, (D, 128), 1
    )
    compact = compact.astype(full).astype(low)
    pad_lanes = jnp.zeros((16, 256), low)
    def cut_vec(g):
        for i in range(8):
            owner = 8 * g + i
            wanted = jnp.where(jnp.logical_or(number == 6, number == 7), owner - 8 * s, owner)
            few = dot(jnp.where(lane == wanted, plain, 0.0).astype(low), compact).astype(low)
            part_vec[g, i // 4, i % 4] = jnp.concatenate([few, pad_lanes], axis=1)

    loop(G, cut_vec)
    advance(5)
    pick_row = lax.broadcasted_iota(jnp.int32, (D, PAD), 0)
    pick_lane = lax.broadcasted_iota(jnp.int32, (D, PAD), 1)
    pick = jnp.where(pick_lane < OWN, pick_lane + s * OWN, -1) == pick_row
    pick = pick.astype(full).astype(low)
    share_branch.arrive()
    picked = jnp.concatenate([dot(branch[t], pick).astype(low) for t in range(G)], axis=0)

    def cut_out(g):
        made = t_dot(got_ctx[g], picked)
        for i in range(8):
            one, two, three = [made[i * ROWS + 8 * r : i * ROWS + 8 * r + 8] for r in range(3)]
            upper = jnp.concatenate([one, two[:, :128]], axis=1)
            lower = jnp.concatenate([two[:, 128:], three], axis=1)
            part_out[g, i // 4, i % 4] = jnp.concatenate([upper, lower], axis=0).astype(low)

    loop(G, cut_out)
    advance(2)
    advance(3, 4)
    advance(1)
    out_rows[:TOK, :] = (own_res + sum_out.total() + vec[5:6, :]).astype(low)
    place_row = lax.broadcasted_iota(jnp.int32, (PAD, D), 0)
    place_lane = lax.broadcasted_iota(jnp.int32, (PAD, D), 1)
    places = [
        (jnp.where(place_row < OWN, place_row + g * OWN, -1) == place_lane).astype(full).astype(low)
        for g in range(G)
    ]
    advance(5)
    advance(3, 4)
    advance(0)
    advance(2)
    advance(1)
    def place_up(g):
        n = lax.broadcasted_iota(jnp.int32, (1, 1536), 1)
        inside = lax.rem(n, 96) - ROWS * g
        source = jnp.where(jnp.logical_and(inside >= 0, inside < ROWS), n // 96 * ROWS + inside, -1)
        places = lax.broadcasted_iota(jnp.int32, (384, 1536), 0) == source
        made = dot(joined(fin_up, g).astype(low), places.astype(full).astype(low))
        out_wide[:, 4 * D : 6 * D] += made[:ROWS]
        out_wide[:, 6 * D :] += made[ROWS:]

    out_wide[:, 4 * D :] = jnp.zeros((ROWS, 4 * D), full)
    loop(G, place_up)
    for g in range(G):
        block = joined(fin_down, g)
        out_down[g * ROWS : (g + 1) * ROWS, :384] = block[:ROWS]
        out_down[g * ROWS : (g + 1) * ROWS, 384:] = block[ROWS:]
    advance(5)
    advance(2)
    advance(3, 4)
    unit, inverse = norm_parts(got_x[s].astype(full))
    out_rows[TOK:, :] = (d_res[...] + norm_back(sum_one.total(), gain, unit, inverse)).astype(low)
    advance(5, 2)
    advance(3, 4)
    total_in = jnp.zeros((3 * ROWS, D), full)
    for g in range(G):
        block = jnp.concatenate([joined(fin_a, g), joined(fin_b, g)], axis=0)
        wide = jnp.concatenate([block[:ROWS], block[ROWS:]], axis=1)
        tall = jnp.concatenate([wide[:, k * PAD : (k + 1) * PAD] for k in range(3)], axis=0)
        total_in = total_in + dot(tall.astype(low), places[g])
    for k in range(3):
        out_wide[:, k * D : (k + 1) * D] = total_in[k * ROWS : (k + 1) * ROWS]
    advance(5, 2)
    total_out = jnp.zeros((ROWS, D), full)
    total_vec = jnp.zeros((16, 128), full)
    for g in range(G):
        both = joined(fin_out, g)
        upper, lower = both[:8], both[8:]
        middle = jnp.concatenate([upper[:, PAD:], lower[:, :128]], axis=1)
        block = jnp.concatenate([upper[:, :PAD], middle, lower[:, 128:]], axis=0)
        total_out = total_out + dot(block.astype(low), places[g])
        total_vec = total_vec + joined(fin_vec, g)[:, :128]
    out_wide[:, 3 * D : 4 * D] = total_out
    out_vec[...] = total_vec
    for k in range(6):
        for _ in lives[k]:
            pass
    for share in [share_x, share_dy, share_branch] + shares + finals:
        share.drain()
    for k in range(3):
        take(d_send.at[0], seq_ss.at[13, k])
    for ring in rings:
        ring.drain()
    for adder in adders + [sum_out, sum_two, sum_one]:
        adder.drain()


def layer(*sources):
    low, full = jnp.bfloat16, jnp.float32
    any_space, vmem = pl.BlockSpec(memory_space=pl.ANY), pl.BlockSpec(memory_space=pltpu.VMEM)
    outs = [jax.ShapeDtypeStruct((2 * TOK, D), low)]
    outs += [
        jax.ShapeDtypeStruct(shape, full)
        for shape in ((ROWS, 8 * D), (G * ROWS, D), (16, 128))
    ]
    seq_part = [pltpu.VMEM((G, TOK, D), low), pltpu.VMEM((2, TOK, D), low), pltpu.VMEM((TOK, D), low)]
    return pl.pallas_call(
        layer_kernel,
        out_shape=outs,
        in_specs=[any_space] * 6,
        out_specs=[vmem] * len(outs),
        scratch_shapes=[pltpu.VMEM((G, 2, rows, 384), low) for _, rows in RING_PLAN]
        + [
            pltpu.VMEM((G, TOK, D), low),
            pltpu.VMEM((16, D), full),
            pltpu.VMEM((LEN, D), low),
            pltpu.VMEM((LEN, 3 * PAD), low),
            pltpu.VMEM((D, 3 * PAD), low),
            pltpu.VMEM((HEADS, LEN, 1), full),
            pltpu.VMEM((G, LEN, PAD), low),
            pltpu.VMEM((D, D), low),
            pltpu.VMEM((D, FFG), low),
            pltpu.VMEM((FFG, D), low),
            pltpu.VMEM((G, TOK, D), low),
        ]
        + [pltpu.VMEM((4, 2, 4, rows, 384), low) for _, rows in GATHER_PLAN]
        + [
            pltpu.VMEM((LEN, D), full),
            pltpu.VMEM((LEN, D), low),
            pltpu.VMEM((LEN, FFG), low),
            pltpu.VMEM((LEN, FFG), low),
            pltpu.VMEM((G, TOK, D), low),
            pltpu.VMEM((G, TOK, PAD), low),
            pltpu.VMEM((G, TOK, PAD), low),
            pltpu.VMEM((LEN, 3 * PAD), low),
            pltpu.VMEM((LEN, PAD), full),
            pltpu.VMEM((LEN, PAD), full),
            pltpu.VMEM((TOK, D), full),
            pltpu.VMEM((16, D), full),
        ]
        + seq_part * 3
        + [pltpu.VMEM((4, 2, 4, rows, 384), low) for _, rows in RING_PLAN]
        + [pltpu.VMEM(shape, low) for order, rows in RING_PLAN for shape in ring_inbox(order, rows)]
        + [pltpu.SemaphoreType.DMA((4, 9))] * 2
        + [pltpu.SemaphoreType.DMA((14, 3))] * 2
        + [pltpu.SemaphoreType.DMA((2,))]
        + [pltpu.SemaphoreType.DMA((6, 9))] * 2
        + [pltpu.SemaphoreType.DMA((3, 3))] * 2,
        compiler_params=pltpu.CompilerParams(
            collective_id=0, has_side_effects=True, vmem_limit_bytes=62 * 2**20
        ),
    )(*sources)


def on_device(
    inputs,
    proj_in,
    bias_query,
    bias_value,
    proj_out,
    bias_out,
    norm_gain,
    norm_shift,
    up_weight,
    up_bias,
    down_weight,
    down_bias,
    post_gain,
    post_shift,
    cotangent,
):
    low = jnp.bfloat16
    full = jnp.float32
    f, s = place()
    split = proj_in.reshape(ROWS, 3, G, OWN).transpose(2, 0, 1, 3)
    send_in = pack(pad_heads(split).reshape(G, ROWS, 3 * PAD))
    units = up_weight.reshape(ROWS, N, G, ROWS).transpose(2, 0, 1, 3).reshape(G, ROWS, FFG)
    send_out = jnp.broadcast_to(pack(proj_out)[None], (G, 48, 384))
    vectors = jnp.stack(
        [norm_gain, norm_shift, post_gain, post_shift, bias_out, down_bias, jnp.zeros_like(bias_out), bias_query, bias_value]
    )
    compact = jnp.pad(vectors, ((0, 7), (0, 384 - ROWS)))
    compact = compact + jnp.pad(up_bias[None], ((6, 9), (0, 384 - 96)))
    send_up = pack(units)
    compact = jnp.broadcast_to(compact[None], (G, 16, 384))
    src_a = send_in[:, :32]
    src_b = jnp.concatenate([send_in[:, 32:], compact], axis=1)
    src_c = jnp.concatenate([send_out, send_up[:, :32]], axis=1)
    src_d = jnp.concatenate([send_up[:, 32:], pack(down_weight.reshape(G, ROWS, D))], axis=1)
    final_rows, final_wide, final_down, final_vec = layer(src_a, src_b, src_c, src_d, inputs, cotangent)
    final_vec = final_vec[:, :ROWS]
    return (
        final_rows[:TOK],
        final_rows[TOK:],
        final_wide[:, : 3 * D],
        final_vec[6],
        final_vec[7],
        final_wide[:, 3 * D : 4 * D],
        final_vec[4],
        final_vec[0],
        final_vec[1],
        final_wide[:, 4 * D :],
        final_vec[8:12].reshape(96),
        final_down,
        final_vec[5],
        final_vec[2],
        final_vec[3],
    )


def solution(mesh):
    rows, wide, flat = P(("fsdp", "seq"), None), P("fsdp", None), P("fsdp")
    return jax.shard_map(
        on_device,
        mesh=mesh,
        in_specs=(rows, wide, flat, flat, wide, flat, flat, flat, wide, flat, wide, flat, flat, flat, rows),
        out_specs=(rows, rows, wide, flat, flat, wide, flat, flat, flat, wide, flat, wide, flat, flat, flat),
        check_vma=False,
    )
```
